32 devices in a mesh: tm: 8 (over z, core), op: 4 (over y, x).
Axes of the slice: x: 2, y: 2, z: 4, core: 2. Of those that a mesh axis runs over, the one named last changes fastest.
Arguments:
- sink_fields: bfloat16 [8, 2, 2, 512, 512], P('tm', None, None, 'op'), may hold values from -0.1875 to 0.1875
- source_fields: bfloat16 [8, 2, 2, 512, 512], P('tm', None, None, 'op'), may hold values from -0.1875 to 0.1875
- source_live: int32 [8], P('tm'), may hold values 0 or 1
- chain_factors: int32 [128, 4], replicated, may hold values from 0 to 1
- chain_target: int32 [128], replicated, may hold values from 0 to 15
Outputs:
- correlators: float32 [2, 16, 2], replicated
The draws below stay inside these ranges and needn't reach their ends.
All inputs are finite; a program needn't handle non-finite values. No bound on the sum of `source_live` on one device may be relied on, other than what follows from the above.
Results may differ from the reference program's by a relative error of at most 0.0039.
Values may be sent and summed in bfloat16 or wider, within the bound.
No kernel may reach another device: no remote copies, remote signals or barrier semaphores. Data moves between devices by JAX's collectives and lax.ppermute only.
A program may use at most 64 MiB of HBM per device.

```python
import math
import jax
import jax.numpy as jnp
from jax import lax

E = 512
NF = 2
WIN = 2
NCH = 128
NCORR = 16
NT = 8


def place_ends(array, stream_key, smallest, largest):
    place = [jax.random.randint(jax.random.fold_in(stream_key, axis), (), 0, length) for axis, length in enumerate(array.shape)]
    longest = array.shape.index(max(array.shape))
    neighbour = place[:longest] + [(place[longest] + 1) % array.shape[longest]] + place[longest + 1:]
    return array.at[tuple(place)].set(smallest).at[tuple(neighbour)].set(largest)


def block_scale(rng, shape, shards, smallest, largest):
    loudness = 1.0
    for axis_at, parts in shards:
        steps = jax.random.uniform(jax.random.fold_in(jax.random.fold_in(rng, 6), axis_at), (parts,), jnp.float32, smallest / len(shards), largest / len(shards))
        loudness = loudness * jnp.repeat(jnp.exp(steps), shape[axis_at] // parts).reshape((-1,) + (1,) * (len(shape) - 1 - axis_at))
    return loudness


def noise(key, shape, scale, reach, pieces=(), kind=jnp.bfloat16):
    factor_of = block_scale(key, shape, pieces, -0.22, 0.18) if pieces else 1.0
    array = jax.random.normal(key, shape, jnp.float32) * scale * factor_of
    return jnp.minimum(jnp.maximum(array, -reach), reach).astype(kind)


def setup_inputs(seed: int = 0) -> dict:
    keys = jax.random.split(jax.random.key(seed), 6)
    sink_fields = noise(keys[0], (NT, NF, 2, E, E), (2 * E) ** -0.5, 0.1875, ((0, 8), (3, 4)))
    source_fields = noise(keys[1], (NT, NF, 2, E, E), (2 * E) ** -0.5, 0.1875, ((0, 8), (3, 4)))
    source_live = place_ends((jax.random.randint(keys[2], (NT,), 0, 4) < 3).astype(jnp.int32), jax.random.fold_in(keys[2], 1), 0, 1)
    chain_factors = place_ends(jax.random.randint(keys[3], (NCH, 4), 0, NF), jax.random.fold_in(keys[3], 1), 0, NF - 1).astype(jnp.int32)
    chain_target = place_ends(jax.random.randint(keys[4], (NCH,), 0, NCORR), jax.random.fold_in(keys[4], 1), 0, NCORR - 1).astype(jnp.int32)
    return dict(sink_fields=sink_fields, source_fields=source_fields, source_live=source_live, chain_factors=chain_factors, chain_target=chain_target)


def stacked_block(planes):
    real_part = planes[..., 0, :, :]
    imag_part = planes[..., 1, :, :]
    upper_half = jnp.concatenate([real_part, imag_part], -1)
    lower_half = jnp.concatenate([-imag_part, real_part], -1)
    return jnp.concatenate([upper_half, lower_half], -2)

def reference(sink_fields, source_fields, source_live, chain_factors, chain_target):
    pair_count = NF * NF
    chain_codes = (chain_factors[:, 0] * NF + chain_factors[:, 1]) * pair_count + chain_factors[:, 2] * NF + chain_factors[:, 3]
    chain_onehot = (chain_codes[:, None] == jnp.arange(pair_count * pair_count, dtype=jnp.int32)[None, :]).astype(jnp.float32)
    target_onehot = (chain_target[:, None] == jnp.arange(NCORR, dtype=jnp.int32)[None, :]).astype(jnp.float32)
    selector = jnp.dot(target_onehot.T, chain_onehot, precision=lax.Precision.HIGHEST)
    results = []
    for separation in range(1, WIN + 1):

        def per_source(source_time):
            sink_time = ((source_time + separation) % NT).astype(jnp.int32)
            sink_now = lax.dynamic_index_in_dim(sink_fields, sink_time, 0, keepdims=False).astype(jnp.float32)
            source_now = lax.dynamic_index_in_dim(source_fields, source_time, 0, keepdims=False).astype(jnp.float32)
            left_stack = jnp.concatenate([sink_now[:, 0], sink_now[:, 1]], -1)
            products = jnp.einsum('aix,bxy->abiy', left_stack, stacked_block(source_now), precision=lax.Precision.HIGHEST)
            rounded = lax.optimization_barrier(products.astype(jnp.bfloat16)).astype(jnp.float32)
            flattened = rounded.reshape(pair_count, E, 2 * E)
            real_block = flattened[..., :E]
            imag_block = flattened[..., E:]
            real_trace = jnp.einsum('pij,qji->pq', real_block, real_block, precision=lax.Precision.HIGHEST) - jnp.einsum('pij,qji->pq', imag_block, imag_block, precision=lax.Precision.HIGHEST)
            imag_trace = jnp.einsum('pij,qji->pq', real_block, imag_block, precision=lax.Precision.HIGHEST) + jnp.einsum('pij,qji->pq', imag_block, real_block, precision=lax.Precision.HIGHEST)
            traces = jnp.stack([real_trace.reshape(-1), imag_trace.reshape(-1)])
            weight = lax.dynamic_index_in_dim(source_live, source_time, 0, keepdims=False).astype(jnp.float32)
            return weight * traces
        summed = lax.optimization_barrier(jnp.sum(lax.map(per_source, jnp.arange(NT, dtype=jnp.int32)), axis=0))
        results.append(jnp.dot(summed, selector.T, precision=lax.Precision.HIGHEST))
    return jnp.stack(results, -1) / math.sqrt(NT)
```

```python
import functools
import math

import jax
import jax.numpy as jnp
from jax import lax
from jax.experimental import pallas as pl
from jax.experimental.pallas import tpu as pltpu
from jax.sharding import PartitionSpec as P

WIN = 2
NCORR = 16
AXES = ("tm", "op")
LANES = 128


def routes(times, ops, place):
    pairs = []
    for pair in range(times // 2):
        for core in range(2):
            for op in range(ops):
                to_pair, to_core, to_op = place(pair, core, op)
                to_time = (to_pair % (times // 2)) * 2 + to_core
                pairs.append(((pair * 2 + core) * ops + op, to_time * ops + to_op))
    return pairs


def sink_route(times, ops, step):
    half = ops // 2
    return routes(times, ops, lambda pair, core, op: (pair, op // half, core * half + ((op % half) ^ step)))


def source_route(times, ops, step):
    half = ops // 2

    def place(pair, core, op):
        target = (((op >> 1) ^ step) << 1) | core
        stays = core == 0 and target // half == 1
        return (pair if stays else pair + 1), op & 1, target

    return routes(times, ops, place)


def pair_sum(value, axis, count):
    step = 1
    while step < count:
        value = value + lax.ppermute(value, axis, [(i, i ^ step) for i in range(count)])
        step *= 2
    return value


def trace_kernel(ops, group, *refs):
    sinks, sources = refs[:ops], refs[ops : 2 * ops]
    weights, columns, out = refs[2 * ops : 2 * ops + 3]
    left, right, flip, product, flipped, sems = refs[2 * ops + 3 :]
    fields, _, rows, full = sinks[0].shape
    half = ops // 2
    share = product.shape[0] * group
    parts = product.shape[1]
    core = lax.rem(lax.axis_index("tm"), 2)
    chip = lax.axis_index("op")
    copies = []

    def fetch(block, dst):
        copy = pltpu.make_async_copy(block, dst, sems.at[len(copies)])
        copy.start()
        copies.append(copy)

    for turn in range(2):
        side = core if turn == 0 else 1 - core
        for step in range(half):
            block = sinks[turn * half + step]
            slot = side * half + (lax.rem(chip, half) ^ step)
            at = pl.ds(pl.multiple_of(slot * rows, rows), rows)
            for part in range(2):
                fetch(block.at[:, part], left.at[:, at, pl.ds(part * full, full)])
            block = sources[turn * half + step]
            slot = (((chip >> 1) ^ step) << 1) + side
            at = pl.ds(pl.multiple_of(slot * rows, rows), rows)
            low = pl.ds(pl.multiple_of(full + slot * rows, rows), rows)
            for part in range(2):
                fetch(block.at[:, part], right.at[:, at, pl.ds(part * full, full)])
            fetch(block.at[:, 0], right.at[:, low, pl.ds(full, full)])
    for copy in copies:
        copy.wait()

    member = lax.rem(chip, half) // 2 * 2 + core
    start = pl.multiple_of(member * share, share)
    mine = pl.ds(start, share)
    mine_imag = pl.ds(pl.multiple_of(full + start, share), share)
    for b in range(fields):
        right[b, full:, :full] = -right[b, :full, full:]
        real_turned = right[b, :full, mine].T
        imag_turned = right[b, :full, mine_imag].T
        flip[b, 0, :, :full] = real_turned
        flip[b, 0, :, full:] = -imag_turned
        flip[b, 1, :, :full] = imag_turned
        flip[b, 1, :, full:] = real_turned
    groups = share // group
    for a in range(fields):
        for b in range(fields):
            for part in range(2):
                at = (a * fields + b) * 2 + part
                value = jnp.dot(
                    left[a, mine, :],
                    right[b, :, part * full : (part + 1) * full],
                    preferred_element_type=jnp.float32,
                ).astype(jnp.bfloat16)
                product[:, at] = value.reshape(groups, group, full)
                value = lax.dot_general(
                    flip[b, part], left[a], (((1,), (1,)), ((), ())), preferred_element_type=jnp.float32
                ).astype(jnp.bfloat16)
                flipped[:, at] = value.reshape(groups, group, full)
    side = parts * group
    total = jnp.zeros((side, side), jnp.float32)
    for g in range(groups):
        total = total + lax.dot_general(
            product[g].reshape(side, full),
            flipped[g].reshape(side, full),
            (((1,), (1,)), ((), ())),
            preferred_element_type=jnp.float32,
        )
    row = lax.broadcasted_iota(jnp.int32, (side, side), 0)
    lane = lax.broadcasted_iota(jnp.int32, (side, side), 1)
    total = jnp.where(lax.rem(row, group) == lax.rem(lane, group), total, 0.0)
    total = jnp.sum(total.reshape(parts, group, side), 1)
    source = lax.broadcasted_iota(jnp.int32, (side, LANES), 0)
    lane = lax.broadcasted_iota(jnp.int32, (side, LANES), 1)
    spread = (source // group == lax.rem(lane, parts)).astype(jnp.float32)
    total = jnp.dot(total, spread, precision=lax.Precision.HIGHEST, preferred_element_type=jnp.float32)
    row = lax.broadcasted_iota(jnp.int32, (parts, LANES), 0)
    lane = lax.broadcasted_iota(jnp.int32, (parts, LANES), 1)
    total = jnp.where(lane // parts == row, total, 0.0)
    total = jnp.dot(total, weights[...], precision=lax.Precision.HIGHEST, preferred_element_type=jnp.float32)
    out[...] = jnp.sum(total, 0, keepdims=True) * columns[...]


def chain_weights(chain_factors, chain_target, fields):
    pairs = fields * fields
    parts = 2 * pairs
    codes = (
        (chain_factors[:, 0] * fields + chain_factors[:, 1]) * pairs
        + chain_factors[:, 2] * fields
        + chain_factors[:, 3]
    )
    row = jnp.arange(LANES, dtype=jnp.int32)
    first, second = row // parts, row % parts
    row_code = jnp.where(row < parts * parts, (first // 2) * pairs + second // 2, -1)
    column = jnp.arange(LANES, dtype=jnp.int32)
    on_row = (row_code[:, None] == codes[None, :]).astype(jnp.float32)
    on_column = (chain_target[:, None] == (column % NCORR)[None, :]).astype(jnp.float32)
    counts = jnp.dot(on_row, on_column, precision=lax.Precision.HIGHEST)
    mixed = (first % 2 != second % 2)[:, None]
    both_imag = (first % 2 + second % 2 == 2)[:, None]
    real_sign = jnp.where(mixed, 0.0, jnp.where(both_imag, -1.0, 1.0))
    imag_sign = jnp.where(mixed, 1.0, 0.0)
    sign = jnp.where((column < NCORR)[None, :], real_sign, imag_sign)
    sign = jnp.where((column < 2 * NCORR)[None, :], sign, 0.0)
    return counts * sign


def per_device(times, ops, sink_fields, source_fields, source_live, chain_factors, chain_target):
    fields, _, rows, full = sink_fields.shape[1:]
    half = ops // 2
    share = full // half
    group = 2 * LANES // (2 * fields * fields)
    chip = lax.axis_index("op")
    swap = routes(times, ops, lambda pair, core, op: (pair, 1 - core, op))
    live = lax.ppermute(source_live.astype(jnp.bfloat16), AXES, source_route(times, ops, 0))
    sinks = [lax.ppermute(sink_fields[0], AXES, sink_route(times, ops, step)) for step in range(half)]
    sources = [lax.ppermute(source_fields[0], AXES, source_route(times, ops, step)) for step in range(half)]
    sinks = sinks + [lax.ppermute(block, AXES, swap) for block in sinks]
    sources = sources + [lax.ppermute(block, AXES, swap) for block in sources]
    separation = jnp.where(chip // half == lax.rem(chip, 2), 2, 1)
    scale = live[0].astype(jnp.float32) / math.sqrt(times)
    row = jnp.arange(WIN, dtype=jnp.int32)[:, None]
    columns = jnp.broadcast_to(jnp.where(row + 1 == separation, scale, 0.0), (WIN, LANES))
    weights = chain_weights(chain_factors, chain_target, fields)
    parts = 2 * fields * fields
    any_spec = pl.BlockSpec(memory_space=pl.ANY)
    vmem_spec = pl.BlockSpec(memory_space=pltpu.VMEM)
    partial_sums = pl.pallas_call(
        functools.partial(trace_kernel, ops, group),
        out_shape=jax.ShapeDtypeStruct((WIN, LANES), jnp.float32),
        in_specs=[any_spec] * (2 * ops) + [vmem_spec] * 2,
        out_specs=vmem_spec,
        scratch_shapes=[
            pltpu.VMEM((fields, full, 2 * full), jnp.bfloat16),
            pltpu.VMEM((fields, 2 * full, 2 * full), jnp.bfloat16),
            pltpu.VMEM((fields, 2, share, 2 * full), jnp.bfloat16),
            pltpu.VMEM((share // group, parts, group, full), jnp.bfloat16),
            pltpu.VMEM((share // group, parts, group, full), jnp.bfloat16),
            pltpu.SemaphoreType.DMA((5 * ops,)),
        ],
        compiler_params=pltpu.CompilerParams(vmem_limit_bytes=40 * 1024 * 1024),
        cost_estimate=pl.CostEstimate(
            flops=2 * 2 * 4 * fields * fields * share * full * full, bytes_accessed=10 * ops * rows * full, transcendentals=0
        ),
    )(*sinks, *sources, weights, columns)
    totals = pair_sum(pair_sum(partial_sums, "tm", times), "op", ops)
    return totals[:, : 2 * NCORR].reshape(WIN, 2, NCORR).transpose(1, 2, 0)


def solution(mesh):
    in_specs = (P("tm", None, None, "op", None), P("tm", None, None, "op", None), P("tm"), P(), P())
    body = functools.partial(per_device, mesh.shape["tm"], mesh.shape["op"])
    return jax.shard_map(body, mesh=mesh, in_specs=in_specs, out_specs=P(), check_vma=False)
```

```python
import functools
import math

import jax
import jax.numpy as jnp
from jax import lax
from jax.experimental import pallas as pl
from jax.experimental.pallas import tpu as pltpu
from jax.sharding import PartitionSpec as P

WIN = 2
NCORR = 16
AXES = ("tm", "op")
LANES = 128


def routes(times, ops, place):
    pairs = []
    for pair in range(times // 2):
        for core in range(2):
            for op in range(ops):
                to_pair, to_core, to_op = place(pair, core, op)
                to_time = (to_pair % (times // 2)) * 2 + to_core
                pairs.append(((pair * 2 + core) * ops + op, to_time * ops + to_op))
    return pairs


def sink_route(times, ops, step):
    half = ops // 2

    def place(pair, core, op):
        side = op // half
        return pair, side, core * half + ((op % half) ^ side ^ core ^ step)

    return routes(times, ops, place)


def source_route(times, ops, step):
    half = ops // 2

    def place(pair, core, op):
        target = (((op >> 1) ^ 1 ^ (op & 1) ^ core ^ step) << 1) | core
        stays = core == 0 and target // half == 1
        return (pair if stays else pair + 1), op & 1, target

    return routes(times, ops, place)


def pair_sum(value, axis, count):
    step = 1
    while step < count:
        value = value + lax.ppermute(value, axis, [(i, i ^ step) for i in range(count)])
        step *= 2
    return value


def trace_kernel(ops, group, *refs):
    sinks, sources = refs[:ops], refs[ops : 2 * ops]
    weights, columns, out = refs[2 * ops : 2 * ops + 3]
    left, right, flip, product, flipped, far_product, far_flipped, sems = refs[2 * ops + 3 :]
    fields, _, rows, full = sinks[0].shape
    half = ops // 2
    share = full // half
    parts = product.shape[1]
    core = lax.rem(lax.axis_index("tm"), 2)
    chip = lax.axis_index("op")
    copies = []

    def fetch(block, dst):
        copy = pltpu.make_async_copy(block, dst, sems.at[len(copies)])
        copy.start()
        copies.append(copy)

    for turn in range(2):
        side = core if turn == 0 else 1 - core
        for step in range(half):
            block = sinks[turn * half + step]
            slot = side * half + (lax.rem(chip, half) ^ side ^ (chip // half) ^ step)
            at = pl.ds(pl.multiple_of(slot * rows, rows), rows)
            for part in range(2):
                fetch(block.at[:, part], left.at[:, at, pl.ds(part * full, full)])
            block = sources[turn * half + step]
            slot = (((chip >> 1) ^ 1 ^ side ^ (chip & 1) ^ step) << 1) + side
            at = pl.ds(pl.multiple_of(slot * rows, rows), rows)
            low = pl.ds(pl.multiple_of(full + slot * rows, rows), rows)
            for part in range(2):
                fetch(block.at[:, part], right.at[:, at, pl.ds(part * full, full)])
            fetch(block.at[:, 0], right.at[:, low, pl.ds(full, full)])
    for copy in copies:
        copy.wait()
    for b in range(fields):
        right[b, full:, :full] = -right[b, :full, full:]

    def span(start, size):
        return pl.ds(pl.multiple_of(start, math.gcd(size, share // 2)), size)

    def stacked_sinks(at):
        return jnp.concatenate([left[a, at, :] for a in range(fields)], 0)

    def forward(row_at, col_start, cols, into, turned=None):
        lhs = stacked_sinks(row_at)
        count = lhs.shape[0] // fields
        for b in range(fields):
            for part in range(2):
                rhs = right[b, :, span(part * full + col_start, cols)]
                value = jnp.dot(lhs, rhs, preferred_element_type=jnp.float32).astype(jnp.bfloat16)
                for a in range(fields):
                    block = value[a * count : (a + 1) * count]
                    at = (a * fields + b) * 2 + part
                    into[:, at] = block.reshape(count // group, group, cols)
                    if turned is not None:
                        turned[:, at] = block.T.reshape(count // group, group, cols)

    def backward(row_start, count, col_at, into):
        for b in range(fields):
            real_turned = right[b, :full, span(row_start, count)].T
            imag_turned = right[b, :full, span(full + row_start, count)].T
            flip[b, 0, :count, :full] = real_turned
            flip[b, 0, :count, full:] = -imag_turned
            flip[b, 1, :count, :full] = imag_turned
            flip[b, 1, :count, full:] = real_turned
        rhs = stacked_sinks(col_at)
        cols = rhs.shape[0] // fields
        lhs = flip[:, :, :count, :].reshape(fields * 2 * count, 2 * full)
        value = lax.dot_general(lhs, rhs, (((1,), (1,)), ((), ())), preferred_element_type=jnp.float32)
        value = value.astype(jnp.bfloat16)
        for b in range(fields):
            for part in range(2):
                for a in range(fields):
                    at = (a * fields + b) * 2 + part
                    block = value[(b * 2 + part) * count : (b * 2 + part + 1) * count, a * cols : (a + 1) * cols]
                    into[:, at] = block.reshape(count // group, group, cols)

    side = parts * group

    def traces(total, first, second, groups):
        for g in range(groups):
            total = total + lax.dot_general(
                first[g].reshape(side, first.shape[-1]),
                second[g].reshape(side, second.shape[-1]),
                (((1,), (1,)), ((), ())),
                preferred_element_type=jnp.float32,
            )
        return total

    member = lax.rem(chip, half) // 2 * 2 + core
    start = member * share
    forward(span(start, share), start, share, product, flipped)
    once = traces(jnp.zeros((side, side), jnp.float32), product, flipped, share // group)
    twice = jnp.zeros((side, side), jnp.float32)
    for apart in range(1, half // 2 + 1):
        row_start, count, col_start = start, share, lax.rem(member + apart, half) * share
        again = 2 * apart == half
        split = again and share // 2 % LANES == 0
        if split:
            low = lax.rem(member, half // 2)
            row_start = low * share + member // (half // 2) * (share // 2)
            count, col_start = share // 2, (low + half // 2) * share
        forward(span(row_start, count), col_start, share, far_product.at[: count // group])
        backward(row_start, count, span(col_start, share), far_flipped.at[: count // group])
        if again and not split:
            once = traces(once, far_product, far_flipped, count // group)
        else:
            twice = traces(twice, far_product, far_flipped, count // group)
    total = once + 2.0 * twice
    row = lax.broadcasted_iota(jnp.int32, (side, side), 0)
    lane = lax.broadcasted_iota(jnp.int32, (side, side), 1)
    total = jnp.where(lax.rem(row, group) == lax.rem(lane, group), total, 0.0)
    total = jnp.sum(total.reshape(parts, group, side), 1)
    source = lax.broadcasted_iota(jnp.int32, (side, LANES), 0)
    lane = lax.broadcasted_iota(jnp.int32, (side, LANES), 1)
    spread = (source // group == lax.rem(lane, parts)).astype(jnp.float32)
    total = jnp.dot(total, spread, precision=lax.Precision.HIGHEST, preferred_element_type=jnp.float32)
    row = lax.broadcasted_iota(jnp.int32, (parts, LANES), 0)
    lane = lax.broadcasted_iota(jnp.int32, (parts, LANES), 1)
    total = jnp.where(lane // parts == row, total, 0.0)
    total = jnp.dot(total, weights[...], precision=lax.Precision.HIGHEST, preferred_element_type=jnp.float32)
    total = jnp.sum(total, 0, keepdims=True)
    for part in range(2):
        out[part] = total[:, part * NCORR : (part + 1) * NCORR] * columns[...]


def chain_weights(chain_factors, chain_target, fields):
    pairs = fields * fields
    parts = 2 * pairs
    codes = (
        (chain_factors[:, 0] * fields + chain_factors[:, 1]) * pairs
        + chain_factors[:, 2] * fields
        + chain_factors[:, 3]
    )
    row = jnp.arange(LANES, dtype=jnp.int32)
    first, second = row // parts, row % parts
    used = row < parts * parts
    ahead = jnp.where(used, (first // 2) * pairs + second // 2, -1)
    behind = jnp.where(used, (second // 2) * pairs + first // 2, -1)
    column = jnp.arange(LANES, dtype=jnp.int32)
    on_row = (ahead[:, None] == codes[None, :]).astype(jnp.float32)
    on_row = 0.5 * (on_row + (behind[:, None] == codes[None, :]).astype(jnp.float32))
    on_column = (chain_target[:, None] == (column % NCORR)[None, :]).astype(jnp.float32)
    counts = jnp.dot(on_row, on_column, precision=lax.Precision.HIGHEST)
    mixed = (first % 2 != second % 2)[:, None]
    both_imag = (first % 2 + second % 2 == 2)[:, None]
    real_sign = jnp.where(mixed, 0.0, jnp.where(both_imag, -1.0, 1.0))
    imag_sign = jnp.where(mixed, 1.0, 0.0)
    sign = jnp.where((column < NCORR)[None, :], real_sign, imag_sign)
    sign = jnp.where((column < 2 * NCORR)[None, :], sign, 0.0)
    return counts * sign


def per_device(times, ops, sink_fields, source_fields, source_live, chain_factors, chain_target):
    fields, _, rows, full = sink_fields.shape[1:]
    half = ops // 2
    share = full // half
    parts = 2 * fields * fields
    group = 2 * LANES // parts
    chip = lax.axis_index("op")
    swap = routes(times, ops, lambda pair, core, op: (pair, 1 - core, op))
    source = source_fields[0] * source_live[0].astype(jnp.bfloat16)
    sinks = [lax.ppermute(sink_fields[0], AXES, sink_route(times, ops, step)) for step in range(half)]
    sources = [lax.ppermute(source, AXES, source_route(times, ops, step)) for step in range(half)]
    sinks = sinks + [lax.ppermute(block, AXES, swap) for block in sinks]
    sources = sources + [lax.ppermute(block, AXES, swap) for block in sources]
    separation = jnp.where(chip // half == lax.rem(chip, 2), 2, 1)
    row = jnp.arange(WIN, dtype=jnp.int32)[:, None]
    columns = jnp.broadcast_to(jnp.where(row + 1 == separation, 1.0 / math.sqrt(times), 0.0), (WIN, NCORR))
    weights = chain_weights(chain_factors, chain_target, fields)
    any_spec = pl.BlockSpec(memory_space=pl.ANY)
    vmem_spec = pl.BlockSpec(memory_space=pltpu.VMEM)
    partial_sums = pl.pallas_call(
        functools.partial(trace_kernel, ops, group),
        out_shape=jax.ShapeDtypeStruct((2, WIN, NCORR), jnp.float32),
        in_specs=[any_spec] * (2 * ops) + [vmem_spec] * 2,
        out_specs=vmem_spec,
        scratch_shapes=[
            pltpu.VMEM((fields, full, 2 * full), jnp.bfloat16),
            pltpu.VMEM((fields, 2 * full, 2 * full), jnp.bfloat16),
            pltpu.VMEM((fields, 2, share, 2 * full), jnp.bfloat16),
        ]
        + [pltpu.VMEM((share // group, parts, group, share), jnp.bfloat16)] * 4
        + [pltpu.SemaphoreType.DMA((5 * ops,))],
        compiler_params=pltpu.CompilerParams(vmem_limit_bytes=32 * 1024 * 1024),
        cost_estimate=pl.CostEstimate(
            flops=2 * 2 * 4 * fields * fields * share * full * full, bytes_accessed=10 * ops * rows * full, transcendentals=0
        ),
    )(*sinks, *sources, weights, columns.astype(jnp.float32))
    totals = pair_sum(pair_sum(partial_sums, "tm", times), "op", ops)
    return totals.transpose(0, 2, 1)


def solution(mesh):
    in_specs = (P("tm", None, None, "op", None), P("tm", None, None, "op", None), P("tm"), P(), P())
    body = functools.partial(per_device, mesh.shape["tm"], mesh.shape["op"])
    return jax.shard_map(body, mesh=mesh, in_specs=in_specs, out_specs=P(), check_vma=False)
```

```python
import functools
import math

import jax
import jax.numpy as jnp
from jax import lax
from jax.experimental import pallas as pl
from jax.experimental.pallas import tpu as pltpu
from jax.sharding import PartitionSpec as P

WIN = 2
NCORR = 16
AXES = ("tm", "op")
LANES = 128


def routes(times, ops, place):
    pairs = []
    for pair in range(times // 2):
        for core in range(2):
            for op in range(ops):
                to_pair, to_core, to_op = place(pair, core, op)
                to_time = (to_pair % (times // 2)) * 2 + to_core
                pairs.append(((pair * 2 + core) * ops + op, to_time * ops + to_op))
    return pairs


def sink_route(times, ops, step):
    half = ops // 2

    def place(pair, core, op):
        side = op // half
        return pair, side, core * half + ((op % half) ^ side ^ core ^ step)

    return routes(times, ops, place)


def source_route(times, ops, step):
    half = ops // 2

    def place(pair, core, op):
        target = (((op >> 1) ^ 1 ^ (op & 1) ^ core ^ step) << 1) | core
        stays = core == 0 and target // half == 1
        return (pair if stays else pair + 1), op & 1, target

    return routes(times, ops, place)


def finish_kernel(ops, parts_ref, out):
    count = parts_ref.shape[0]
    half = ops // 2
    pairs = count // (2 * ops)
    used = 2 * WIN * NCORR
    device = lax.broadcasted_iota(jnp.int32, (count, count), 0)
    holder = lax.broadcasted_iota(jnp.int32, (count, count), 1)
    chip = lax.rem(device, ops)
    stays = (lax.rem(chip, 2) == 0) & (chip // half == 1)
    pair = lax.rem(device // (2 * ops) + jnp.where(stays, 0, pairs - 1), pairs)
    pick = ((pair * 2 + lax.rem(chip, 2)) * ops + chip == holder).astype(jnp.float32)
    rows = parts_ref[...]
    live = jnp.broadcast_to(rows[:, used : used + 1], rows.shape)
    live = jnp.dot(pick, live, precision=lax.Precision.HIGHEST, preferred_element_type=jnp.float32)
    total = jnp.sum(rows * live, 0, keepdims=True)
    for part in range(2):
        for apart in range(WIN):
            at = (part * WIN + apart) * NCORR
            out[part, apart : apart + 1] = total[:, at : at + NCORR]


def trace_kernel(ops, group, *refs):
    sinks, sources = refs[:ops], refs[ops : 2 * ops]
    weights, columns, out = refs[2 * ops : 2 * ops + 3]
    left, right, flip, product, flipped, far_product, far_flipped, sems = refs[2 * ops + 3 :]
    fields, _, rows, full = sinks[0].shape
    half = ops // 2
    share = full // half
    parts = product.shape[1]
    core = lax.rem(lax.axis_index("tm"), 2)
    chip = lax.axis_index("op")
    copies = []

    def fetch(block, dst):
        copy = pltpu.make_async_copy(block, dst, sems.at[len(copies)])
        copy.start()
        copies.append(copy)

    for turn in range(2):
        side = core if turn == 0 else 1 - core
        for step in range(half):
            block = sinks[turn * half + step]
            slot = side * half + (lax.rem(chip, half) ^ side ^ (chip // half) ^ step)
            at = pl.ds(pl.multiple_of(slot * rows, rows), rows)
            for part in range(2):
                fetch(block.at[:, part], left.at[:, at, pl.ds(part * full, full)])
            block = sources[turn * half + step]
            slot = (((chip >> 1) ^ 1 ^ side ^ (chip & 1) ^ step) << 1) + side
            at = pl.ds(pl.multiple_of(slot * rows, rows), rows)
            low = pl.ds(pl.multiple_of(full + slot * rows, rows), rows)
            for part in range(2):
                fetch(block.at[:, part], right.at[:, at, pl.ds(part * full, full)])
            fetch(block.at[:, 0], right.at[:, low, pl.ds(full, full)])
    for copy in copies:
        copy.wait()
    for b in range(fields):
        right[b, full:, :full] = -right[b, :full, full:]

    def span(start, size):
        return pl.ds(pl.multiple_of(start, math.gcd(size, share // 2)), size)

    def stacked_sinks(at):
        return jnp.concatenate([left[a, at, :] for a in range(fields)], 0)

    def forward(row_at, col_start, cols, into, turned=None):
        lhs = stacked_sinks(row_at)
        count = lhs.shape[0] // fields
        for b in range(fields):
            for part in range(2):
                rhs = right[b, :, span(part * full + col_start, cols)]
                value = jnp.dot(lhs, rhs, preferred_element_type=jnp.float32).astype(jnp.bfloat16)
                for a in range(fields):
                    block = value[a * count : (a + 1) * count]
                    at = (a * fields + b) * 2 + part
                    into[:, at] = block.reshape(count // group, group, cols)
                    if turned is not None:
                        turned[:, at] = block.T.reshape(count // group, group, cols)

    def backward(row_start, count, col_at, into):
        for b in range(fields):
            real_turned = right[b, :full, span(row_start, count)].T
            imag_turned = right[b, :full, span(full + row_start, count)].T
            flip[b, 0, :count, :full] = real_turned
            flip[b, 0, :count, full:] = -imag_turned
            flip[b, 1, :count, :full] = imag_turned
            flip[b, 1, :count, full:] = real_turned
        rhs = stacked_sinks(col_at)
        cols = rhs.shape[0] // fields
        lhs = flip[:, :, :count, :].reshape(fields * 2 * count, 2 * full)
        value = lax.dot_general(lhs, rhs, (((1,), (1,)), ((), ())), preferred_element_type=jnp.float32)
        value = value.astype(jnp.bfloat16)
        for b in range(fields):
            for part in range(2):
                for a in range(fields):
                    at = (a * fields + b) * 2 + part
                    block = value[(b * 2 + part) * count : (b * 2 + part + 1) * count, a * cols : (a + 1) * cols]
                    into[:, at] = block.reshape(count // group, group, cols)

    side = parts * group

    def traces(total, first, second, groups):
        for g in range(groups):
            total = total + lax.dot_general(
                first[g].reshape(side, first.shape[-1]),
                second[g].reshape(side, second.shape[-1]),
                (((1,), (1,)), ((), ())),
                preferred_element_type=jnp.float32,
            )
        return total

    member = lax.rem(chip, half) // 2 * 2 + core
    start = member * share
    forward(span(start, share), start, share, product, flipped)
    once = traces(jnp.zeros((side, side), jnp.float32), product, flipped, share // group)
    twice = jnp.zeros((side, side), jnp.float32)
    for apart in range(1, half // 2 + 1):
        row_start, count, col_start = start, share, lax.rem(member + apart, half) * share
        again = 2 * apart == half
        split = again and share // 2 % LANES == 0
        if split:
            low = lax.rem(member, half // 2)
            row_start = low * share + member // (half // 2) * (share // 2)
            count, col_start = share // 2, (low + half // 2) * share
        forward(span(row_start, count), col_start, share, far_product.at[: count // group])
        backward(row_start, count, span(col_start, share), far_flipped.at[: count // group])
        if again and not split:
            once = traces(once, far_product, far_flipped, count // group)
        else:
            twice = traces(twice, far_product, far_flipped, count // group)
    total = once + 2.0 * twice
    row = lax.broadcasted_iota(jnp.int32, (side, side), 0)
    lane = lax.broadcasted_iota(jnp.int32, (side, side), 1)
    total = jnp.where(lax.rem(row, group) == lax.rem(lane, group), total, 0.0)
    total = jnp.sum(total.reshape(parts, group, side), 1)
    source = lax.broadcasted_iota(jnp.int32, (side, LANES), 0)
    lane = lax.broadcasted_iota(jnp.int32, (side, LANES), 1)
    spread = (source // group == lax.rem(lane, parts)).astype(jnp.float32)
    total = jnp.dot(total, spread, precision=lax.Precision.HIGHEST, preferred_element_type=jnp.float32)
    row = lax.broadcasted_iota(jnp.int32, (parts, LANES), 0)
    lane = lax.broadcasted_iota(jnp.int32, (parts, LANES), 1)
    total = jnp.where(lane // parts == row, total, 0.0)
    total = jnp.dot(total, weights[...], precision=lax.Precision.HIGHEST, preferred_element_type=jnp.float32)
    total = jnp.sum(total, 0, keepdims=True) * columns[:1] + columns[1:]
    out[...] = jnp.broadcast_to(total[:, None, :], out.shape)


def chain_weights(chain_factors, chain_target, fields):
    pairs = fields * fields
    parts = 2 * pairs
    codes = (
        (chain_factors[:, 0] * fields + chain_factors[:, 1]) * pairs
        + chain_factors[:, 2] * fields
        + chain_factors[:, 3]
    )
    row = jnp.arange(LANES, dtype=jnp.int32)
    first, second = row // parts, row % parts
    used = row < parts * parts
    ahead = jnp.where(used, (first // 2) * pairs + second // 2, -1)
    behind = jnp.where(used, (second // 2) * pairs + first // 2, -1)
    column = jnp.arange(LANES, dtype=jnp.int32)
    on_row = (ahead[:, None] == codes[None, :]).astype(jnp.float32)
    on_row = 0.5 * (on_row + (behind[:, None] == codes[None, :]).astype(jnp.float32))
    on_column = (chain_target[:, None] == (column % NCORR)[None, :]).astype(jnp.float32)
    counts = jnp.dot(on_row, on_column, precision=lax.Precision.HIGHEST)
    mixed = (first % 2 != second % 2)[:, None]
    both_imag = (first % 2 + second % 2 == 2)[:, None]
    real_sign = jnp.where(mixed, 0.0, jnp.where(both_imag, -1.0, 1.0))
    imag_sign = jnp.where(mixed, 1.0, 0.0)
    sign = jnp.where((column < WIN * NCORR)[None, :], real_sign, imag_sign)
    return counts * sign


def per_device(times, ops, sink_fields, source_fields, source_live, chain_factors, chain_target):
    fields, _, rows, full = sink_fields.shape[1:]
    half = ops // 2
    share = full // half
    parts = 2 * fields * fields
    group = 2 * LANES // parts
    chip = lax.axis_index("op")
    swap = routes(times, ops, lambda pair, core, op: (pair, 1 - core, op))
    sinks = [lax.ppermute(sink_fields[0], AXES, sink_route(times, ops, step)) for step in range(half)]
    sources = [lax.ppermute(source_fields[0], AXES, source_route(times, ops, step)) for step in range(half)]
    sinks = sinks + [lax.ppermute(block, AXES, swap) for block in sinks]
    sources = sources + [lax.ppermute(block, AXES, swap) for block in sources]
    separation = jnp.where(chip // half == lax.rem(chip, 2), 2, 1)
    lane = jnp.arange(LANES, dtype=jnp.int32)
    used = 2 * WIN * NCORR
    wanted = (lane < used) & (lane // NCORR % WIN + 1 == separation)
    scale = jnp.where(wanted, 1.0 / math.sqrt(times), 0.0)
    flag = jnp.where(lane == used, source_live[0].astype(jnp.float32), 0.0)
    columns = jnp.stack([scale, flag]).astype(jnp.float32)
    weights = chain_weights(chain_factors, chain_target, fields)
    any_spec = pl.BlockSpec(memory_space=pl.ANY)
    vmem_spec = pl.BlockSpec(memory_space=pltpu.VMEM)
    partial_sums = pl.pallas_call(
        functools.partial(trace_kernel, ops, group),
        out_shape=jax.ShapeDtypeStruct((times * ops, 1, LANES), jnp.float32),
        in_specs=[any_spec] * (2 * ops) + [vmem_spec] * 2,
        out_specs=vmem_spec,
        scratch_shapes=[
            pltpu.VMEM((fields, full, 2 * full), jnp.bfloat16),
            pltpu.VMEM((fields, 2 * full, 2 * full), jnp.bfloat16),
            pltpu.VMEM((fields, 2, share, 2 * full), jnp.bfloat16),
        ]
        + [pltpu.VMEM((share // group, parts, group, share), jnp.bfloat16)] * 4
        + [pltpu.SemaphoreType.DMA((5 * ops,))],
        compiler_params=pltpu.CompilerParams(vmem_limit_bytes=32 * 1024 * 1024),
        cost_estimate=pl.CostEstimate(
            flops=2 * 2 * 4 * fields * fields * share * full * full, bytes_accessed=10 * ops * rows * full, transcendentals=0
        ),
    )(*sinks, *sources, weights, columns)
    shares = lax.all_to_all(partial_sums, AXES, 0, 0, tiled=True)
    totals = pl.pallas_call(
        functools.partial(finish_kernel, ops),
        out_shape=jax.ShapeDtypeStruct((2, WIN, NCORR), jnp.float32),
        in_specs=[vmem_spec],
        out_specs=vmem_spec,
    )(shares.reshape(times * ops, LANES))
    return totals.transpose(0, 2, 1)


def solution(mesh):
    in_specs = (P("tm", None, None, "op", None), P("tm", None, None, "op", None), P("tm"), P(), P())
    body = functools.partial(per_device, mesh.shape["tm"], mesh.shape["op"])
    return jax.shard_map(body, mesh=mesh, in_specs=in_specs, out_specs=P(), check_vma=False)
```

```python
import functools
import math

import jax
import jax.numpy as jnp
from jax import lax
from jax.experimental import pallas as pl
from jax.experimental.pallas import tpu as pltpu
from jax.sharding import PartitionSpec as P

WIN = 2
NCORR = 16
AXES = ("tm", "op")
LANES = 128


def routes(times, ops, place):
    pairs = []
    for pair in range(times // 2):
        for core in range(2):
            for op in range(ops):
                to_pair, to_core, to_op = place(pair, core, op)
                to_time = (to_pair % (times // 2)) * 2 + to_core
                pairs.append(((pair * 2 + core) * ops + op, to_time * ops + to_op))
    return pairs


def sink_route(times, ops, step):
    half = ops // 2

    def place(pair, core, op):
        side = op // half
        return pair, side, core * half + ((op % half) ^ side ^ core ^ step)

    return routes(times, ops, place)


def source_route(times, ops, step):
    half = ops // 2

    def place(pair, core, op):
        target = (((op >> 1) ^ 1 ^ (op & 1) ^ core ^ step) << 1) | core
        stays = core == 0 and target // half == 1
        return (pair if stays else pair + 1), op & 1, target

    return routes(times, ops, place)


def finish_kernel(ops, parts_ref, out):
    count = parts_ref.shape[0]
    half = ops // 2
    used = 2 * WIN * NCORR
    rows = parts_ref[...]
    live = jnp.broadcast_to(rows[:, used : used + 1], rows.shape)
    row = lax.broadcasted_iota(jnp.int32, rows.shape, 0)
    chip = lax.rem(row, ops)
    stays = (lax.rem(chip, 2) == 0) & (chip // half == 1)
    behind = lax.rem(row // ops, 2) - lax.rem(chip, 2) + jnp.where(stays, 0, 2)
    weight = jnp.zeros_like(live)
    for step in range(4):
        at = (count - step * ops) % count
        moved = live if step == 0 else jnp.concatenate([live[at:], live[:at]], 0)
        weight = jnp.where(behind == step, moved, weight)
    total = jnp.sum(rows * weight, 0, keepdims=True)
    for part in range(2):
        for apart in range(WIN):
            at = (part * WIN + apart) * NCORR
            out[part, apart : apart + 1] = total[:, at : at + NCORR]


class Fetches:
    def __init__(self, sems):
        self.sems, self.copies = sems, []

    def start(self, src, dst):
        copy = pltpu.make_async_copy(src, dst, self.sems.at[len(self.copies)])
        copy.start()
        self.copies.append(copy)

    def wait(self):
        for copy in self.copies:
            copy.wait()


def aligned(start, size, unit):
    return pl.ds(pl.multiple_of(start, unit), size)


def inner_pieces(ops, rows, chip, late):
    half = ops // 2
    quarter = half // 2
    step = 0 if late else quarter
    if quarter == 1:
        pieces = []
        for side in range(2):
            slot = (((chip >> 1) ^ 1 ^ side ^ (chip & 1) ^ step) << 1) + side
            pieces.append((slot * rows, rows, side * rows))
        return pieces
    first = (((chip >> 1) ^ step) // quarter) * quarter * 2
    return [(first * rows, half * rows, 0)]


def fetch_sources(ops, blocks, right, chip, core, late, fetches):
    rows, full = blocks[0].shape[2:]
    quarter = ops // 4
    inner = 2 * quarter * rows
    first = inner_pieces(ops, rows, chip, late)[0][0]
    for turn in range(2):
        side = core if turn == 0 else 1 - core
        for index in range(quarter):
            block = blocks[turn * quarter + index]
            step = index if late else quarter + index
            slot = (((chip >> 1) ^ 1 ^ side ^ (chip & 1) ^ step) << 1) + side
            place = side * rows if quarter == 1 else slot * rows - first
            for part in range(2):
                fetches.start(block.at[:, part], right.at[:, aligned(place, rows, rows), pl.ds(part * full, full)])
            fetches.start(block.at[:, 0], right.at[:, aligned(inner + place, rows, rows), pl.ds(full, full)])


def fetch_sinks(ops, blocks, left, chip, core, late, fetches):
    rows = blocks[0].shape[2]
    half = ops // 2
    inner = half * rows
    for turn in range(2):
        side = core if turn == 0 else 1 - core
        for step in range(half):
            block = blocks[turn * half + step]
            slot = side * half + (lax.rem(chip, half) ^ side ^ (chip // half) ^ step)
            for start, size, place in inner_pieces(ops, rows, chip, late):
                for part in range(2):
                    fetches.start(
                        block.at[:, part, :, aligned(start, size, size)],
                        left.at[:, aligned(slot * rows, rows, rows), pl.ds(part * inner + place, size)],
                    )


def jobs_of(half, share, member):
    jobs = [(member * share, share, member * share, share, 0)]
    for apart in range(1, half // 2 + 1):
        if 2 * apart < half:
            jobs.append((member * share, share, lax.rem(member + apart, half) * share, share, 2.0))
        elif share // 2 % LANES:
            jobs.append((member * share, share, lax.rem(member + apart, half) * share, share, 1.0))
        else:
            low = lax.rem(member, half // 2)
            start = low * share + member // (half // 2) * (share // 2)
            jobs.append((start, share // 2, (low + half // 2) * share, share, 2.0))
    return jobs


def products(job, left, right, flip):
    row_start, count, col_start, cols, weight = job
    fields, full = left.shape[0], left.shape[1]
    inner = left.shape[2] // 2
    unit = math.gcd(count, LANES)
    lhs = jnp.concatenate([left[a, aligned(row_start, count, unit), :] for a in range(fields)], 0)
    ahead = []
    for b in range(fields):
        for part in range(2):
            rhs = right[b, :, aligned(part * full + col_start, cols, LANES)]
            ahead.append(jnp.dot(lhs, rhs, preferred_element_type=jnp.float32))
    if not weight:
        return ahead, None
    for b in range(fields):
        real_turned = right[b, :inner, aligned(row_start, count, unit)].T
        imag_turned = right[b, :inner, aligned(full + row_start, count, unit)].T
        flip[b, 0, :count, :inner] = real_turned
        flip[b, 0, :count, inner:] = -imag_turned
        flip[b, 1, :count, :inner] = imag_turned
        flip[b, 1, :count, inner:] = real_turned
    lhs = flip[:, :, :count, :].reshape(fields * 2 * count, 2 * inner)
    rhs = jnp.concatenate([left[a, aligned(col_start, cols, LANES), :] for a in range(fields)], 0)
    return ahead, lax.dot_general(lhs, rhs, (((1,), (1,)), ((), ())), preferred_element_type=jnp.float32)


def fill_signs(right):
    inner, full = right.shape[1] // 2, right.shape[2] // 2
    for b in range(right.shape[0]):
        right[b, inner:, :full] = -right[b, :inner, full:]


def place_in(half, share):
    core = lax.rem(lax.axis_index("tm"), 2)
    chip = lax.axis_index("op")
    return core, chip, jobs_of(half, share, lax.rem(chip, half) // 2 * 2 + core)


def early_kernel(ops, *refs):
    half = ops // 2
    sinks, sources = refs[:ops], refs[ops : ops + half]
    later, partials = refs[ops + half], refs[ops + half + 1 : -4]
    left, right, flip, sems = refs[-4:]
    core, chip, jobs = place_in(half, left.shape[1] // half)
    fetches = Fetches(sems)
    fetch_sources(ops, sources, right, chip, core, False, fetches)
    fetch_sinks(ops, sinks, left, chip, core, False, fetches)
    fetch_sinks(ops, sinks, later, chip, core, True, fetches)
    fetches.wait()
    fill_signs(right)
    at = 0
    for job in jobs:
        ahead, behind = products(job, left, right, flip)
        for index, value in enumerate(ahead):
            partials[at][index] = value
        at += 1
        if behind is not None:
            partials[at][...] = behind
            at += 1


def late_kernel(ops, group, *refs):
    half = ops // 2
    sources, left = refs[:half], refs[half]
    partials = refs[half + 1 : -8]
    weights, columns, out, right, flip, product, flipped, sems = refs[-8:]
    fields, full = left.shape[:2]
    parts = 2 * fields * fields
    core, chip, jobs = place_in(half, full // half)
    fetches = Fetches(sems)
    fetch_sources(ops, sources, right, chip, core, True, fetches)
    fetches.wait()
    fill_signs(right)

    def put(into, lane, at, block):
        cols = block.shape[1]
        for g in range(block.shape[0] // group):
            into[at * group : (at + 1) * group, lane + g * cols : lane + (g + 1) * cols] = block[g * group : (g + 1) * group]

    at = lane = 0
    for job in jobs:
        _, count, _, cols, weight = job
        ahead, behind = products(job, left, right, flip)
        for index, value in enumerate(ahead):
            value = (value + partials[at][index]).astype(jnp.bfloat16)
            for a in range(fields):
                block = value[a * count : (a + 1) * count]
                place = a * fields * 2 + index
                put(product, lane, place, block)
                if behind is None:
                    put(flipped, lane, place, block.T)
        at += 1
        if behind is not None:
            value = (weight * (behind + partials[at][...])).astype(jnp.bfloat16)
            at += 1
            for index in range(fields * 2):
                for a in range(fields):
                    put(flipped, lane, a * fields * 2 + index, value[index * count : (index + 1) * count, a * cols : (a + 1) * cols])
        lane += count // group * cols
    total = lax.dot_general(
        product[...], flipped[...], (((1,), (1,)), ((), ())), preferred_element_type=jnp.float32
    )
    side = parts * group
    row = lax.broadcasted_iota(jnp.int32, (side, side), 0)
    lane = lax.broadcasted_iota(jnp.int32, (side, side), 1)
    total = jnp.where(lax.rem(row, group) == lax.rem(lane, group), total, 0.0)
    total = jnp.sum(total.reshape(parts, group, side), 1)
    source = lax.broadcasted_iota(jnp.int32, (side, LANES), 0)
    lane = lax.broadcasted_iota(jnp.int32, (side, LANES), 1)
    spread = (source // group == lax.rem(lane, parts)).astype(jnp.float32)
    total = jnp.dot(total, spread, precision=lax.Precision.HIGHEST, preferred_element_type=jnp.float32)
    row = lax.broadcasted_iota(jnp.int32, (parts, LANES), 0)
    lane = lax.broadcasted_iota(jnp.int32, (parts, LANES), 1)
    total = jnp.where(lane // parts == row, total, 0.0)
    total = jnp.dot(total, weights[...], precision=lax.Precision.HIGHEST, preferred_element_type=jnp.float32)
    total = jnp.sum(total, 0, keepdims=True) * columns[:1] + columns[1:]
    out[...] = jnp.broadcast_to(total[:, None, :], out.shape)


def chain_weights(chain_factors, chain_target, fields):
    pairs = fields * fields
    parts = 2 * pairs
    codes = (
        (chain_factors[:, 0] * fields + chain_factors[:, 1]) * pairs
        + chain_factors[:, 2] * fields
        + chain_factors[:, 3]
    )
    row = jnp.arange(LANES, dtype=jnp.int32)
    first, second = row // parts, row % parts
    used = row < parts * parts
    ahead = jnp.where(used, (first // 2) * pairs + second // 2, -1)
    behind = jnp.where(used, (second // 2) * pairs + first // 2, -1)
    column = jnp.arange(LANES, dtype=jnp.int32)
    on_row = (ahead[:, None] == codes[None, :]).astype(jnp.float32)
    on_row = 0.5 * (on_row + (behind[:, None] == codes[None, :]).astype(jnp.float32))
    on_column = (chain_target[:, None] == (column % NCORR)[None, :]).astype(jnp.float32)
    counts = jnp.dot(on_row, on_column, precision=lax.Precision.HIGHEST)
    mixed = (first % 2 != second % 2)[:, None]
    both_imag = (first % 2 + second % 2 == 2)[:, None]
    real_sign = jnp.where(mixed, 0.0, jnp.where(both_imag, -1.0, 1.0))
    imag_sign = jnp.where(mixed, 1.0, 0.0)
    sign = jnp.where((column < WIN * NCORR)[None, :], real_sign, imag_sign)
    return counts * sign


def per_device(times, ops, sink_fields, source_fields, source_live, chain_factors, chain_target):
    fields, _, rows, full = sink_fields.shape[1:]
    half = ops // 2
    share = full // half
    parts = 2 * fields * fields
    group = 2 * LANES // parts
    chip = lax.axis_index("op")
    swap = routes(times, ops, lambda pair, core, op: (pair, 1 - core, op))
    sinks = [lax.ppermute(sink_fields[0], AXES, sink_route(times, ops, step)) for step in range(half)]
    sources = [lax.ppermute(source_fields[0], AXES, source_route(times, ops, step)) for step in range(half)]
    sinks = sinks + [lax.ppermute(block, AXES, swap) for block in sinks]
    sources = sources + [lax.ppermute(block, AXES, swap) for block in sources]
    separation = jnp.where(chip // half == lax.rem(chip, 2), 2, 1)
    lane = jnp.arange(LANES, dtype=jnp.int32)
    used = 2 * WIN * NCORR
    wanted = (lane < used) & (lane // NCORR % WIN + 1 == separation)
    scale = jnp.where(wanted, 1.0 / math.sqrt(times), 0.0)
    flag = jnp.where(lane == used, source_live[0].astype(jnp.float32), 0.0)
    columns = jnp.stack([scale, flag]).astype(jnp.float32)
    weights = chain_weights(chain_factors, chain_target, fields)
    any_spec = pl.BlockSpec(memory_space=pl.ANY)
    vmem_spec = pl.BlockSpec(memory_space=pltpu.VMEM)
    quarter = half // 2
    inner = full // 2
    shapes, lanes, most = [], 0, 0
    for _, count, _, cols, weight in jobs_of(half, share, 0):
        shapes.append((fields * 2, fields * count, cols))
        if weight:
            shapes.append((fields * 2 * count, fields * cols))
            most = max(most, count)
        lanes += count // group * cols
    shapes = [jax.ShapeDtypeStruct(shape, jnp.float32) for shape in shapes]
    flop = 4 * 2 * fields * fields * share * full * full
    right_scratch = pltpu.VMEM((fields, 2 * inner, 2 * full), jnp.bfloat16)
    flip_scratch = pltpu.VMEM((fields, 2, most, 2 * inner), jnp.bfloat16)
    later, *partials = pl.pallas_call(
        functools.partial(early_kernel, ops),
        out_shape=[jax.ShapeDtypeStruct((fields, full, 2 * inner), jnp.bfloat16)] + shapes,
        in_specs=[any_spec] * (ops + half),
        out_specs=[vmem_spec] * (1 + len(shapes)),
        scratch_shapes=[
            pltpu.VMEM((fields, full, 2 * inner), jnp.bfloat16),
            right_scratch,
            flip_scratch,
            pltpu.SemaphoreType.DMA((3 * half + 8 * ops,)),
        ],
        compiler_params=pltpu.CompilerParams(vmem_limit_bytes=24 * 1024 * 1024),
        cost_estimate=pl.CostEstimate(flops=flop, bytes_accessed=6 * ops * rows * full, transcendentals=0),
    )(*sinks, *sources[quarter:half], *sources[half + quarter :])
    partial_sums = pl.pallas_call(
        functools.partial(late_kernel, ops, group),
        out_shape=jax.ShapeDtypeStruct((times * ops, 1, LANES), jnp.float32),
        in_specs=[any_spec] * half + [vmem_spec] * (3 + len(shapes)),
        out_specs=vmem_spec,
        scratch_shapes=[
            right_scratch,
            flip_scratch,
            pltpu.VMEM((parts * group, lanes), jnp.bfloat16),
            pltpu.VMEM((parts * group, lanes), jnp.bfloat16),
            pltpu.SemaphoreType.DMA((3 * half,)),
        ],
        compiler_params=pltpu.CompilerParams(vmem_limit_bytes=24 * 1024 * 1024),
        cost_estimate=pl.CostEstimate(flops=flop, bytes_accessed=6 * ops * rows * full, transcendentals=0),
    )(*sources[:quarter], *sources[half : half + quarter], later, *partials, weights, columns)
    shares = lax.all_to_all(partial_sums, AXES, 0, 0, tiled=True)
    totals = pl.pallas_call(
        functools.partial(finish_kernel, ops),
        out_shape=jax.ShapeDtypeStruct((2, WIN, NCORR), jnp.float32),
        in_specs=[vmem_spec],
        out_specs=vmem_spec,
    )(shares.reshape(times * ops, LANES))
    return totals.transpose(0, 2, 1)


def solution(mesh):
    in_specs = (P("tm", None, None, "op", None), P("tm", None, None, "op", None), P("tm"), P(), P())
    body = functools.partial(per_device, mesh.shape["tm"], mesh.shape["op"])
    return jax.shard_map(body, mesh=mesh, in_specs=in_specs, out_specs=P(), check_vma=False)
```

```python
import functools
import math

import jax
import jax.numpy as jnp
import numpy as np
from jax import lax
from jax.experimental import pallas as pl
from jax.experimental.pallas import tpu as pltpu
from jax.sharding import PartitionSpec as P

WIN = 2
NCORR = 16
AXES = ("tm", "op")
LANES = 128


def routes(times, ops, place):
    pairs = []
    for pair in range(times // 2):
        for core in range(2):
            for op in range(ops):
                target = place(pair, core, op)
                if target is not None:
                    to_pair, to_core, to_op = target
                    to_time = (to_pair % (times // 2)) * 2 + to_core
                    pairs.append(((pair * 2 + core) * ops + op, to_time * ops + to_op))
    return pairs


def sink_slot(ops, chip, core, step):
    half = ops // 2
    return core * half + ((chip % half) ^ (chip // half) ^ core ^ step)


def sink_target(ops, core, op, step):
    half = ops // 2
    side = op // half
    return side, core * half + ((op % half) ^ side ^ core ^ step)


def source_slot(ops, chip, core, step):
    return (((chip >> 1) ^ 1 ^ (chip & 1) ^ core ^ step) << 1) + core


def source_lag(ops, chip):
    return 1 - (1 - chip % 2) * (chip // (ops // 2))


def source_target(ops, core, op, step):
    return op & 1, (((op >> 1) ^ 1 ^ (op & 1) ^ core ^ step) << 1) | core


def sink_direct(ops, core, chip):
    return core == chip // (ops // 2)


def source_direct(core, chip):
    return core == chip % 2


def send_blocks(times, ops, sink, source, tables, between):
    def along(block, place):
        return lax.ppermute(block, AXES, routes(times, ops, place))

    def plain_sink(step, only):
        def place(pair, core, op):
            to_core, to_op = sink_target(ops, core, op, step)
            return None if only and not sink_direct(ops, to_core, to_op) else (pair, to_core, to_op)

        return place

    def plain_source(step, only):
        def place(pair, core, op):
            to_core, to_op = source_target(ops, core, op, step)
            to_pair = (pair + source_lag(ops, to_op)) % (times // 2)
            return None if only and not source_direct(to_core, to_op) else (to_pair, to_core, to_op)

        return place

    def sink_on(pair, core, op):
        return pair, core, op if sink_direct(ops, core, op) else op ^ 1

    def source_on(pair, core, op):
        to_op = op ^ 2
        to_pair = (pair - source_lag(ops, op) + source_lag(ops, to_op)) % (times // 2)
        return None if source_direct(core, to_op) else (to_pair, core, to_op)

    def across(block):
        return along(block, lambda pair, core, op: (pair, 1 - core, op))

    here = sink_direct(ops, lax.rem(lax.axis_index("tm"), 2), lax.axis_index("op"))
    sinks, sources, last = [], [], []
    for pair in range(ops // 4):
        first = along(sink, plain_sink(2 * pair + 1, False))
        own = sink if pair == 0 else along(sink, plain_sink(2 * pair, True))
        second = along(jnp.where(here, own, first), sink_on)
        sinks += [first, second, across(first), across(second)]
        first = along(source, plain_source(2 * pair, False))
        late_source, tables = lax.optimization_barrier((source, tables))
        own = along(late_source, plain_source(2 * pair + 1, True))
        last.append(along(first, source_on))
        sources += [first, own, across(first), across(own)]
    done = None if between is None else between(sinks, sources)
    return sinks, sources, last + [across(block) for block in last], done, tables


class Fetches:
    def __init__(self, sems):
        self.sems, self.copies = sems, []

    def start(self, dst, *choices):
        sem = self.sems.at[len(self.copies)]
        taken = None
        for index, (condition, src) in enumerate(choices):
            copy = pltpu.make_async_copy(src, dst, sem)
            if index == len(choices) - 1:
                condition = taken
            elif taken is not None:
                condition, taken = jnp.logical_and(taken, condition), jnp.logical_and(taken, jnp.logical_not(condition))
            else:
                taken = jnp.logical_not(condition)
            if condition is None:
                copy.start()
            else:
                pl.when(condition)(copy.start)
        self.copies.append(copy)

    def wait(self):
        for copy in self.copies:
            copy.wait()


def aligned(start, size, unit):
    return pl.ds(pl.multiple_of(start, unit), size)


def fetch_sinks(ops, sinks, left, lanes, fetches):
    rows = sinks[0].shape[2]
    inner = left.shape[2] // 2
    core, chip = lax.rem(lax.axis_index("tm"), 2), lax.axis_index("op")
    for pair in range(ops // 4):
        for turn in range(2):
            for index in range(2):
                block = sinks[4 * pair + 2 * turn + index]
                slot = sink_slot(ops, chip, core if turn == 0 else 1 - core, 2 * pair + 1 - index)
                for start, size, place in lanes:
                    for part in range(2):
                        fetches.start(
                            left.at[:, aligned(slot * rows, rows, rows), pl.ds(part * inner + place, size)],
                            (None, block.at[:, part, :, aligned(start, size, LANES)]),
                        )


def fetch_source(right, place, fetches, *choices):
    rows, full = choices[0][1].shape[2:]
    inner = right.shape[1] // 2
    at, low = aligned(place, rows, rows), aligned(inner + place, rows, rows)
    for part, dst in ((0, right.at[:, at, :full]), (1, right.at[:, at, full:]), (0, right.at[:, low, full:])):
        fetches.start(dst, *[(condition, block.at[:, part]) for condition, block in choices])


def jobs_of(half, share, member):
    jobs = [(member * share, share, member * share, share, 0)]
    for apart in range(1, half // 2 + 1):
        if 2 * apart < half:
            jobs.append((member * share, share, lax.rem(member + apart, half) * share, share, 2.0))
        elif share // 2 % LANES:
            jobs.append((member * share, share, lax.rem(member + apart, half) * share, share, 1.0))
        else:
            low = lax.rem(member, half // 2)
            start = low * share + member // (half // 2) * (share // 2)
            jobs.append((start, share // 2, (low + half // 2) * share, share, 2.0))
    return jobs


def products(job, left, right, flip):
    row_start, count, col_start, cols, weight = job
    fields, full = left.shape[0], left.shape[1]
    inner = left.shape[2] // 2
    unit = math.gcd(count, LANES)
    lhs = jnp.concatenate([left[a, aligned(row_start, count, unit), :] for a in range(fields)], 0)
    ahead = []
    for b in range(fields):
        for part in range(2):
            rhs = right[b, :, aligned(part * full + col_start, cols, LANES)]
            ahead.append(jnp.dot(lhs, rhs, preferred_element_type=jnp.float32))
    if not weight:
        return ahead, None
    for b in range(fields):
        real_turned = right[b, :inner, aligned(row_start, count, unit)].T
        imag_turned = right[b, :inner, aligned(full + row_start, count, unit)].T
        flip[b, 0, :count, :inner] = real_turned
        flip[b, 0, :count, inner:] = -imag_turned
        flip[b, 1, :count, :inner] = imag_turned
        flip[b, 1, :count, inner:] = real_turned
    lhs = flip[:, :, :count, :].reshape(fields * 2 * count, 2 * inner)
    rhs = jnp.concatenate([left[a, aligned(col_start, cols, LANES), :] for a in range(fields)], 0)
    return ahead, lax.dot_general(lhs, rhs, (((1,), (1,)), ((), ())), preferred_element_type=jnp.float32)


def fill_signs(right):
    inner, full = right.shape[1] // 2, right.shape[2] // 2
    for b in range(right.shape[0]):
        right[b, inner:, :full] = -right[b, :inner, full:]


def place_in(half, share):
    core = lax.rem(lax.axis_index("tm"), 2)
    chip = lax.axis_index("op")
    return core, chip, jobs_of(half, share, lax.rem(chip, half) // 2 * 2 + core)


def late_slot(ops, chip):
    return source_slot(ops, chip, 1 - chip % 2, 1)


def early_kernel(ops, *refs):
    sinks, sources = refs[:ops], refs[ops : 2 * ops]
    later, partials = refs[2 * ops], refs[2 * ops + 1 : -4]
    left, right, flip, sems = refs[-4:]
    rows, full = sinks[0].shape[2:]
    core, chip, jobs = place_in(ops // 2, full // (ops // 2))
    late = late_slot(ops, chip)
    fetches = Fetches(sems)
    lanes = [((index + (index >= late).astype(jnp.int32)) * rows, rows, index * rows) for index in range(ops - 1)]
    fetch_sinks(ops, sinks, left, lanes, fetches)
    fetch_sinks(ops, sinks, later, [(late * rows, rows, 0)], fetches)

    def packed(side, step):
        slot = source_slot(ops, chip, side, step)
        return (slot - (slot > late).astype(jnp.int32)) * rows

    fetch_source(right, packed(core, 0), fetches, (None, sources[0]))
    fetch_source(right, packed(1 - core, 0), fetches, (None, sources[2]))
    fetch_source(right, packed(chip % 2, 1), fetches, (core == chip % 2, sources[1]), (None, sources[3]))
    fetches.wait()
    fill_signs(right)
    at = 0
    for job in jobs:
        ahead, behind = products(job, left, right, flip)
        for index, value in enumerate(ahead):
            partials[at][index] = value
        at += 1
        if behind is not None:
            partials[at][...] = behind
            at += 1


def late_kernel(ops, group, *refs):
    last, last_across, left = refs[:3]
    partials = refs[3:-8]
    weights, columns, out, right, flip, product, flipped, sems = refs[-8:]
    core, chip, jobs = place_in(ops // 2, left.shape[1] // (ops // 2))
    fetches = Fetches(sems)
    fetch_source(right, 0, fetches, (core == 1 - chip % 2, last), (None, last_across))
    fetches.wait()
    fill_signs(right)
    trace_rows(group, jobs, left, right, flip, partials, weights, columns, out, product, flipped)


def whole_kernel(ops, group, *refs):
    half = ops // 2
    sinks, sources, last = refs[:ops], refs[ops : 2 * ops], refs[2 * ops : 2 * ops + half]
    weights, columns, out, left, right, flip, product, flipped, sems = refs[2 * ops + half :]
    rows, full = sinks[0].shape[2:]
    core, chip, jobs = place_in(half, full // half)
    fetches = Fetches(sems)
    fetch_sinks(ops, sinks, left, [(0, full, 0)], fetches)
    for pair in range(ops // 4):
        for turn in range(2):
            side = core if turn == 0 else 1 - core
            first, own = sources[4 * pair + 2 * turn : 4 * pair + 2 * turn + 2]
            fetch_source(right, source_slot(ops, chip, side, 2 * pair) * rows, fetches, (None, first))
            direct = source_direct(side, chip)
            passed = last[turn * (ops // 4) + pair]
            fetch_source(right, source_slot(ops, chip, side, 2 * pair + 1) * rows, fetches, (direct, own), (None, passed))
    fetches.wait()
    fill_signs(right)
    trace_rows(group, jobs, left, right, flip, None, weights, columns, out, product, flipped)


def trace_rows(group, jobs, left, right, flip, partials, weights, columns, out, product, flipped):
    fields = left.shape[0]
    parts = 2 * fields * fields

    def put(into, lane, at, block):
        cols = block.shape[1]
        for g in range(block.shape[0] // group):
            into[at * group : (at + 1) * group, lane + g * cols : lane + (g + 1) * cols] = block[g * group : (g + 1) * group]

    at = lane = 0
    for job in jobs:
        _, count, _, cols, weight = job
        ahead, behind = products(job, left, right, flip)
        for index, value in enumerate(ahead):
            value = (value if partials is None else value + partials[at][index]).astype(jnp.bfloat16)
            for a in range(fields):
                block = value[a * count : (a + 1) * count]
                place = a * fields * 2 + index
                put(product, lane, place, block)
                if behind is None:
                    put(flipped, lane, place, block.T)
        at += 1
        if behind is not None:
            behind = behind if partials is None else behind + partials[at][...]
            value = (weight * behind).astype(jnp.bfloat16)
            at += 1
            for index in range(fields * 2):
                for a in range(fields):
                    block = value[index * count : (index + 1) * count, a * cols : (a + 1) * cols]
                    put(flipped, lane, a * fields * 2 + index, block)
        lane += count // group * cols
    total = lax.dot_general(
        product[...], flipped[...], (((1,), (1,)), ((), ())), preferred_element_type=jnp.float32
    )
    side = parts * group
    row = lax.broadcasted_iota(jnp.int32, (side, side), 0)
    lane = lax.broadcasted_iota(jnp.int32, (side, side), 1)
    total = jnp.where(lax.rem(row, group) == lax.rem(lane, group), total, 0.0)
    total = jnp.sum(total.reshape(parts, group, side), 1)
    source = lax.broadcasted_iota(jnp.int32, (side, LANES), 0)
    lane = lax.broadcasted_iota(jnp.int32, (side, LANES), 1)
    spread = (source // group == lax.rem(lane, parts)).astype(jnp.float32)
    total = jnp.dot(total, spread, precision=lax.Precision.HIGHEST, preferred_element_type=jnp.float32)
    row = lax.broadcasted_iota(jnp.int32, (parts, LANES), 0)
    lane = lax.broadcasted_iota(jnp.int32, (parts, LANES), 1)
    total = jnp.where(lane // parts == row, total, 0.0)
    total = jnp.dot(total, weights[...], precision=lax.Precision.HIGHEST, preferred_element_type=jnp.float32)
    total = jnp.sum(total, 0, keepdims=True) * columns[:1] + columns[1:]
    out[...] = jnp.broadcast_to(total[:, None, :], out.shape)


def chain_weights(chain_factors, chain_target, fields):
    pairs = fields * fields
    parts = 2 * pairs
    codes = (
        (chain_factors[:, 0] * fields + chain_factors[:, 1]) * pairs
        + chain_factors[:, 2] * fields
        + chain_factors[:, 3]
    )
    row = jnp.arange(LANES, dtype=jnp.int32)
    first, second = row // parts, row % parts
    used = row < parts * parts
    ahead = jnp.where(used, (first // 2) * pairs + second // 2, -1)
    behind = jnp.where(used, (second // 2) * pairs + first // 2, -1)
    column = jnp.arange(LANES, dtype=jnp.int32)
    on_row = (ahead[:, None] == codes[None, :]).astype(jnp.float32)
    on_row = 0.5 * (on_row + (behind[:, None] == codes[None, :]).astype(jnp.float32))
    on_column = (chain_target[:, None] == (column % NCORR)[None, :]).astype(jnp.float32)
    counts = jnp.dot(on_row, on_column, precision=lax.Precision.HIGHEST)
    mixed = (first % 2 != second % 2)[:, None]
    both_imag = (first % 2 + second % 2 == 2)[:, None]
    real_sign = jnp.where(mixed, 0.0, jnp.where(both_imag, -1.0, 1.0))
    imag_sign = jnp.where(mixed, 1.0, 0.0)
    sign = jnp.where((column < WIN * NCORR)[None, :], real_sign, imag_sign)
    return counts * sign


def source_times(times, ops):
    table = np.zeros((times, ops, times), np.float32)
    for time in range(times):
        for chip in range(ops):
            pair = (time // 2 - source_lag(ops, chip)) % (times // 2)
            table[time, chip, pair * 2 + chip % 2] = 1
    return table


def per_device(times, ops, sink_fields, source_fields, source_live, chain_factors, chain_target):
    fields, _, rows, full = sink_fields.shape[1:]
    half = ops // 2
    share = full // half
    parts = 2 * fields * fields
    group = 2 * LANES // parts
    chip = lax.axis_index("op")
    separation = jnp.where(chip // half == lax.rem(chip, 2), 2, 1)
    lane = jnp.arange(LANES, dtype=jnp.int32)
    used = 2 * WIN * NCORR
    wanted = (lane < used) & (lane // NCORR % WIN + 1 == separation)
    scale = jnp.where(wanted, 1.0 / math.sqrt(times), 0.0)
    flag = jnp.where(lane == used, source_live[0].astype(jnp.float32), 0.0)
    columns = jnp.stack([scale, flag]).astype(jnp.float32)
    weights = chain_weights(chain_factors, chain_target, fields)

    any_spec = pl.BlockSpec(memory_space=pl.ANY)
    vmem_spec = pl.BlockSpec(memory_space=pltpu.VMEM)
    shapes, lanes, most = [], 0, 0
    for _, count, _, cols, weight in jobs_of(half, share, 0):
        shapes.append((fields * 2, fields * count, cols))
        if weight:
            shapes.append((fields * 2 * count, fields * cols))
            most = max(most, count)
        lanes += count // group * cols
    shapes = [jax.ShapeDtypeStruct(shape, jnp.float32) for shape in shapes]
    flop = 4 * 2 * fields * fields * share * full * full

    def call(kernel, out_shape, any_specs, vmem_specs, scratch, copies, flop):
        return pl.pallas_call(
            kernel,
            out_shape=out_shape,
            in_specs=[any_spec] * any_specs + [vmem_spec] * vmem_specs,
            out_specs=jax.tree.map(lambda _: vmem_spec, out_shape),
            scratch_shapes=scratch + [pltpu.SemaphoreType.DMA((copies,))],
            compiler_params=pltpu.CompilerParams(vmem_limit_bytes=24 * 1024 * 1024),
            cost_estimate=pl.CostEstimate(flops=flop, bytes_accessed=flop // 1000, transcendentals=0),
        )

    def scratches(inner):
        return [
            pltpu.VMEM((fields, 2 * inner, 2 * full), jnp.bfloat16),
            pltpu.VMEM((fields, 2, most, 2 * inner), jnp.bfloat16),
        ]

    out_shape = jax.ShapeDtypeStruct((times * ops, 1, LANES), jnp.float32)
    stacks = [pltpu.VMEM((parts * group, lanes), jnp.bfloat16)] * 2
    split = ops == 4 and rows % LANES == 0

    def early(sinks, sources):
        inner = full - rows
        return call(
            functools.partial(early_kernel, ops),
            [jax.ShapeDtypeStruct((fields, full, 2 * rows), jnp.bfloat16)] + shapes,
            2 * ops,
            0,
            [pltpu.VMEM((fields, full, 2 * inner), jnp.bfloat16)] + scratches(inner),
            8 * ops + 9,
            1000,
        )(*sinks, *sources)

    sinks, sources, last, done, (weights, columns) = send_blocks(
        times, ops, sink_fields[0], source_fields[0], (weights, columns), early if split else None
    )
    if split:
        partial_sums = call(
            functools.partial(late_kernel, ops, group), out_shape, 2, 3 + len(shapes), scratches(rows) + stacks, 3, flop
        )(*last, *done, weights, columns)
    else:
        partial_sums = call(
            functools.partial(whole_kernel, ops, group),
            out_shape,
            2 * ops + half,
            2,
            [pltpu.VMEM((fields, full, 2 * full), jnp.bfloat16)] + scratches(full) + stacks,
            5 * ops,
            flop,
        )(*sinks, *sources, *last, weights, columns)
    shares = lax.all_to_all(partial_sums, AXES, 0, 0, tiled=True).reshape(times, ops, LANES)
    live = shares[:, 0, used]
    weight = jnp.sum(source_times(times, ops) * live, -1)
    totals = jnp.sum(shares * weight[:, :, None], (0, 1))[:used]
    return totals.reshape(2, WIN, NCORR).transpose(0, 2, 1)


def solution(mesh):
    in_specs = (P("tm", None, None, "op", None), P("tm", None, None, "op", None), P("tm"), P(), P())
    body = functools.partial(per_device, mesh.shape["tm"], mesh.shape["op"])
    return jax.shard_map(body, mesh=mesh, in_specs=in_specs, out_specs=P(), check_vma=False)
```

```python
import functools
import math

import jax
import jax.numpy as jnp
import numpy as np
from jax import lax
from jax.experimental import pallas as pl
from jax.experimental.pallas import tpu as pltpu
from jax.sharding import PartitionSpec as P

WIN = 2
NCORR = 16
AXES = ("tm", "op")
LANES = 128


def routes(times, ops, place):
    pairs = []
    for pair in range(times // 2):
        for core in range(2):
            for op in range(ops):
                target = place(pair, core, op)
                if target is not None:
                    to_pair, to_core, to_op = target
                    to_time = (to_pair % (times // 2)) * 2 + to_core
                    pairs.append(((pair * 2 + core) * ops + op, to_time * ops + to_op))
    return pairs


def sink_slot(ops, chip, core, step):
    half = ops // 2
    return core * half + ((chip % half) ^ (chip // half) ^ core ^ step)


def sink_target(ops, core, op, step):
    half = ops // 2
    side = op // half
    return side, core * half + ((op % half) ^ side ^ core ^ step)


def source_slot(ops, chip, core, step):
    low = core ^ (chip // (ops // 2)) ^ (chip & 1) ^ 1
    return (((chip >> 1) ^ 1 ^ (chip & 1) ^ low ^ step) << 1) + low


def source_lag(ops, chip):
    return 1 - (1 - chip % 2) * (chip // (ops // 2))


def source_target(ops, core, op, step):
    target = (((op >> 1) ^ 1 ^ (op & 1) ^ core ^ step) << 1) | core
    return (op & 1) ^ core ^ 1 ^ (target // (ops // 2)), target


def sink_holder(ops, core, chip):
    return core == chip // (ops // 2)


def send_blocks(times, ops, sink, source, tables):
    def along(block, place):
        return lax.ppermute(block, AXES, routes(times, ops, place))

    def plain_sink(step, only):
        def place(pair, core, op):
            to_core, to_op = sink_target(ops, core, op, step)
            return None if only and not sink_holder(ops, to_core, to_op) else (pair, to_core, to_op)

        return place

    def plain_source(step, only):
        def place(pair, core, op):
            to_core, to_op = source_target(ops, core, op, step)
            to_pair = pair + source_lag(ops, to_op)
            return None if only and sink_holder(ops, to_core, to_op) else (to_pair, to_core, to_op)

        return place

    def pass_on(pair, core, op):
        if not sink_holder(ops, core, op):
            return pair, core, op ^ 1
        to_op = op ^ 2
        return pair - source_lag(ops, op) + source_lag(ops, to_op), to_op // (ops // 2), to_op

    def across(block):
        return along(block, lambda pair, core, op: (pair, 1 - core, op))

    holder = sink_holder(ops, lax.rem(lax.axis_index("tm"), 2), lax.axis_index("op"))
    blocks = []
    for pair in range(ops // 4):
        sink_first = along(sink, plain_sink(2 * pair + 1, False))
        source_first = along(source, plain_source(2 * pair, False))
        passed = along(jnp.where(holder, source_first, sink_first), pass_on)
        late_source, tables = lax.optimization_barrier((source, tables))
        source_own = along(late_source, plain_source(2 * pair + 1, True))
        sink_own = sink if pair == 0 else along(sink, plain_sink(2 * pair, True))
        own = jnp.where(holder, sink_own, source_own)
        four = [sink_first, source_first, own, passed]
        blocks += four + [across(block) for block in four]
    return blocks, tables


class Fetches:
    def __init__(self, sems):
        self.sems, self.copies = sems, []

    def start(self, dst, *choices):
        sem = self.sems.at[len(self.copies)]
        taken = None
        for index, (condition, src) in enumerate(choices):
            copy = pltpu.make_async_copy(src, dst, sem)
            if index == len(choices) - 1:
                condition = taken
            elif taken is not None:
                condition, taken = jnp.logical_and(taken, condition), jnp.logical_and(taken, jnp.logical_not(condition))
            else:
                taken = jnp.logical_not(condition)
            if condition is None:
                copy.start()
            else:
                pl.when(condition)(copy.start)
        self.copies.append(copy)

    def wait(self):
        for copy in self.copies:
            copy.wait()


def aligned(start, size, unit):
    return pl.ds(pl.multiple_of(start, unit), size)


def fetch_source(right, place, fetches, *choices):
    rows, full = choices[0][1].shape[2:]
    inner = right.shape[1] // 2
    at, low = aligned(place, rows, rows), aligned(inner + place, rows, rows)
    for part, dst in ((0, right.at[:, at, :full]), (1, right.at[:, at, full:]), (0, right.at[:, low, full:])):
        fetches.start(dst, *[(condition, block.at[:, part]) for condition, block in choices])


def jobs_of(half, share, member):
    jobs = [(member * share, share, member * share, share, 0)]
    for apart in range(1, half // 2 + 1):
        if 2 * apart < half:
            jobs.append((member * share, share, lax.rem(member + apart, half) * share, share, 2.0))
        elif share // 2 % LANES:
            jobs.append((member * share, share, lax.rem(member + apart, half) * share, share, 1.0))
        else:
            low = lax.rem(member, half // 2)
            start = low * share + member // (half // 2) * (share // 2)
            jobs.append((start, share // 2, (low + half // 2) * share, share, 2.0))
    return jobs


def products(job, left, right, flip):
    row_start, count, col_start, cols, weight = job
    fields, full = left.shape[0], left.shape[1]
    inner = left.shape[2] // 2
    unit = math.gcd(count, LANES)
    lhs = jnp.concatenate([left[a, aligned(row_start, count, unit), :] for a in range(fields)], 0)
    ahead = []
    for b in range(fields):
        for part in range(2):
            rhs = right[b, :, aligned(part * full + col_start, cols, LANES)]
            ahead.append(jnp.dot(lhs, rhs, preferred_element_type=jnp.float32))
    if not weight:
        return ahead, None
    for b in range(fields):
        real_turned = right[b, :inner, aligned(row_start, count, unit)].T
        imag_turned = right[b, :inner, aligned(full + row_start, count, unit)].T
        flip[b, 0, :count, :inner] = real_turned
        flip[b, 0, :count, inner:] = -imag_turned
        flip[b, 1, :count, :inner] = imag_turned
        flip[b, 1, :count, inner:] = real_turned
    lhs = flip[:, :, :count, :].reshape(fields * 2 * count, 2 * inner)
    rhs = jnp.concatenate([left[a, aligned(col_start, cols, LANES), :] for a in range(fields)], 0)
    return ahead, lax.dot_general(lhs, rhs, (((1,), (1,)), ((), ())), preferred_element_type=jnp.float32)


def fill_signs(right):
    inner, full = right.shape[1] // 2, right.shape[2] // 2
    for b in range(right.shape[0]):
        right[b, inner:, :full] = -right[b, :inner, full:]


def place_in(half, share):
    core = lax.rem(lax.axis_index("tm"), 2)
    chip = lax.axis_index("op")
    return core, chip, jobs_of(half, share, lax.rem(chip, half) // 2 * 2 + core)


def trace_kernel(ops, group, *refs):
    half = ops // 2
    many = 8 * (ops // 4)
    blocks = refs[:many]
    weights, columns, out, left, right, flip, product, flipped, sems = refs[many:]
    rows, full = blocks[0].shape[2:]
    core, chip, jobs = place_in(half, full // half)
    fetches = Fetches(sems)
    for pair in range(ops // 4):
        for turn in range(2):
            side = core if turn == 0 else 1 - core
            sink_first, source_first, own, passed = blocks[8 * pair + 4 * turn : 8 * pair + 4 * turn + 4]
            holder = sink_holder(ops, side, chip)
            for step, choices in (
                (2 * pair, [(None, source_first)]),
                (2 * pair + 1, [(holder, passed), (None, own)]),
            ):
                fetch_source(right, source_slot(ops, chip, side, step) * rows, fetches, *choices)
            for step, choices in ((2 * pair + 1, [(None, sink_first)]), (2 * pair, [(holder, own), (None, passed)])):
                at = aligned(sink_slot(ops, chip, side, step) * rows, rows, rows)
                for part in range(2):
                    fetches.start(
                        left.at[:, at, pl.ds(part * full, full)],
                        *[(condition, block.at[:, part]) for condition, block in choices],
                    )
    fetches.wait()
    fill_signs(right)
    trace_rows(group, jobs, left, right, flip, weights, columns, out, product, flipped)


def trace_rows(group, jobs, left, right, flip, weights, columns, out, product, flipped):
    fields = left.shape[0]
    parts = 2 * fields * fields

    def put(into, lane, at, block):
        cols = block.shape[1]
        for g in range(block.shape[0] // group):
            into[at * group : (at + 1) * group, lane + g * cols : lane + (g + 1) * cols] = block[g * group : (g + 1) * group]

    lane = 0
    for job in jobs:
        _, count, _, cols, weight = job
        ahead, behind = products(job, left, right, flip)
        for index, value in enumerate(ahead):
            value = value.astype(jnp.bfloat16)
            for a in range(fields):
                block = value[a * count : (a + 1) * count]
                place = a * fields * 2 + index
                put(product, lane, place, block)
                if behind is None:
                    put(flipped, lane, place, block.T)
        if behind is not None:
            value = (weight * behind).astype(jnp.bfloat16)
            for index in range(fields * 2):
                for a in range(fields):
                    block = value[index * count : (index + 1) * count, a * cols : (a + 1) * cols]
                    put(flipped, lane, a * fields * 2 + index, block)
        lane += count // group * cols
    total = lax.dot_general(
        product[...], flipped[...], (((1,), (1,)), ((), ())), preferred_element_type=jnp.float32
    )
    side = parts * group
    row = lax.broadcasted_iota(jnp.int32, (side, side), 0)
    lane = lax.broadcasted_iota(jnp.int32, (side, side), 1)
    total = jnp.where(lax.rem(row, group) == lax.rem(lane, group), total, 0.0)
    total = jnp.sum(total.reshape(parts, group, side), 1)
    source = lax.broadcasted_iota(jnp.int32, (side, LANES), 0)
    lane = lax.broadcasted_iota(jnp.int32, (side, LANES), 1)
    spread = (source // group == lax.rem(lane, parts)).astype(jnp.float32)
    total = jnp.dot(total, spread, precision=lax.Precision.HIGHEST, preferred_element_type=jnp.float32)
    row = lax.broadcasted_iota(jnp.int32, (parts, LANES), 0)
    lane = lax.broadcasted_iota(jnp.int32, (parts, LANES), 1)
    total = jnp.where(lane // parts == row, total, 0.0)
    total = jnp.dot(total, weights[...], precision=lax.Precision.HIGHEST, preferred_element_type=jnp.float32)
    total = jnp.sum(total, 0, keepdims=True) * columns[:1] + columns[1:]
    out[...] = jnp.broadcast_to(total[:, None, :], out.shape)


def chain_weights(chain_factors, chain_target, fields):
    pairs = fields * fields
    parts = 2 * pairs
    codes = (
        (chain_factors[:, 0] * fields + chain_factors[:, 1]) * pairs
        + chain_factors[:, 2] * fields
        + chain_factors[:, 3]
    )
    row = jnp.arange(LANES, dtype=jnp.int32)
    first, second = row // parts, row % parts
    used = row < parts * parts
    ahead = jnp.where(used, (first // 2) * pairs + second // 2, -1)
    behind = jnp.where(used, (second // 2) * pairs + first // 2, -1)
    column = jnp.arange(LANES, dtype=jnp.int32)
    on_row = (ahead[:, None] == codes[None, :]).astype(jnp.float32)
    on_row = 0.5 * (on_row + (behind[:, None] == codes[None, :]).astype(jnp.float32))
    on_column = (chain_target[:, None] == (column % NCORR)[None, :]).astype(jnp.float32)
    counts = jnp.dot(on_row, on_column, precision=lax.Precision.HIGHEST)
    mixed = (first % 2 != second % 2)[:, None]
    both_imag = (first % 2 + second % 2 == 2)[:, None]
    real_sign = jnp.where(mixed, 0.0, jnp.where(both_imag, -1.0, 1.0))
    imag_sign = jnp.where(mixed, 1.0, 0.0)
    sign = jnp.where((column < WIN * NCORR)[None, :], real_sign, imag_sign)
    return counts * sign


def source_times(times, ops):
    table = np.zeros((times, ops, times), np.float32)
    for time in range(times):
        for chip in range(ops):
            pair = (time // 2 - source_lag(ops, chip)) % (times // 2)
            table[time, chip, pair * 2 + chip % 2] = 1
    return table


def per_device(times, ops, sink_fields, source_fields, source_live, chain_factors, chain_target):
    fields, _, rows, full = sink_fields.shape[1:]
    half = ops // 2
    share = full // half
    parts = 2 * fields * fields
    group = 2 * LANES // parts
    chip = lax.axis_index("op")
    separation = jnp.where(chip // half == lax.rem(chip, 2), 2, 1)
    lane = jnp.arange(LANES, dtype=jnp.int32)
    used = 2 * WIN * NCORR
    wanted = (lane < used) & (lane // NCORR % WIN + 1 == separation)
    scale = jnp.where(wanted, 1.0 / math.sqrt(times), 0.0)
    flag = jnp.where(lane == used, source_live[0].astype(jnp.float32), 0.0)
    columns = jnp.stack([scale, flag]).astype(jnp.float32)
    weights = chain_weights(chain_factors, chain_target, fields)

    any_spec = pl.BlockSpec(memory_space=pl.ANY)
    vmem_spec = pl.BlockSpec(memory_space=pltpu.VMEM)
    jobs = jobs_of(half, share, 0)
    lanes = sum(count // group * cols for _, count, _, cols, _ in jobs)
    most = max(count for _, count, _, _, weight in jobs if weight)
    blocks, (weights, columns) = send_blocks(times, ops, sink_fields[0], source_fields[0], (weights, columns))
    partial_sums = pl.pallas_call(
        functools.partial(trace_kernel, ops, group),
        out_shape=jax.ShapeDtypeStruct((times * ops, 1, LANES), jnp.float32),
        in_specs=[any_spec] * len(blocks) + [vmem_spec] * 2,
        out_specs=vmem_spec,
        scratch_shapes=[
            pltpu.VMEM((fields, full, 2 * full), jnp.bfloat16),
            pltpu.VMEM((fields, 2 * full, 2 * full), jnp.bfloat16),
            pltpu.VMEM((fields, 2, most, 2 * full), jnp.bfloat16),
            pltpu.VMEM((parts * group, lanes), jnp.bfloat16),
            pltpu.VMEM((parts * group, lanes), jnp.bfloat16),
            pltpu.SemaphoreType.DMA((5 * ops,)),
        ],
        compiler_params=pltpu.CompilerParams(vmem_limit_bytes=24 * 1024 * 1024),
        cost_estimate=pl.CostEstimate(
            flops=4 * 2 * fields * fields * share * full * full, bytes_accessed=10 * ops * rows * full, transcendentals=0
        ),
    )(*blocks, weights, columns)
    shares = lax.all_to_all(partial_sums, AXES, 0, 0, tiled=True).reshape(times, ops, LANES)
    live = shares[:, 0, used]
    weight = jnp.sum(source_times(times, ops) * live, -1)
    totals = jnp.sum(shares * weight[:, :, None], (0, 1))[:used]
    return totals.reshape(2, WIN, NCORR).transpose(0, 2, 1)


def solution(mesh):
    in_specs = (P("tm", None, None, "op", None), P("tm", None, None, "op", None), P("tm"), P(), P())
    body = functools.partial(per_device, mesh.shape["tm"], mesh.shape["op"])
    return jax.shard_map(body, mesh=mesh, in_specs=in_specs, out_specs=P(), check_vma=False)
```

```python
import functools
import math

import jax
import jax.numpy as jnp
from jax import lax
from jax.experimental import pallas as pl
from jax.experimental.pallas import tpu as pltpu
from jax.sharding import PartitionSpec as P

WIN = 2
NCORR = 16
AXES = ("tm", "op")
LANES = 128


def routes(times, ops, place):
    pairs = []
    for pair in range(times // 2):
        for core in range(2):
            for op in range(ops):
                target = place(pair, core, op)
                if target is not None:
                    to_pair, to_core, to_op = target
                    to_time = (to_pair % (times // 2)) * 2 + to_core
                    pairs.append(((pair * 2 + core) * ops + op, to_time * ops + to_op))
    return pairs


def sink_slot(ops, chip, core, step):
    half = ops // 2
    return core * half + ((chip % half) ^ (chip // half) ^ core ^ step)


def sink_target(ops, core, op, step):
    half = ops // 2
    side = op // half
    return side, core * half + ((op % half) ^ side ^ core ^ step)


def source_slot(ops, chip, core, step):
    low = core ^ (chip // (ops // 2)) ^ (chip & 1) ^ 1
    return (((chip >> 1) ^ 1 ^ (chip & 1) ^ low ^ step) << 1) + low


def source_lag(ops, chip):
    return 1 - (1 - chip % 2) * (chip // (ops // 2))


def source_target(ops, core, op, step):
    target = (((op >> 1) ^ 1 ^ (op & 1) ^ core ^ step) << 1) | core
    return (op & 1) ^ core ^ 1 ^ (target // (ops // 2)), target


def sink_holder(ops, core, chip):
    return core == chip // (ops // 2)


def send_blocks(times, ops, sink, source, tables):
    def along(block, place):
        return lax.ppermute(block, AXES, routes(times, ops, place))

    def plain_sink(step, only):
        def place(pair, core, op):
            to_core, to_op = sink_target(ops, core, op, step)
            return None if only and not sink_holder(ops, to_core, to_op) else (pair, to_core, to_op)

        return place

    def plain_source(step, only):
        def place(pair, core, op):
            to_core, to_op = source_target(ops, core, op, step)
            to_pair = pair + source_lag(ops, to_op)
            return None if only and sink_holder(ops, to_core, to_op) else (to_pair, to_core, to_op)

        return place

    def pass_on(pair, core, op):
        if not sink_holder(ops, core, op):
            return pair, core, op ^ 1
        to_op = op ^ 2
        return pair - source_lag(ops, op) + source_lag(ops, to_op), to_op // (ops // 2), to_op

    def across(block):
        return along(block, lambda pair, core, op: (pair, 1 - core, op))

    holder = sink_holder(ops, lax.rem(lax.axis_index("tm"), 2), lax.axis_index("op"))
    blocks = []
    for pair in range(ops // 4):
        sink_first = along(sink, plain_sink(2 * pair + 1, False))
        source_first = along(source, plain_source(2 * pair, False))
        passed = along(jnp.where(holder, source_first, sink_first), pass_on)
        late_source, tables = lax.optimization_barrier((source, tables))
        source_own = along(late_source, plain_source(2 * pair + 1, True))
        sink_own = sink if pair == 0 else along(sink, plain_sink(2 * pair, True))
        own = jnp.where(holder, sink_own, source_own)
        four = [sink_first, source_first, own, passed]
        blocks += four + [across(block) for block in four]
    return blocks, tables


class Fetches:
    def __init__(self, sems):
        self.sems, self.copies = sems, []

    def start(self, dst, *choices):
        sem = self.sems.at[len(self.copies)]
        taken = None
        for index, (condition, src) in enumerate(choices):
            copy = pltpu.make_async_copy(src, dst, sem)
            if index == len(choices) - 1:
                condition = taken
            elif taken is not None:
                condition, taken = jnp.logical_and(taken, condition), jnp.logical_and(taken, jnp.logical_not(condition))
            else:
                taken = jnp.logical_not(condition)
            if condition is None:
                copy.start()
            else:
                pl.when(condition)(copy.start)
        self.copies.append(copy)

    def wait(self):
        for copy in self.copies:
            copy.wait()


def aligned(start, size, unit):
    return pl.ds(pl.multiple_of(start, unit), size)


def fetch_source(right, place, fetches, *choices):
    rows, full = choices[0][1].shape[2:]
    inner = right.shape[1] // 2
    at, low = aligned(place, rows, rows), aligned(inner + place, rows, rows)
    for part, dst in ((0, right.at[:, at, :full]), (1, right.at[:, at, full:]), (0, right.at[:, low, full:])):
        fetches.start(dst, *[(condition, block.at[:, part]) for condition, block in choices])


def jobs_of(half, share, member):
    jobs = [(member * share, share, member * share, share, 0)]
    for apart in range(1, half // 2 + 1):
        if 2 * apart < half:
            jobs.append((member * share, share, lax.rem(member + apart, half) * share, share, 2.0))
        elif share // 2 % LANES:
            jobs.append((member * share, share, lax.rem(member + apart, half) * share, share, 1.0))
        else:
            low = lax.rem(member, half // 2)
            start = low * share + member // (half // 2) * (share // 2)
            jobs.append((start, share // 2, (low + half // 2) * share, share, 2.0))
    return jobs


def products(job, left, right, flip):
    row_start, count, col_start, cols, weight = job
    fields, full = left.shape[0], left.shape[1]
    inner = left.shape[2] // 2
    unit = math.gcd(count, LANES)
    lhs = jnp.concatenate([left[a, aligned(row_start, count, unit), :] for a in range(fields)], 0)
    ahead = []
    for b in range(fields):
        for part in range(2):
            rhs = right[b, :, aligned(part * full + col_start, cols, LANES)]
            ahead.append(jnp.dot(lhs, rhs, preferred_element_type=jnp.float32))
    if not weight:
        return ahead, None
    for b in range(fields):
        real_turned = right[b, :inner, aligned(row_start, count, unit)].T
        imag_turned = right[b, :inner, aligned(full + row_start, count, unit)].T
        flip[b, 0, :count, :inner] = real_turned
        flip[b, 0, :count, inner:] = -imag_turned
        flip[b, 1, :count, :inner] = imag_turned
        flip[b, 1, :count, inner:] = real_turned
    lhs = flip[:, :, :count, :].reshape(fields * 2 * count, 2 * inner)
    rhs = jnp.concatenate([left[a, aligned(col_start, cols, LANES), :] for a in range(fields)], 0)
    return ahead, lax.dot_general(lhs, rhs, (((1,), (1,)), ((), ())), preferred_element_type=jnp.float32)


def fill_signs(right):
    inner, full = right.shape[1] // 2, right.shape[2] // 2
    for b in range(right.shape[0]):
        right[b, inner:, :full] = -right[b, :inner, full:]


def place_in(half, share):
    core = lax.rem(lax.axis_index("tm"), 2)
    chip = lax.axis_index("op")
    return core, chip, jobs_of(half, share, lax.rem(chip, half) // 2 * 2 + core)


def trace_kernel(ops, group, *refs):
    half = ops // 2
    many = 8 * (ops // 4)
    blocks = refs[:many]
    weights, columns, out, left, right, flip, product, flipped, sems = refs[many:]
    rows, full = blocks[0].shape[2:]
    core, chip, jobs = place_in(half, full // half)
    fetches = Fetches(sems)
    for pair in range(ops // 4):
        for turn in range(2):
            side = core if turn == 0 else 1 - core
            sink_first, source_first, own, passed = blocks[8 * pair + 4 * turn : 8 * pair + 4 * turn + 4]
            holder = sink_holder(ops, side, chip)
            for step, choices in (
                (2 * pair, [(None, source_first)]),
                (2 * pair + 1, [(holder, passed), (None, own)]),
            ):
                fetch_source(right, source_slot(ops, chip, side, step) * rows, fetches, *choices)
            for step, choices in ((2 * pair + 1, [(None, sink_first)]), (2 * pair, [(holder, own), (None, passed)])):
                at = aligned(sink_slot(ops, chip, side, step) * rows, rows, rows)
                for part in range(2):
                    fetches.start(
                        left.at[:, at, pl.ds(part * full, full)],
                        *[(condition, block.at[:, part]) for condition, block in choices],
                    )
    fetches.wait()
    fill_signs(right)
    trace_rows(group, jobs, left, right, flip, weights, columns, out, product, flipped)


def trace_rows(group, jobs, left, right, flip, weights, columns, out, product, flipped):
    fields = left.shape[0]
    parts = 2 * fields * fields

    def put(into, lane, at, block):
        cols = block.shape[1]
        for g in range(block.shape[0] // group):
            into[at * group : (at + 1) * group, lane + g * cols : lane + (g + 1) * cols] = block[g * group : (g + 1) * group]

    lane = 0
    for job in jobs:
        _, count, _, cols, weight = job
        ahead, behind = products(job, left, right, flip)
        for index, value in enumerate(ahead):
            value = value.astype(jnp.bfloat16)
            for a in range(fields):
                block = value[a * count : (a + 1) * count]
                place = a * fields * 2 + index
                put(product, lane, place, block)
                if behind is None:
                    put(flipped, lane, place, block.T)
        if behind is not None:
            value = (weight * behind).astype(jnp.bfloat16)
            for index in range(fields * 2):
                for a in range(fields):
                    block = value[index * count : (index + 1) * count, a * cols : (a + 1) * cols]
                    put(flipped, lane, a * fields * 2 + index, block)
        lane += count // group * cols
    total = lax.dot_general(
        product[...], flipped[...], (((1,), (1,)), ((), ())), preferred_element_type=jnp.float32
    )
    side = parts * group
    row = lax.broadcasted_iota(jnp.int32, (side, side), 0)
    lane = lax.broadcasted_iota(jnp.int32, (side, side), 1)
    total = jnp.where(lax.rem(row, group) == lax.rem(lane, group), total, 0.0)
    total = jnp.sum(total.reshape(parts, group, side), 1)
    source = lax.broadcasted_iota(jnp.int32, (side, LANES), 0)
    lane = lax.broadcasted_iota(jnp.int32, (side, LANES), 1)
    spread = (source // group == lax.rem(lane, parts)).astype(jnp.float32)
    total = jnp.dot(total, spread, precision=lax.Precision.HIGHEST, preferred_element_type=jnp.float32)
    row = lax.broadcasted_iota(jnp.int32, (parts, LANES), 0)
    lane = lax.broadcasted_iota(jnp.int32, (parts, LANES), 1)
    total = jnp.where(lane // parts == row, total, 0.0)
    total = jnp.dot(total, weights[...], precision=lax.Precision.HIGHEST, preferred_element_type=jnp.float32)
    total = jnp.sum(total, 0, keepdims=True) * columns[:1] + columns[1:]
    out[...] = jnp.broadcast_to(total[:, None, :], out.shape)


def chain_weights(chain_factors, chain_target, fields):
    pairs = fields * fields
    parts = 2 * pairs
    codes = (
        (chain_factors[:, 0] * fields + chain_factors[:, 1]) * pairs
        + chain_factors[:, 2] * fields
        + chain_factors[:, 3]
    )
    row = jnp.arange(LANES, dtype=jnp.int32)
    first, second = row // parts, row % parts
    used = row < parts * parts
    ahead = jnp.where(used, (first // 2) * pairs + second // 2, -1)
    behind = jnp.where(used, (second // 2) * pairs + first // 2, -1)
    column = jnp.arange(LANES, dtype=jnp.int32)
    on_row = (ahead[:, None] == codes[None, :]).astype(jnp.float32)
    on_row = 0.5 * (on_row + (behind[:, None] == codes[None, :]).astype(jnp.float32))
    on_column = (chain_target[:, None] == (column % NCORR)[None, :]).astype(jnp.float32)
    counts = jnp.dot(on_row, on_column, precision=lax.Precision.HIGHEST)
    mixed = (first % 2 != second % 2)[:, None]
    both_imag = (first % 2 + second % 2 == 2)[:, None]
    real_sign = jnp.where(mixed, 0.0, jnp.where(both_imag, -1.0, 1.0))
    imag_sign = jnp.where(mixed, 1.0, 0.0)
    sign = jnp.where((column < WIN * NCORR)[None, :], real_sign, imag_sign)
    return counts * sign


def source_times(times, ops):
    time, chip, source = (lax.broadcasted_iota(jnp.int32, (times, ops, times), axis) for axis in range(3))
    pair = (time // 2 + times // 2 - source_lag(ops, chip)) % (times // 2)
    return (source == pair * 2 + chip % 2).astype(jnp.float32)


def per_device(times, ops, sink_fields, source_fields, source_live, chain_factors, chain_target):
    fields, _, rows, full = sink_fields.shape[1:]
    half = ops // 2
    share = full // half
    parts = 2 * fields * fields
    group = 2 * LANES // parts
    chip = lax.axis_index("op")
    separation = jnp.where(chip // half == lax.rem(chip, 2), 2, 1)
    lane = jnp.arange(LANES, dtype=jnp.int32)
    used = 2 * WIN * NCORR
    wanted = (lane < used) & (lane // NCORR % WIN + 1 == separation)
    scale = jnp.where(wanted, 1.0 / math.sqrt(times), 0.0)
    flag = jnp.where(lane == used, source_live[0].astype(jnp.float32), 0.0)
    columns = jnp.stack([scale, flag]).astype(jnp.float32)
    weights = chain_weights(chain_factors, chain_target, fields)

    any_spec = pl.BlockSpec(memory_space=pl.ANY)
    vmem_spec = pl.BlockSpec(memory_space=pltpu.VMEM)
    jobs = jobs_of(half, share, 0)
    lanes = sum(count // group * cols for _, count, _, cols, _ in jobs)
    most = max(count for _, count, _, _, weight in jobs if weight)
    tables = weights, columns, source_times(times, ops)
    blocks, (weights, columns, picks) = send_blocks(times, ops, sink_fields[0], source_fields[0], tables)
    partial_sums = pl.pallas_call(
        functools.partial(trace_kernel, ops, group),
        out_shape=jax.ShapeDtypeStruct((times * ops, 1, LANES), jnp.float32),
        in_specs=[any_spec] * len(blocks) + [vmem_spec] * 2,
        out_specs=vmem_spec,
        scratch_shapes=[
            pltpu.VMEM((fields, full, 2 * full), jnp.bfloat16),
            pltpu.VMEM((fields, 2 * full, 2 * full), jnp.bfloat16),
            pltpu.VMEM((fields, 2, most, 2 * full), jnp.bfloat16),
            pltpu.VMEM((parts * group, lanes), jnp.bfloat16),
            pltpu.VMEM((parts * group, lanes), jnp.bfloat16),
            pltpu.SemaphoreType.DMA((5 * ops,)),
        ],
        compiler_params=pltpu.CompilerParams(vmem_limit_bytes=24 * 1024 * 1024),
        cost_estimate=pl.CostEstimate(
            flops=4 * 2 * fields * fields * share * full * full, bytes_accessed=10 * ops * rows * full, transcendentals=0
        ),
    )(*blocks, weights, columns)
    shares = lax.all_to_all(partial_sums, AXES, 0, 0, tiled=True).reshape(times, ops, LANES)
    live = shares[:, 0, used]
    weight = jnp.sum(picks * live, -1)
    totals = jnp.sum(shares * weight[:, :, None], (0, 1))[:used]
    return totals.reshape(2, WIN, NCORR).transpose(0, 2, 1)


def solution(mesh):
    in_specs = (P("tm", None, None, "op", None), P("tm", None, None, "op", None), P("tm"), P(), P())
    body = functools.partial(per_device, mesh.shape["tm"], mesh.shape["op"])
    return jax.shard_map(body, mesh=mesh, in_specs=in_specs, out_specs=P(), check_vma=False)
```

```python
import functools
import math

import jax
import jax.numpy as jnp
from jax import lax
from jax.experimental import pallas as pl
from jax.experimental.pallas import tpu as pltpu
from jax.sharding import PartitionSpec as P

WIN = 2
NCORR = 16
AXES = ("tm", "op")
LANES = 128


def routes(times, ops, place):
    pairs = []
    for pair in range(times // 2):
        for core in range(2):
            for op in range(ops):
                target = place(pair, core, op)
                if target is not None:
                    to_pair, to_core, to_op = target
                    to_time = (to_pair % (times // 2)) * 2 + to_core
                    pairs.append(((pair * 2 + core) * ops + op, to_time * ops + to_op))
    return pairs


def sink_slot(ops, chip, core, step):
    half = ops // 2
    return core * half + ((chip % half) ^ (chip // half) ^ core ^ step)


def sink_target(ops, core, op, step):
    half = ops // 2
    side = op // half
    return side, core * half + ((op % half) ^ side ^ core ^ step)


def source_slot(ops, chip, core, step):
    low = core ^ (chip // (ops // 2)) ^ (chip & 1) ^ 1
    return (((chip >> 1) ^ 1 ^ (chip & 1) ^ low ^ step) << 1) + low


def source_lag(ops, chip):
    return 1 - (1 - chip % 2) * (chip // (ops // 2))


def source_target(ops, core, op, step):
    target = (((op >> 1) ^ 1 ^ (op & 1) ^ core ^ step) << 1) | core
    return (op & 1) ^ core ^ 1 ^ (target // (ops // 2)), target


def sink_holder(ops, core, chip):
    return core == chip // (ops // 2)


def send_blocks(times, ops, sink, source, tables):
    def along(block, place):
        return lax.ppermute(block, AXES, routes(times, ops, place))

    def plain_sink(step, only):
        def place(pair, core, op):
            to_core, to_op = sink_target(ops, core, op, step)
            return None if only and not sink_holder(ops, to_core, to_op) else (pair, to_core, to_op)

        return place

    def plain_source(step, only):
        def place(pair, core, op):
            to_core, to_op = source_target(ops, core, op, step)
            to_pair = pair + source_lag(ops, to_op)
            return None if only and sink_holder(ops, to_core, to_op) else (to_pair, to_core, to_op)

        return place

    def pass_on(pair, core, op):
        if not sink_holder(ops, core, op):
            return pair, core, op ^ 1
        to_op = op ^ 2
        return pair - source_lag(ops, op) + source_lag(ops, to_op), to_op // (ops // 2), to_op

    def across(block):
        return along(block, lambda pair, core, op: (pair, 1 - core, op))

    holder = sink_holder(ops, lax.rem(lax.axis_index("tm"), 2), lax.axis_index("op"))
    blocks, last = [], []
    for pair in range(ops // 4):
        sink_first = along(sink, plain_sink(2 * pair + 1, False))
        source_first = along(source, plain_source(2 * pair, False))
        passed = along(jnp.where(holder, source_first, sink_first), pass_on)
        late_source, tables = lax.optimization_barrier((source, tables))
        source_own = along(late_source, plain_source(2 * pair + 1, True))
        sink_own = sink if pair == 0 else along(sink, plain_sink(2 * pair, True))
        own = jnp.where(holder, sink_own, source_own)
        three = [sink_first, source_first, own]
        blocks += three + [across(block) for block in three] + [passed]
        last.append(across(passed))
    return blocks, last, tables


class Fetches:
    def __init__(self, sems, used=0):
        self.sems, self.used, self.copies = sems, used, []

    def start(self, dst, *choices):
        sem = self.sems.at[self.used + len(self.copies)]
        taken = None
        for index, (condition, src) in enumerate(choices):
            copy = pltpu.make_async_copy(src, dst, sem)
            if index == len(choices) - 1:
                condition = taken
            elif taken is not None:
                condition, taken = jnp.logical_and(taken, condition), jnp.logical_and(taken, jnp.logical_not(condition))
            else:
                taken = jnp.logical_not(condition)
            if condition is None:
                copy.start()
            else:
                pl.when(condition)(copy.start)
        self.copies.append(copy)

    def wait(self):
        for copy in self.copies:
            copy.wait()


def aligned(start, size, unit):
    return pl.ds(pl.multiple_of(start, unit), size)


def fetch_source(right, place, fetches, *choices):
    rows, full = choices[0][1].shape[2:]
    inner = right.shape[1] // 2
    at, low = aligned(place, rows, rows), aligned(inner + place, rows, rows)
    for part, dst in ((0, right.at[:, at, :full]), (1, right.at[:, at, full:]), (0, right.at[:, low, full:])):
        fetches.start(dst, *[(condition, block.at[:, part]) for condition, block in choices])


def fetch_sink(left, place, fetches, *choices):
    rows, full = choices[0][1].shape[2:]
    for part in range(2):
        dst = left.at[:, aligned(place, rows, rows), pl.ds(part * full, full)]
        fetches.start(dst, *[(condition, block.at[:, part]) for condition, block in choices])


def jobs_of(half, share, member):
    jobs = [(member * share, share, member * share, share, 0)]
    for apart in range(1, half // 2 + 1):
        if 2 * apart < half:
            jobs.append((member * share, share, lax.rem(member + apart, half) * share, share, 2.0))
        elif share // 2 % LANES:
            jobs.append((member * share, share, lax.rem(member + apart, half) * share, share, 1.0))
        else:
            low = lax.rem(member, half // 2)
            start = low * share + member // (half // 2) * (share // 2)
            jobs.append((start, share // 2, (low + half // 2) * share, share, 2.0))
    return jobs


def products(job, left, right, flip):
    row_start, count, col_start, cols, weight = job
    fields, full = left.shape[0], left.shape[1]
    inner = left.shape[2] // 2
    unit = math.gcd(count, LANES)
    lhs = jnp.concatenate([left[a, aligned(row_start, count, unit), :] for a in range(fields)], 0)
    ahead = []
    for b in range(fields):
        for part in range(2):
            rhs = right[b, :, aligned(part * full + col_start, cols, LANES)]
            ahead.append(jnp.dot(lhs, rhs, preferred_element_type=jnp.float32))
    if not weight:
        return ahead, None
    for b in range(fields):
        real_turned = right[b, :inner, aligned(row_start, count, unit)].T
        imag_turned = right[b, :inner, aligned(full + row_start, count, unit)].T
        flip[b, 0, :count, :inner] = real_turned
        flip[b, 0, :count, inner:] = -imag_turned
        flip[b, 1, :count, :inner] = imag_turned
        flip[b, 1, :count, inner:] = real_turned
    lhs = flip[:, :, :count, :].reshape(fields * 2 * count, 2 * inner)
    rhs = jnp.concatenate([left[a, aligned(col_start, cols, LANES), :] for a in range(fields)], 0)
    return ahead, lax.dot_general(lhs, rhs, (((1,), (1,)), ((), ())), preferred_element_type=jnp.float32)


def fill_signs(right):
    inner, full = right.shape[1] // 2, right.shape[2] // 2
    for b in range(right.shape[0]):
        right[b, inner:, :full] = -right[b, :inner, full:]


def place_in(half, share):
    core = lax.rem(lax.axis_index("tm"), 2)
    chip = lax.axis_index("op")
    return core, chip, jobs_of(half, share, lax.rem(chip, half) // 2 * 2 + core)


def lay_kernel(ops, *refs):
    half = ops // 2
    left, right, sems = refs[-3:]
    rows, full = refs[0].shape[2:]
    core, chip, _ = place_in(half, full // half)
    here = sink_holder(ops, core, chip)
    side = chip // half
    fetches = Fetches(sems)
    for pair in range(ops // 4):
        blocks = refs[7 * pair : 7 * pair + 7]
        for turn in range(2):
            at = core if turn == 0 else 1 - core
            sink_first, source_first, _ = blocks[3 * turn : 3 * turn + 3]
            fetch_sink(left, sink_slot(ops, chip, at, 2 * pair + 1) * rows, fetches, (None, sink_first))
            fetch_source(right, source_slot(ops, chip, at, 2 * pair) * rows, fetches, (None, source_first))
        own, own_across, passed = blocks[2], blocks[5], blocks[6]
        place = sink_slot(ops, chip, side, 2 * pair) * rows
        fetch_sink(left, place, fetches, (here, own), (None, own_across))
        place = source_slot(ops, chip, 1 - side, 2 * pair + 1) * rows
        fetch_source(right, place, fetches, (here, own_across), (None, own))


        @pl.when(here)
        def _():
            mine = Fetches(sems, len(fetches.copies))
            fetch_source(right, source_slot(ops, chip, side, 2 * pair + 1) * rows, mine, (None, passed))
            mine.wait()

        @pl.when(jnp.logical_not(here))
        def _():
            mine = Fetches(sems, len(fetches.copies))
            fetch_sink(left, sink_slot(ops, chip, 1 - side, 2 * pair) * rows, mine, (None, passed))
            mine.wait()
    fetches.wait()
    for b in range(right.shape[0]):
        right[b, full:, :full] = -right[b, :full, full:]


def trace_kernel(ops, group, *refs):
    half = ops // 2
    quarter = ops // 4
    blocks = refs[:quarter]
    left, right, weights, columns, out = refs[quarter : quarter + 5]
    flip, product, flipped, sems = refs[-4:]
    rows, full = blocks[0].shape[2:]
    core, chip, jobs = place_in(half, full // half)
    here = sink_holder(ops, core, chip)
    side = chip // half

    @pl.when(here)
    def _():
        fetches = Fetches(sems)
        for pair in range(quarter):
            fetch_sink(left, sink_slot(ops, chip, 1 - side, 2 * pair) * rows, fetches, (None, blocks[pair]))
        fetches.wait()

    @pl.when(jnp.logical_not(here))
    def _():
        fetches = Fetches(sems)
        for pair in range(quarter):
            fetch_source(right, source_slot(ops, chip, side, 2 * pair + 1) * rows, fetches, (None, blocks[pair]))
        fetches.wait()
        for pair in range(quarter):
            place = source_slot(ops, chip, side, 2 * pair + 1) * rows
            for b in range(right.shape[0]):
                right[b, aligned(full + place, rows, rows), :full] = -right[b, aligned(place, rows, rows), full:]

    trace_rows(group, jobs, left, right, flip, weights, columns, out, product, flipped)


def trace_rows(group, jobs, left, right, flip, weights, columns, out, product, flipped):
    fields = left.shape[0]
    parts = 2 * fields * fields

    def put(into, lane, at, block):
        cols = block.shape[1]
        for g in range(block.shape[0] // group):
            into[at * group : (at + 1) * group, lane + g * cols : lane + (g + 1) * cols] = block[g * group : (g + 1) * group]

    lane = 0
    for job in jobs:
        _, count, _, cols, weight = job
        ahead, behind = products(job, left, right, flip)
        for index, value in enumerate(ahead):
            value = value.astype(jnp.bfloat16)
            for a in range(fields):
                block = value[a * count : (a + 1) * count]
                place = a * fields * 2 + index
                put(product, lane, place, block)
                if behind is None:
                    put(flipped, lane, place, block.T)
        if behind is not None:
            value = (weight * behind).astype(jnp.bfloat16)
            for index in range(fields * 2):
                for a in range(fields):
                    block = value[index * count : (index + 1) * count, a * cols : (a + 1) * cols]
                    put(flipped, lane, a * fields * 2 + index, block)
        lane += count // group * cols
    total = lax.dot_general(
        product[...], flipped[...], (((1,), (1,)), ((), ())), preferred_element_type=jnp.float32
    )
    side = parts * group
    row = lax.broadcasted_iota(jnp.int32, (side, side), 0)
    lane = lax.broadcasted_iota(jnp.int32, (side, side), 1)
    total = jnp.where(lax.rem(row, group) == lax.rem(lane, group), total, 0.0)
    total = jnp.sum(total.reshape(parts, group, side), 1)
    source = lax.broadcasted_iota(jnp.int32, (side, LANES), 0)
    lane = lax.broadcasted_iota(jnp.int32, (side, LANES), 1)
    spread = (source // group == lax.rem(lane, parts)).astype(jnp.float32)
    total = jnp.dot(total, spread, precision=lax.Precision.HIGHEST, preferred_element_type=jnp.float32)
    row = lax.broadcasted_iota(jnp.int32, (parts, LANES), 0)
    lane = lax.broadcasted_iota(jnp.int32, (parts, LANES), 1)
    total = jnp.where(lane // parts == row, total, 0.0)
    total = jnp.dot(total, weights[...], precision=lax.Precision.HIGHEST, preferred_element_type=jnp.float32)
    total = jnp.sum(total, 0, keepdims=True) * columns[:1] + columns[1:]
    out[...] = jnp.broadcast_to(total[:, None, :], out.shape)


def chain_weights(chain_factors, chain_target, fields):
    pairs = fields * fields
    parts = 2 * pairs
    codes = (
        (chain_factors[:, 0] * fields + chain_factors[:, 1]) * pairs
        + chain_factors[:, 2] * fields
        + chain_factors[:, 3]
    )
    row = jnp.arange(LANES, dtype=jnp.int32)
    first, second = row // parts, row % parts
    used = row < parts * parts
    ahead = jnp.where(used, (first // 2) * pairs + second // 2, -1)
    behind = jnp.where(used, (second // 2) * pairs + first // 2, -1)
    column = jnp.arange(LANES, dtype=jnp.int32)
    on_row = (ahead[:, None] == codes[None, :]).astype(jnp.float32)
    on_row = 0.5 * (on_row + (behind[:, None] == codes[None, :]).astype(jnp.float32))
    on_column = (chain_target[:, None] == (column % NCORR)[None, :]).astype(jnp.float32)
    counts = jnp.dot(on_row, on_column, precision=lax.Precision.HIGHEST)
    mixed = (first % 2 != second % 2)[:, None]
    both_imag = (first % 2 + second % 2 == 2)[:, None]
    real_sign = jnp.where(mixed, 0.0, jnp.where(both_imag, -1.0, 1.0))
    imag_sign = jnp.where(mixed, 1.0, 0.0)
    sign = jnp.where((column < WIN * NCORR)[None, :], real_sign, imag_sign)
    return counts * sign


def source_times(times, ops):
    time, chip, source = (lax.broadcasted_iota(jnp.int32, (times, ops, times), axis) for axis in range(3))
    pair = (time // 2 + times // 2 - source_lag(ops, chip)) % (times // 2)
    return (source == pair * 2 + chip % 2).astype(jnp.float32)


def per_device(times, ops, sink_fields, source_fields, source_live, chain_factors, chain_target):
    fields, _, rows, full = sink_fields.shape[1:]
    half = ops // 2
    share = full // half
    parts = 2 * fields * fields
    group = 2 * LANES // parts
    chip = lax.axis_index("op")
    separation = jnp.where(chip // half == lax.rem(chip, 2), 2, 1)
    lane = jnp.arange(LANES, dtype=jnp.int32)
    used = 2 * WIN * NCORR
    wanted = (lane < used) & (lane // NCORR % WIN + 1 == separation)
    scale = jnp.where(wanted, 1.0 / math.sqrt(times), 0.0)
    flag = jnp.where(lane == used, source_live[0].astype(jnp.float32), 0.0)
    columns = jnp.stack([scale, flag]).astype(jnp.float32)
    weights = chain_weights(chain_factors, chain_target, fields)

    any_spec = pl.BlockSpec(memory_space=pl.ANY)
    vmem_spec = pl.BlockSpec(memory_space=pltpu.VMEM)
    jobs = jobs_of(half, share, 0)
    lanes = sum(count // group * cols for _, count, _, cols, _ in jobs)
    most = max(count for _, count, _, _, weight in jobs if weight)
    tables = weights, columns, source_times(times, ops)
    blocks, last, (weights, columns, picks) = send_blocks(times, ops, sink_fields[0], source_fields[0], tables)
    operands = [
        jax.ShapeDtypeStruct((fields, full, 2 * full), jnp.bfloat16),
        jax.ShapeDtypeStruct((fields, 2 * full, 2 * full), jnp.bfloat16),
    ]
    params = pltpu.CompilerParams(vmem_limit_bytes=24 * 1024 * 1024)
    left, right = pl.pallas_call(
        functools.partial(lay_kernel, ops),
        out_shape=operands,
        in_specs=[any_spec] * len(blocks),
        out_specs=[vmem_spec] * 2,
        scratch_shapes=[pltpu.SemaphoreType.DMA((5 * ops,))],
        compiler_params=params,
        cost_estimate=pl.CostEstimate(flops=0, bytes_accessed=10 * ops * rows * full, transcendentals=0),
    )(*blocks)
    count = len(last)
    partial_sums, *_ = pl.pallas_call(
        functools.partial(trace_kernel, ops, group),
        out_shape=[jax.ShapeDtypeStruct((times * ops, 1, LANES), jnp.float32)] + operands,
        in_specs=[any_spec] * count + [vmem_spec] * 4,
        out_specs=[vmem_spec] * 3,
        scratch_shapes=[
            pltpu.VMEM((fields, 2, most, 2 * full), jnp.bfloat16),
            pltpu.VMEM((parts * group, lanes), jnp.bfloat16),
            pltpu.VMEM((parts * group, lanes), jnp.bfloat16),
            pltpu.SemaphoreType.DMA((3 * ops // 4,)),
        ],
        input_output_aliases={count: 1, count + 1: 2},
        compiler_params=params,
        cost_estimate=pl.CostEstimate(
            flops=4 * 2 * fields * fields * share * full * full, bytes_accessed=10 * ops * rows * full, transcendentals=0
        ),
    )(*last, left, right, weights, columns)
    shares = lax.all_to_all(partial_sums, AXES, 0, 0, tiled=True).reshape(times, ops, LANES)
    live = shares[:, 0, used]
    weight = jnp.sum(picks * live, -1)
    totals = jnp.sum(shares * weight[:, :, None], (0, 1))[:used]
    return totals.reshape(2, WIN, NCORR).transpose(0, 2, 1)


def solution(mesh):
    in_specs = (P("tm", None, None, "op", None), P("tm", None, None, "op", None), P("tm"), P(), P())
    body = functools.partial(per_device, mesh.shape["tm"], mesh.shape["op"])
    return jax.shard_map(body, mesh=mesh, in_specs=in_specs, out_specs=P(), check_vma=False)
```

```python
import functools
import math

import jax
import jax.numpy as jnp
from jax import lax
from jax.experimental import pallas as pl
from jax.experimental.pallas import tpu as pltpu
from jax.sharding import PartitionSpec as P

WIN = 2
NCORR = 16
AXES = ("tm", "op")
LANES = 128


def routes(times, ops, place):
    pairs = []
    for pair in range(times // 2):
        for core in range(2):
            for op in range(ops):
                target = place(pair, core, op)
                if target is not None:
                    to_pair, to_core, to_op = target
                    to_time = (to_pair % (times // 2)) * 2 + to_core
                    pairs.append(((pair * 2 + core) * ops + op, to_time * ops + to_op))
    return pairs


def sink_slot(ops, chip, core, step):
    half = ops // 2
    return core * half + ((chip % half) ^ (chip // half) ^ core ^ step)


def sink_target(ops, core, op, step):
    half = ops // 2
    side = op // half
    return side, core * half + ((op % half) ^ side ^ core ^ step)


def source_slot(ops, chip, core, step):
    low = core ^ (chip // (ops // 2)) ^ (chip & 1) ^ 1
    return (((chip >> 1) ^ 1 ^ (chip & 1) ^ low ^ step) << 1) + low


def source_lag(ops, chip):
    return 1 - (1 - chip % 2) * (chip // (ops // 2))


def source_target(ops, core, op, step):
    target = (((op >> 1) ^ 1 ^ (op & 1) ^ core ^ step) << 1) | core
    return (op & 1) ^ core ^ 1 ^ (target // (ops // 2)), target


def sink_holder(ops, core, chip):
    return core == chip // (ops // 2)


def send_blocks(times, ops, sink, source, tables):
    def along(block, place):
        return lax.ppermute(block, AXES, routes(times, ops, place))

    def plain_sink(step, only):
        def place(pair, core, op):
            to_core, to_op = sink_target(ops, core, op, step)
            return None if only and not sink_holder(ops, to_core, to_op) else (pair, to_core, to_op)

        return place

    def plain_source(step, only):
        def place(pair, core, op):
            to_core, to_op = source_target(ops, core, op, step)
            to_pair = pair + source_lag(ops, to_op)
            return None if only and sink_holder(ops, to_core, to_op) else (to_pair, to_core, to_op)

        return place

    def pass_on(pair, core, op):
        if not sink_holder(ops, core, op):
            return pair, core, op ^ 1
        to_op = op ^ 2
        return pair - source_lag(ops, op) + source_lag(ops, to_op), to_op // (ops // 2), to_op

    def across(block):
        return along(block, lambda pair, core, op: (pair, 1 - core, op))

    holder = sink_holder(ops, lax.rem(lax.axis_index("tm"), 2), lax.axis_index("op"))
    blocks, last = [], []
    for pair in range(ops // 4):
        sink_first = along(sink, plain_sink(2 * pair + 1, False))
        source_first = along(source, plain_source(2 * pair, False))
        passed = along(jnp.where(holder, source_first, sink_first), pass_on)
        late_source, tables = lax.optimization_barrier((source, tables))
        source_own = along(late_source, plain_source(2 * pair + 1, True))
        sink_own = sink if pair == 0 else along(sink, plain_sink(2 * pair, True))
        own = jnp.where(holder, sink_own, source_own)
        three = [sink_first, source_first, own]
        blocks += three + [across(block) for block in three] + [passed]
        last.append(across(passed))
    return blocks, last, tables


class Fetches:
    def __init__(self, sems, used=0):
        self.sems, self.used, self.copies = sems, used, []

    def start(self, dst, *choices):
        sem = self.sems.at[self.used + len(self.copies)]
        taken = None
        for index, (condition, src) in enumerate(choices):
            copy = pltpu.make_async_copy(src, dst, sem)
            if index == len(choices) - 1:
                condition = taken
            elif taken is not None:
                condition, taken = jnp.logical_and(taken, condition), jnp.logical_and(taken, jnp.logical_not(condition))
            else:
                taken = jnp.logical_not(condition)
            if condition is None:
                copy.start()
            else:
                pl.when(condition)(copy.start)
        self.copies.append(copy)

    def wait(self):
        for copy in self.copies:
            copy.wait()


def aligned(start, size, unit):
    return pl.ds(pl.multiple_of(start, unit), size)


def fetch_source(right, place, fetches, *choices):
    rows, full = choices[0][1].shape[2:]
    inner = right.shape[1] // 2
    at, low = aligned(place, rows, rows), aligned(inner + place, rows, rows)
    for part, dst in ((0, right.at[:, at, :full]), (1, right.at[:, at, full:]), (0, right.at[:, low, full:])):
        fetches.start(dst, *[(condition, block.at[:, part]) for condition, block in choices])


def fetch_sink(left, place, fetches, *choices):
    rows, full = choices[0][1].shape[2:]
    for part in range(2):
        dst = left.at[:, aligned(place, rows, rows), pl.ds(part * full, full)]
        fetches.start(dst, *[(condition, block.at[:, part]) for condition, block in choices])


def jobs_of(half, share, member):
    jobs = [(member * share, share, member * share, share, 0)]
    for apart in range(1, half // 2 + 1):
        if 2 * apart < half:
            jobs.append((member * share, share, lax.rem(member + apart, half) * share, share, 2.0))
        elif share // 2 % LANES:
            jobs.append((member * share, share, lax.rem(member + apart, half) * share, share, 1.0))
        else:
            low = lax.rem(member, half // 2)
            start = low * share + member // (half // 2) * (share // 2)
            jobs.append((start, share // 2, (low + half // 2) * share, share, 2.0))
    return jobs


def stacked(left, start, count, lanes=slice(None)):
    rows = aligned(start, count, math.gcd(count, LANES))
    return jnp.concatenate([left[a, rows, lanes] for a in range(left.shape[0])], 0)


def products_ahead(job, left, right, index):
    row_start, count, col_start, cols, _ = job
    full = left.shape[1]
    rhs = right[index // 2, :, aligned(index % 2 * full + col_start, cols, LANES)]
    return jnp.dot(stacked(left, row_start, count), rhs, preferred_element_type=jnp.float32)


def products_behind(job, left, right, flip):
    row_start, count, col_start, cols, _ = job
    fields, full = left.shape[0], left.shape[1]
    unit = math.gcd(count, LANES)
    for b in range(fields):
        real_turned = right[b, :full, aligned(row_start, count, unit)].T
        imag_turned = right[b, :full, aligned(full + row_start, count, unit)].T
        flip[b, 0, :count, :full] = real_turned
        flip[b, 0, :count, full:] = -imag_turned
        flip[b, 1, :count, :full] = imag_turned
        flip[b, 1, :count, full:] = real_turned
    lhs = flip[:, :, :count, :].reshape(fields * 2 * count, 2 * full)
    rhs = stacked(left, col_start, cols)
    return lax.dot_general(lhs, rhs, (((1,), (1,)), ((), ())), preferred_element_type=jnp.float32)


def place_in(half, share):
    core = lax.rem(lax.axis_index("tm"), 2)
    chip = lax.axis_index("op")
    return core, chip, jobs_of(half, share, lax.rem(chip, half) // 2 * 2 + core)


def lay_kernel(ops, *refs):
    half = ops // 2
    many = 7 * (ops // 4)
    left, right, *partials, sems = refs[many:]
    rows, full = refs[0].shape[2:]
    core, chip, jobs = place_in(half, full // half)
    here = sink_holder(ops, core, chip)
    side = chip // half
    fetches = Fetches(sems)
    for pair in range(ops // 4):
        blocks = refs[7 * pair : 7 * pair + 7]
        for turn in range(2):
            at = core if turn == 0 else 1 - core
            sink_first, source_first, _ = blocks[3 * turn : 3 * turn + 3]
            fetch_sink(left, sink_slot(ops, chip, at, 2 * pair + 1) * rows, fetches, (None, sink_first))
            fetch_source(right, source_slot(ops, chip, at, 2 * pair) * rows, fetches, (None, source_first))
        own, own_across, passed = blocks[2], blocks[5], blocks[6]
        place = sink_slot(ops, chip, side, 2 * pair) * rows
        fetch_sink(left, place, fetches, (here, own), (None, own_across))
        place = source_slot(ops, chip, 1 - side, 2 * pair + 1) * rows
        fetch_source(right, place, fetches, (here, own_across), (None, own))


        @pl.when(here)
        def _():
            mine = Fetches(sems, len(fetches.copies))
            fetch_source(right, source_slot(ops, chip, side, 2 * pair + 1) * rows, mine, (None, passed))
            mine.wait()

        @pl.when(jnp.logical_not(here))
        def _():
            mine = Fetches(sems, len(fetches.copies))
            fetch_sink(left, sink_slot(ops, chip, 1 - side, 2 * pair) * rows, mine, (None, passed))
            mine.wait()
    fetches.wait()
    for b in range(right.shape[0]):
        right[b, full:, :full] = -right[b, :full, full:]
    if partials:

        @pl.when(jnp.logical_not(here))
        def _():
            place = source_slot(ops, chip, side, 1) * rows
            for start in (place, full + place):
                right[:, aligned(start, rows, rows), :] = jnp.zeros((right.shape[0], rows, 2 * full), right.dtype)

        for index in range(partials[0].shape[0]):
            partials[0][index] = products_ahead(jobs[0], left, right, index)


def trace_kernel(ops, group, early, *refs):
    half = ops // 2
    quarter = ops // 4
    blocks = refs[:quarter]
    left, right, *partials, weights, columns, out = refs[quarter : quarter + 2 + early + 3]
    flip, product, flipped, sems = refs[-4:]
    rows, full = blocks[0].shape[2:]
    core, chip, jobs = place_in(half, full // half)
    here = sink_holder(ops, core, chip)
    side = chip // half

    @pl.when(here)
    def _():
        fetches = Fetches(sems)
        for pair in range(quarter):
            fetch_sink(left, sink_slot(ops, chip, 1 - side, 2 * pair) * rows, fetches, (None, blocks[pair]))
        fetches.wait()

    @pl.when(jnp.logical_not(here))
    def _():
        fetches = Fetches(sems)
        for pair in range(quarter):
            fetch_source(right, source_slot(ops, chip, side, 2 * pair + 1) * rows, fetches, (None, blocks[pair]))
        fetches.wait()
        for pair in range(quarter):
            place = source_slot(ops, chip, side, 2 * pair + 1) * rows
            for b in range(right.shape[0]):
                right[b, aligned(full + place, rows, rows), :full] = -right[b, aligned(place, rows, rows), full:]
        if partials:
            row_start, count, col_start, cols, _ = jobs[0]
            place = source_slot(ops, chip, side, 1) * rows
            lhs = [stacked(left, row_start, count, aligned(start, rows, LANES)) for start in (place, full + place)]
            lhs = jnp.concatenate(lhs, 1)
            for index in range(partials[0].shape[0]):
                at = aligned(index % 2 * full + col_start, cols, LANES)
                rhs = [right[index // 2, aligned(start, rows, rows), at] for start in (place, full + place)]
                more = jnp.dot(lhs, jnp.concatenate(rhs, 0), preferred_element_type=jnp.float32)
                partials[0][index] = partials[0][index] + more

    trace_rows(group, jobs, left, right, partials, flip, weights, columns, out, product, flipped)


def trace_rows(group, jobs, left, right, partials, flip, weights, columns, out, product, flipped):
    fields = left.shape[0]
    parts = 2 * fields * fields

    def put(into, lane, at, block):
        cols = block.shape[1]
        for g in range(block.shape[0] // group):
            into[at * group : (at + 1) * group, lane + g * cols : lane + (g + 1) * cols] = block[g * group : (g + 1) * group]

    lane = 0
    for number, job in enumerate(jobs):
        _, count, _, cols, weight = job
        for index in range(fields * 2):
            if number == 0 and partials:
                value = partials[0][index]
            else:
                value = products_ahead(job, left, right, index)
            value = value.astype(jnp.bfloat16)
            for a in range(fields):
                block = value[a * count : (a + 1) * count]
                place = a * fields * 2 + index
                put(product, lane, place, block)
                if not weight:
                    put(flipped, lane, place, block.T)
        if weight:
            value = (weight * products_behind(job, left, right, flip)).astype(jnp.bfloat16)
            for index in range(fields * 2):
                for a in range(fields):
                    block = value[index * count : (index + 1) * count, a * cols : (a + 1) * cols]
                    put(flipped, lane, a * fields * 2 + index, block)
        lane += count // group * cols
    total = lax.dot_general(
        product[...], flipped[...], (((1,), (1,)), ((), ())), preferred_element_type=jnp.float32
    )
    side = parts * group
    row = lax.broadcasted_iota(jnp.int32, (side, side), 0)
    lane = lax.broadcasted_iota(jnp.int32, (side, side), 1)
    total = jnp.where(lax.rem(row, group) == lax.rem(lane, group), total, 0.0)
    total = jnp.sum(total.reshape(parts, group, side), 1)
    source = lax.broadcasted_iota(jnp.int32, (side, LANES), 0)
    lane = lax.broadcasted_iota(jnp.int32, (side, LANES), 1)
    spread = (source // group == lax.rem(lane, parts)).astype(jnp.float32)
    total = jnp.dot(total, spread, precision=lax.Precision.HIGHEST, preferred_element_type=jnp.float32)
    row = lax.broadcasted_iota(jnp.int32, (parts, LANES), 0)
    lane = lax.broadcasted_iota(jnp.int32, (parts, LANES), 1)
    total = jnp.where(lane // parts == row, total, 0.0)
    total = jnp.dot(total, weights[...], precision=lax.Precision.HIGHEST, preferred_element_type=jnp.float32)
    total = jnp.sum(total, 0, keepdims=True) * columns[:1] + columns[1:]
    out[...] = jnp.broadcast_to(total[:, None, :], out.shape)


def chain_weights(chain_factors, chain_target, fields):
    pairs = fields * fields
    parts = 2 * pairs
    codes = (
        (chain_factors[:, 0] * fields + chain_factors[:, 1]) * pairs
        + chain_factors[:, 2] * fields
        + chain_factors[:, 3]
    )
    row = jnp.arange(LANES, dtype=jnp.int32)
    first, second = row // parts, row % parts
    used = row < parts * parts
    ahead = jnp.where(used, (first // 2) * pairs + second // 2, -1)
    behind = jnp.where(used, (second // 2) * pairs + first // 2, -1)
    column = jnp.arange(LANES, dtype=jnp.int32)
    on_row = (ahead[:, None] == codes[None, :]).astype(jnp.float32)
    on_row = 0.5 * (on_row + (behind[:, None] == codes[None, :]).astype(jnp.float32))
    on_column = (chain_target[:, None] == (column % NCORR)[None, :]).astype(jnp.float32)
    counts = jnp.dot(on_row, on_column, precision=lax.Precision.HIGHEST)
    mixed = (first % 2 != second % 2)[:, None]
    both_imag = (first % 2 + second % 2 == 2)[:, None]
    real_sign = jnp.where(mixed, 0.0, jnp.where(both_imag, -1.0, 1.0))
    imag_sign = jnp.where(mixed, 1.0, 0.0)
    sign = jnp.where((column < WIN * NCORR)[None, :], real_sign, imag_sign)
    return counts * sign


def source_times(times, ops):
    time, chip, source = (lax.broadcasted_iota(jnp.int32, (times, ops, times), axis) for axis in range(3))
    pair = (time // 2 + times // 2 - source_lag(ops, chip)) % (times // 2)
    return (source == pair * 2 + chip % 2).astype(jnp.float32)


def per_device(times, ops, sink_fields, source_fields, source_live, chain_factors, chain_target):
    fields, _, rows, full = sink_fields.shape[1:]
    half = ops // 2
    share = full // half
    parts = 2 * fields * fields
    group = 2 * LANES // parts
    chip = lax.axis_index("op")
    separation = jnp.where(chip // half == lax.rem(chip, 2), 2, 1)
    lane = jnp.arange(LANES, dtype=jnp.int32)
    used = 2 * WIN * NCORR
    wanted = (lane < used) & (lane // NCORR % WIN + 1 == separation)
    scale = jnp.where(wanted, 1.0 / math.sqrt(times), 0.0)
    flag = jnp.where(lane == used, source_live[0].astype(jnp.float32), 0.0)
    columns = jnp.stack([scale, flag]).astype(jnp.float32)
    weights = chain_weights(chain_factors, chain_target, fields)

    any_spec = pl.BlockSpec(memory_space=pl.ANY)
    vmem_spec = pl.BlockSpec(memory_space=pltpu.VMEM)
    jobs = jobs_of(half, share, 0)
    lanes = sum(count // group * cols for _, count, _, cols, _ in jobs)
    most = max(count for _, count, _, _, weight in jobs if weight)
    tables = weights, columns, source_times(times, ops)
    blocks, last, (weights, columns, picks) = send_blocks(times, ops, sink_fields[0], source_fields[0], tables)
    operands = [
        jax.ShapeDtypeStruct((fields, full, 2 * full), jnp.bfloat16),
        jax.ShapeDtypeStruct((fields, 2 * full, 2 * full), jnp.bfloat16),
    ]
    early = int(ops == 4 and rows % LANES == 0)
    if early:
        operands.append(jax.ShapeDtypeStruct((fields * 2, fields * share, share), jnp.float32))
    params = pltpu.CompilerParams(vmem_limit_bytes=24 * 1024 * 1024)
    laid = pl.pallas_call(
        functools.partial(lay_kernel, ops),
        out_shape=operands,
        in_specs=[any_spec] * len(blocks),
        out_specs=[vmem_spec] * len(operands),
        scratch_shapes=[pltpu.SemaphoreType.DMA((5 * ops,))],
        compiler_params=params,
        cost_estimate=pl.CostEstimate(flops=0, bytes_accessed=10 * ops * rows * full, transcendentals=0),
    )(*blocks)
    count = len(last)
    partial_sums, *_ = pl.pallas_call(
        functools.partial(trace_kernel, ops, group, early),
        out_shape=[jax.ShapeDtypeStruct((times * ops, 1, LANES), jnp.float32)] + operands,
        in_specs=[any_spec] * count + [vmem_spec] * (len(operands) + 2),
        out_specs=[vmem_spec] * (len(operands) + 1),
        scratch_shapes=[
            pltpu.VMEM((fields, 2, most, 2 * full), jnp.bfloat16),
            pltpu.VMEM((parts * group, lanes), jnp.bfloat16),
            pltpu.VMEM((parts * group, lanes), jnp.bfloat16),
            pltpu.SemaphoreType.DMA((3 * ops // 4,)),
        ],
        input_output_aliases={count + index: 1 + index for index in range(len(operands))},
        compiler_params=params,
        cost_estimate=pl.CostEstimate(
            flops=4 * 2 * fields * fields * share * full * full, bytes_accessed=10 * ops * rows * full, transcendentals=0
        ),
    )(*last, *laid, weights, columns)
    shares = lax.all_to_all(partial_sums, AXES, 0, 0, tiled=True).reshape(times, ops, LANES)
    live = shares[:, 0, used]
    weight = jnp.sum(picks * live, -1)
    totals = jnp.sum(shares * weight[:, :, None], (0, 1))[:used]
    return totals.reshape(2, WIN, NCORR).transpose(0, 2, 1)


def solution(mesh):
    in_specs = (P("tm", None, None, "op", None), P("tm", None, None, "op", None), P("tm"), P(), P())
    body = functools.partial(per_device, mesh.shape["tm"], mesh.shape["op"])
    return jax.shard_map(body, mesh=mesh, in_specs=in_specs, out_specs=P(), check_vma=False)
```

```python
import functools
import math

import jax
import jax.numpy as jnp
from jax import lax
from jax.experimental import pallas as pl
from jax.experimental.pallas import tpu as pltpu
from jax.sharding import PartitionSpec as P

WIN = 2
NCORR = 16
AXES = ("tm", "op")
LANES = 128


def routes(times, ops, place):
    pairs = []
    for pair in range(times // 2):
        for core in range(2):
            for op in range(ops):
                target = place(pair, core, op)
                if target is not None:
                    to_pair, to_core, to_op = target
                    to_time = (to_pair % (times // 2)) * 2 + to_core
                    pairs.append(((pair * 2 + core) * ops + op, to_time * ops + to_op))
    return pairs


def sink_slot(ops, chip, core, step):
    half = ops // 2
    return core * half + ((chip % half) ^ (chip // half) ^ core ^ step)


def sink_target(ops, core, op, step):
    half = ops // 2
    side = op // half
    return side, core * half + ((op % half) ^ side ^ core ^ step)


def source_slot(ops, chip, core, step):
    low = core ^ (chip // (ops // 2)) ^ (chip & 1) ^ 1
    return (((chip >> 1) ^ 1 ^ (chip & 1) ^ low ^ step) << 1) + low


def source_lag(ops, chip):
    return 1 - (1 - chip % 2) * (chip // (ops // 2))


def source_target(ops, core, op, step):
    target = (((op >> 1) ^ 1 ^ (op & 1) ^ core ^ step) << 1) | core
    return (op & 1) ^ core ^ 1 ^ (target // (ops // 2)), target


def sink_holder(ops, core, chip):
    return core == chip // (ops // 2)


def send_blocks(times, ops, sink, source, tables, lay):
    def along(block, place):
        return lax.ppermute(block, AXES, routes(times, ops, place))

    def plain_sink(step, only):
        def place(pair, core, op):
            to_core, to_op = sink_target(ops, core, op, step)
            return None if only and not sink_holder(ops, to_core, to_op) else (pair, to_core, to_op)

        return place

    def plain_source(step, only):
        def place(pair, core, op):
            to_core, to_op = source_target(ops, core, op, step)
            to_pair = pair + source_lag(ops, to_op)
            return None if only and sink_holder(ops, to_core, to_op) else (to_pair, to_core, to_op)

        return place

    def pass_on(pair, core, op):
        if not sink_holder(ops, core, op):
            return pair, core, op ^ 1
        to_op = op ^ 2
        return pair - source_lag(ops, op) + source_lag(ops, to_op), to_op // (ops // 2), to_op

    def across(block):
        return along(block, lambda pair, core, op: (pair, 1 - core, op))

    holder = sink_holder(ops, lax.rem(lax.axis_index("tm"), 2), lax.axis_index("op"))
    here, firsts, held, last = [], [], [], []
    for pair in range(ops // 4):
        sink_first = along(sink, plain_sink(2 * pair + 1, False))
        source_first = along(source, plain_source(2 * pair, False))
        passed = along(jnp.where(holder, source_first, sink_first), pass_on)
        late_source, tables = lax.optimization_barrier((source, tables))
        source_own = along(late_source, plain_source(2 * pair + 1, True))
        sink_own = sink if pair == 0 else along(sink, plain_sink(2 * pair, True))
        here += [sink_first, source_first, sink_own, source_own]
        firsts.append(across(sink_first))
        firsts.append(across(source_first))
        held.append(passed)
        last.append(across(passed))
    *own, left, right = lay(here)
    return [across(block) for block in own] + held + firsts, last, (left, right), tables


class Fetches:
    def __init__(self, sems, used=0):
        self.sems, self.used, self.copies = sems, used, []

    def start(self, dst, *choices):
        sem = self.sems.at[self.used + len(self.copies)]
        taken = None
        for index, (condition, src) in enumerate(choices):
            copy = pltpu.make_async_copy(src, dst, sem)
            if index == len(choices) - 1:
                condition = taken
            elif taken is not None:
                condition, taken = jnp.logical_and(taken, condition), jnp.logical_and(taken, jnp.logical_not(condition))
            else:
                taken = jnp.logical_not(condition)
            if condition is None:
                copy.start()
            else:
                pl.when(condition)(copy.start)
        self.copies.append(copy)

    def wait(self):
        for copy in self.copies:
            copy.wait()


def aligned(start, size, unit):
    return pl.ds(pl.multiple_of(start, unit), size)


def fetch_source(right, place, fetches, *choices):
    rows, full = choices[0][1].shape[2:]
    inner = right.shape[1] // 2
    at, low = aligned(place, rows, rows), aligned(inner + place, rows, rows)
    for part, dst in ((0, right.at[:, at, :full]), (1, right.at[:, at, full:]), (0, right.at[:, low, full:])):
        fetches.start(dst, *[(condition, block.at[:, part]) for condition, block in choices])


def fetch_sink(left, place, fetches, *choices):
    rows, full = choices[0][1].shape[2:]
    for part in range(2):
        dst = left.at[:, aligned(place, rows, rows), pl.ds(part * full, full)]
        fetches.start(dst, *[(condition, block.at[:, part]) for condition, block in choices])


def jobs_of(half, share, member):
    jobs = [(member * share, share, member * share, share, 0)]
    for apart in range(1, half // 2 + 1):
        if 2 * apart < half:
            jobs.append((member * share, share, lax.rem(member + apart, half) * share, share, 2.0))
        elif share // 2 % LANES:
            jobs.append((member * share, share, lax.rem(member + apart, half) * share, share, 1.0))
        else:
            low = lax.rem(member, half // 2)
            start = low * share + member // (half // 2) * (share // 2)
            jobs.append((start, share // 2, (low + half // 2) * share, share, 2.0))
    return jobs


def stacked(left, start, count, lanes=slice(None)):
    rows = aligned(start, count, math.gcd(count, LANES))
    return jnp.concatenate([left[a, rows, lanes] for a in range(left.shape[0])], 0)


def products_ahead(job, left, right, index):
    row_start, count, col_start, cols, _ = job
    full = left.shape[1]
    rhs = right[index // 2, :, aligned(index % 2 * full + col_start, cols, LANES)]
    return jnp.dot(stacked(left, row_start, count), rhs, preferred_element_type=jnp.float32)


def products_behind(job, left, right, flip):
    row_start, count, col_start, cols, _ = job
    fields, full = left.shape[0], left.shape[1]
    unit = math.gcd(count, LANES)
    for b in range(fields):
        real_turned = right[b, :full, aligned(row_start, count, unit)].T
        imag_turned = right[b, :full, aligned(full + row_start, count, unit)].T
        flip[b, 0, :count, :full] = real_turned
        flip[b, 0, :count, full:] = -imag_turned
        flip[b, 1, :count, :full] = imag_turned
        flip[b, 1, :count, full:] = real_turned
    lhs = flip[:, :, :count, :].reshape(fields * 2 * count, 2 * full)
    rhs = stacked(left, col_start, cols)
    return lax.dot_general(lhs, rhs, (((1,), (1,)), ((), ())), preferred_element_type=jnp.float32)


def place_in(half, share):
    core = lax.rem(lax.axis_index("tm"), 2)
    chip = lax.axis_index("op")
    return core, chip, jobs_of(half, share, lax.rem(chip, half) // 2 * 2 + core)


def first_kernel(ops, *refs):
    quarter = ops // 4
    outs = refs[4 * quarter : 5 * quarter]
    left, right, sems = refs[5 * quarter :]
    rows, full = refs[0].shape[2:]
    core, chip, _ = place_in(ops // 2, full // (ops // 2))
    here = sink_holder(ops, core, chip)
    fetches = Fetches(sems)
    for pair in range(quarter):
        firsts, (sink_own, source_own) = refs[4 * pair : 4 * pair + 2], refs[4 * pair + 2 : 4 * pair + 4]
        fetches.start(outs[pair], (here, sink_own), (None, source_own))
        fetch_sink(left, sink_slot(ops, chip, core, 2 * pair + 1) * rows, fetches, (None, firsts[0]))
        fetch_source(right, source_slot(ops, chip, core, 2 * pair) * rows, fetches, (None, firsts[1]))
    fetches.wait()


def lay_kernel(ops, *refs):
    half = ops // 2
    quarter = ops // 4
    blocks = refs[: 5 * quarter]
    left, right = refs[5 * quarter : 5 * quarter + 2]
    partials, sems = refs[5 * quarter + 4 : -1], refs[-1]
    rows, full = blocks[0].shape[2:]
    core, chip, jobs = place_in(half, full // half)
    here = sink_holder(ops, core, chip)
    side = chip // half
    fetches = Fetches(sems)
    for pair in range(quarter):
        own, own_across, passed = blocks[pair], blocks[quarter + pair], blocks[2 * quarter + pair]
        sink_first, source_first = blocks[3 * quarter + 2 * pair : 3 * quarter + 2 * pair + 2]
        fetch_sink(left, sink_slot(ops, chip, 1 - core, 2 * pair + 1) * rows, fetches, (None, sink_first))
        fetch_source(right, source_slot(ops, chip, 1 - core, 2 * pair) * rows, fetches, (None, source_first))
        place = sink_slot(ops, chip, side, 2 * pair) * rows
        fetch_sink(left, place, fetches, (here, own), (None, own_across))
        place = source_slot(ops, chip, 1 - side, 2 * pair + 1) * rows
        fetch_source(right, place, fetches, (here, own_across), (None, own))

        @pl.when(here)
        def _():
            mine = Fetches(sems, len(fetches.copies))
            fetch_source(right, source_slot(ops, chip, side, 2 * pair + 1) * rows, mine, (None, passed))
            mine.wait()

        @pl.when(jnp.logical_not(here))
        def _():
            mine = Fetches(sems, len(fetches.copies))
            fetch_sink(left, sink_slot(ops, chip, 1 - side, 2 * pair) * rows, mine, (None, passed))
            mine.wait()
    fetches.wait()
    for b in range(right.shape[0]):
        right[b, full:, :full] = -right[b, :full, full:]
    if partials:

        @pl.when(jnp.logical_not(here))
        def _():
            place = source_slot(ops, chip, side, 1) * rows
            for start in (place, full + place):
                right[:, aligned(start, rows, rows), :] = jnp.zeros((right.shape[0], rows, 2 * full), right.dtype)

        for index in range(partials[0].shape[0]):
            partials[0][index] = products_ahead(jobs[0], left, right, index)


def trace_kernel(ops, group, early, *refs):
    half = ops // 2
    quarter = ops // 4
    blocks = refs[:quarter]
    left, right, *partials, weights, columns, out = refs[quarter : quarter + 2 + early + 3]
    flip, product, flipped, sems = refs[-4:]
    rows, full = blocks[0].shape[2:]
    core, chip, jobs = place_in(half, full // half)
    here = sink_holder(ops, core, chip)
    side = chip // half

    @pl.when(here)
    def _():
        fetches = Fetches(sems)
        for pair in range(quarter):
            fetch_sink(left, sink_slot(ops, chip, 1 - side, 2 * pair) * rows, fetches, (None, blocks[pair]))
        fetches.wait()

    @pl.when(jnp.logical_not(here))
    def _():
        fetches = Fetches(sems)
        for pair in range(quarter):
            fetch_source(right, source_slot(ops, chip, side, 2 * pair + 1) * rows, fetches, (None, blocks[pair]))
        fetches.wait()
        for pair in range(quarter):
            place = source_slot(ops, chip, side, 2 * pair + 1) * rows
            for b in range(right.shape[0]):
                right[b, aligned(full + place, rows, rows), :full] = -right[b, aligned(place, rows, rows), full:]
        if partials:
            row_start, count, col_start, cols, _ = jobs[0]
            place = source_slot(ops, chip, side, 1) * rows
            lhs = [stacked(left, row_start, count, aligned(start, rows, LANES)) for start in (place, full + place)]
            lhs = jnp.concatenate(lhs, 1)
            for index in range(partials[0].shape[0]):
                at = aligned(index % 2 * full + col_start, cols, LANES)
                rhs = [right[index // 2, aligned(start, rows, rows), at] for start in (place, full + place)]
                more = jnp.dot(lhs, jnp.concatenate(rhs, 0), preferred_element_type=jnp.float32)
                partials[0][index] = partials[0][index] + more

    trace_rows(group, jobs, left, right, partials, flip, weights, columns, out, product, flipped)


def trace_rows(group, jobs, left, right, partials, flip, weights, columns, out, product, flipped):
    fields = left.shape[0]
    parts = 2 * fields * fields

    def put(into, lane, at, block):
        cols = block.shape[1]
        for g in range(block.shape[0] // group):
            into[at * group : (at + 1) * group, lane + g * cols : lane + (g + 1) * cols] = block[g * group : (g + 1) * group]

    lane = 0
    for number, job in enumerate(jobs):
        _, count, _, cols, weight = job
        for index in range(fields * 2):
            if number == 0 and partials:
                value = partials[0][index]
            else:
                value = products_ahead(job, left, right, index)
            value = value.astype(jnp.bfloat16)
            for a in range(fields):
                block = value[a * count : (a + 1) * count]
                place = a * fields * 2 + index
                put(product, lane, place, block)
                if not weight:
                    put(flipped, lane, place, block.T)
        if weight:
            value = (weight * products_behind(job, left, right, flip)).astype(jnp.bfloat16)
            for index in range(fields * 2):
                for a in range(fields):
                    block = value[index * count : (index + 1) * count, a * cols : (a + 1) * cols]
                    put(flipped, lane, a * fields * 2 + index, block)
        lane += count // group * cols
    total = lax.dot_general(
        product[...], flipped[...], (((1,), (1,)), ((), ())), preferred_element_type=jnp.float32
    )
    side = parts * group
    row = lax.broadcasted_iota(jnp.int32, (side, side), 0)
    lane = lax.broadcasted_iota(jnp.int32, (side, side), 1)
    total = jnp.where(lax.rem(row, group) == lax.rem(lane, group), total, 0.0)
    total = jnp.sum(total.reshape(parts, group, side), 1)
    source = lax.broadcasted_iota(jnp.int32, (side, LANES), 0)
    lane = lax.broadcasted_iota(jnp.int32, (side, LANES), 1)
    spread = (source // group == lax.rem(lane, parts)).astype(jnp.float32)
    total = jnp.dot(total, spread, precision=lax.Precision.HIGHEST, preferred_element_type=jnp.float32)
    row = lax.broadcasted_iota(jnp.int32, (parts, LANES), 0)
    lane = lax.broadcasted_iota(jnp.int32, (parts, LANES), 1)
    total = jnp.where(lane // parts == row, total, 0.0)
    total = jnp.dot(total, weights[...], precision=lax.Precision.HIGHEST, preferred_element_type=jnp.float32)
    total = jnp.sum(total, 0, keepdims=True) * columns[:1] + columns[1:]
    out[...] = jnp.broadcast_to(total[:, None, :], out.shape)


def chain_weights(chain_factors, chain_target, fields):
    pairs = fields * fields
    parts = 2 * pairs
    codes = (
        (chain_factors[:, 0] * fields + chain_factors[:, 1]) * pairs
        + chain_factors[:, 2] * fields
        + chain_factors[:, 3]
    )
    row = jnp.arange(LANES, dtype=jnp.int32)
    first, second = row // parts, row % parts
    used = row < parts * parts
    ahead = jnp.where(used, (first // 2) * pairs + second // 2, -1)
    behind = jnp.where(used, (second // 2) * pairs + first // 2, -1)
    column = jnp.arange(LANES, dtype=jnp.int32)
    on_row = (ahead[:, None] == codes[None, :]).astype(jnp.float32)
    on_row = 0.5 * (on_row + (behind[:, None] == codes[None, :]).astype(jnp.float32))
    on_column = (chain_target[:, None] == (column % NCORR)[None, :]).astype(jnp.float32)
    counts = jnp.dot(on_row, on_column, precision=lax.Precision.HIGHEST)
    mixed = (first % 2 != second % 2)[:, None]
    both_imag = (first % 2 + second % 2 == 2)[:, None]
    real_sign = jnp.where(mixed, 0.0, jnp.where(both_imag, -1.0, 1.0))
    imag_sign = jnp.where(mixed, 1.0, 0.0)
    sign = jnp.where((column < WIN * NCORR)[None, :], real_sign, imag_sign)
    return counts * sign


def source_times(times, ops):
    time, chip, source = (lax.broadcasted_iota(jnp.int32, (times, ops, times), axis) for axis in range(3))
    pair = (time // 2 + times // 2 - source_lag(ops, chip)) % (times // 2)
    return (source == pair * 2 + chip % 2).astype(jnp.float32)


def per_device(times, ops, sink_fields, source_fields, source_live, chain_factors, chain_target):
    fields, _, rows, full = sink_fields.shape[1:]
    half = ops // 2
    share = full // half
    parts = 2 * fields * fields
    group = 2 * LANES // parts
    chip = lax.axis_index("op")
    separation = jnp.where(chip // half == lax.rem(chip, 2), 2, 1)
    lane = jnp.arange(LANES, dtype=jnp.int32)
    used = 2 * WIN * NCORR
    wanted = (lane < used) & (lane // NCORR % WIN + 1 == separation)
    scale = jnp.where(wanted, 1.0 / math.sqrt(times), 0.0)
    flag = jnp.where(lane == used, source_live[0].astype(jnp.float32), 0.0)
    columns = jnp.stack([scale, flag]).astype(jnp.float32)
    weights = chain_weights(chain_factors, chain_target, fields)

    any_spec = pl.BlockSpec(memory_space=pl.ANY)
    vmem_spec = pl.BlockSpec(memory_space=pltpu.VMEM)
    jobs = jobs_of(half, share, 0)
    lanes = sum(count // group * cols for _, count, _, cols, _ in jobs)
    most = max(count for _, count, _, _, weight in jobs if weight)
    tables = weights, columns, source_times(times, ops)
    operands = [
        jax.ShapeDtypeStruct((fields, full, 2 * full), jnp.bfloat16),
        jax.ShapeDtypeStruct((fields, 2 * full, 2 * full), jnp.bfloat16),
    ]
    params = pltpu.CompilerParams(vmem_limit_bytes=24 * 1024 * 1024)
    block_shape = jax.ShapeDtypeStruct((fields, 2, rows, full), jnp.bfloat16)
    owns = []

    def lay(blocks):
        outs = pl.pallas_call(
            functools.partial(first_kernel, ops),
            out_shape=[block_shape] * (ops // 4) + operands,
            in_specs=[any_spec] * len(blocks),
            out_specs=[vmem_spec] * (ops // 4 + 2),
            scratch_shapes=[pltpu.SemaphoreType.DMA((11 * ops // 4,))],
            compiler_params=params,
            cost_estimate=pl.CostEstimate(flops=0, bytes_accessed=10 * ops * rows * full, transcendentals=0),
        )(*blocks)
        owns.extend(outs[:-2])
        return outs

    blocks, last, laid, (weights, columns, picks) = send_blocks(times, ops, sink_fields[0], source_fields[0], tables, lay)
    blocks = owns + blocks
    early = int(ops == 4 and rows % LANES == 0)
    if early:
        operands.append(jax.ShapeDtypeStruct((fields * 2, fields * share, share), jnp.float32))
    laid = pl.pallas_call(
        functools.partial(lay_kernel, ops),
        out_shape=operands,
        in_specs=[any_spec] * len(blocks) + [vmem_spec] * 2,
        out_specs=[vmem_spec] * len(operands),
        scratch_shapes=[pltpu.SemaphoreType.DMA((5 * ops,))],
        input_output_aliases={len(blocks): 0, len(blocks) + 1: 1},
        compiler_params=params,
        cost_estimate=pl.CostEstimate(flops=0, bytes_accessed=10 * ops * rows * full, transcendentals=0),
    )(*blocks, *laid)
    count = len(last)
    partial_sums, *_ = pl.pallas_call(
        functools.partial(trace_kernel, ops, group, early),
        out_shape=[jax.ShapeDtypeStruct((times * ops, 1, LANES), jnp.float32)] + operands,
        in_specs=[any_spec] * count + [vmem_spec] * (len(operands) + 2),
        out_specs=[vmem_spec] * (len(operands) + 1),
        scratch_shapes=[
            pltpu.VMEM((fields, 2, most, 2 * full), jnp.bfloat16),
            pltpu.VMEM((parts * group, lanes), jnp.bfloat16),
            pltpu.VMEM((parts * group, lanes), jnp.bfloat16),
            pltpu.SemaphoreType.DMA((3 * ops // 4,)),
        ],
        input_output_aliases={count + index: 1 + index for index in range(len(operands))},
        compiler_params=params,
        cost_estimate=pl.CostEstimate(
            flops=4 * 2 * fields * fields * share * full * full, bytes_accessed=10 * ops * rows * full, transcendentals=0
        ),
    )(*last, *laid, weights, columns)
    shares = lax.all_to_all(partial_sums, AXES, 0, 0, tiled=True).reshape(times, ops, LANES)
    live = shares[:, 0, used]
    weight = jnp.sum(picks * live, -1)
    totals = jnp.sum(shares * weight[:, :, None], (0, 1))[:used]
    return totals.reshape(2, WIN, NCORR).transpose(0, 2, 1)


def solution(mesh):
    in_specs = (P("tm", None, None, "op", None), P("tm", None, None, "op", None), P("tm"), P(), P())
    body = functools.partial(per_device, mesh.shape["tm"], mesh.shape["op"])
    return jax.shard_map(body, mesh=mesh, in_specs=in_specs, out_specs=P(), check_vma=False)
```

```python
import functools
import math

import jax
import jax.numpy as jnp
from jax import lax
from jax.experimental import pallas as pl
from jax.experimental.pallas import tpu as pltpu
from jax.sharding import PartitionSpec as P

WIN = 2
NCORR = 16
AXES = ("tm", "op")
LANES = 128


def routes(times, ops, place):
    pairs = []
    for pair in range(times // 2):
        for core in range(2):
            for op in range(ops):
                target = place(pair, core, op)
                if target is not None:
                    to_pair, to_core, to_op = target
                    to_time = (to_pair % (times // 2)) * 2 + to_core
                    pairs.append(((pair * 2 + core) * ops + op, to_time * ops + to_op))
    return pairs


def sink_slot(ops, chip, core, step):
    half = ops // 2
    return core * half + ((chip % half) ^ (chip // half) ^ core ^ step)


def sink_target(ops, core, op, step):
    half = ops // 2
    side = op // half
    return side, core * half + ((op % half) ^ side ^ core ^ step)


def source_slot(ops, chip, core, step):
    low = core ^ (chip // (ops // 2)) ^ (chip & 1) ^ 1
    return (((chip >> 1) ^ 1 ^ (chip & 1) ^ low ^ step) << 1) + low


def source_lag(ops, chip):
    return 1 - (1 - chip % 2) * (chip // (ops // 2))


def source_target(ops, core, op, step):
    target = (((op >> 1) ^ 1 ^ (op & 1) ^ core ^ step) << 1) | core
    return (op & 1) ^ core ^ 1 ^ (target // (ops // 2)), target


def sink_holder(ops, core, chip):
    return core == chip // (ops // 2)


def send_blocks(times, ops, sink, source, tables, lay):
    def along(block, place):
        return lax.ppermute(block, AXES, routes(times, ops, place))

    def plain_sink(step, only):
        def place(pair, core, op):
            to_core, to_op = sink_target(ops, core, op, step)
            return None if only and not sink_holder(ops, to_core, to_op) else (pair, to_core, to_op)

        return place

    def plain_source(step, only):
        def place(pair, core, op):
            to_core, to_op = source_target(ops, core, op, step)
            to_pair = pair + source_lag(ops, to_op)
            return None if only and sink_holder(ops, to_core, to_op) else (to_pair, to_core, to_op)

        return place

    def pass_on(pair, core, op):
        if not sink_holder(ops, core, op):
            return pair, core, op ^ 1
        to_op = op ^ 2
        return pair - source_lag(ops, op) + source_lag(ops, to_op), to_op // (ops // 2), to_op

    def across(block):
        return along(block, lambda pair, core, op: (pair, 1 - core, op))

    holder = sink_holder(ops, lax.rem(lax.axis_index("tm"), 2), lax.axis_index("op"))
    here, firsts, held, last = [], [], [], []
    for pair in range(ops // 4):
        sink_first = along(sink, plain_sink(2 * pair + 1, False))
        source_first = along(source, plain_source(2 * pair, False))
        passed = along(jnp.where(holder, source_first, sink_first), pass_on)
        late_source, tables = lax.optimization_barrier((source, tables))
        source_own = along(late_source, plain_source(2 * pair + 1, True))
        sink_own = sink if pair == 0 else along(sink, plain_sink(2 * pair, True))
        here += [sink_first, source_first, sink_own, source_own]
        firsts.append(across(sink_first))
        firsts.append(across(source_first))
        held.append(passed)
        last.append(across(passed))
    *own, left, right = lay(here)
    return [across(block) for block in own] + held + firsts, last, (left, right), tables


class Fetches:
    def __init__(self, sems, used=0):
        self.sems, self.used, self.copies = sems, used, []

    def start(self, dst, *choices):
        sem = self.sems.at[self.used + len(self.copies)]
        taken = None
        for index, (condition, src) in enumerate(choices):
            copy = pltpu.make_async_copy(src, dst, sem)
            if index == len(choices) - 1:
                condition = taken
            elif taken is not None:
                condition, taken = jnp.logical_and(taken, condition), jnp.logical_and(taken, jnp.logical_not(condition))
            else:
                taken = jnp.logical_not(condition)
            if condition is None:
                copy.start()
            else:
                pl.when(condition)(copy.start)
        self.copies.append(copy)

    def wait(self):
        for copy in self.copies:
            copy.wait()


def aligned(start, size, unit):
    return pl.ds(pl.multiple_of(start, unit), size)


def fetch_source(right, place, fetches, *choices):
    rows, full = choices[0][1].shape[2:]
    inner = right.shape[1] // 2
    at, low = aligned(place, rows, rows), aligned(inner + place, rows, rows)
    for part, dst in ((0, right.at[:, at, :full]), (1, right.at[:, at, full:]), (0, right.at[:, low, full:])):
        fetches.start(dst, *[(condition, block.at[:, part]) for condition, block in choices])


def fetch_sink(left, place, fetches, *choices):
    rows, full = choices[0][1].shape[2:]
    for part in range(2):
        dst = left.at[:, aligned(place, rows, rows), pl.ds(part * full, full)]
        fetches.start(dst, *[(condition, block.at[:, part]) for condition, block in choices])


def jobs_of(half, share, member):
    jobs = [(member * share, share, member * share, share, 0)]
    for apart in range(1, half // 2 + 1):
        if 2 * apart < half:
            jobs.append((member * share, share, lax.rem(member + apart, half) * share, share, 2.0))
        elif share // 2 % LANES:
            jobs.append((member * share, share, lax.rem(member + apart, half) * share, share, 1.0))
        else:
            low = lax.rem(member, half // 2)
            start = low * share + member // (half // 2) * (share // 2)
            jobs.append((start, share // 2, (low + half // 2) * share, share, 2.0))
    return jobs


def stacked(left, start, count, lanes=slice(None)):
    rows = aligned(start, count, math.gcd(count, LANES))
    return jnp.concatenate([left[a, rows, lanes] for a in range(left.shape[0])], 0)


def products_ahead(job, left, right, index):
    row_start, count, col_start, cols, _ = job
    full = left.shape[1]
    rhs = right[index // 2, :, aligned(index % 2 * full + col_start, cols, LANES)]
    return jnp.dot(stacked(left, row_start, count), rhs, preferred_element_type=jnp.float32)


def products_behind(job, left, right, flip):
    row_start, count, col_start, cols, _ = job
    fields, full = left.shape[0], left.shape[1]
    unit = math.gcd(count, LANES)
    for b in range(fields):
        real_turned = right[b, :full, aligned(row_start, count, unit)].T
        imag_turned = right[b, :full, aligned(full + row_start, count, unit)].T
        flip[b, 0, :count, :full] = real_turned
        flip[b, 0, :count, full:] = -imag_turned
        flip[b, 1, :count, :full] = imag_turned
        flip[b, 1, :count, full:] = real_turned
    lhs = flip[:, :, :count, :].reshape(fields * 2 * count, 2 * full)
    rhs = stacked(left, col_start, cols)
    return lax.dot_general(lhs, rhs, (((1,), (1,)), ((), ())), preferred_element_type=jnp.float32)


def place_in(half, share):
    core = lax.rem(lax.axis_index("tm"), 2)
    chip = lax.axis_index("op")
    return core, chip, jobs_of(half, share, lax.rem(chip, half) // 2 * 2 + core)


def first_kernel(ops, *refs):
    quarter = ops // 4
    outs = refs[4 * quarter : 5 * quarter]
    left, right, sems = refs[5 * quarter :]
    rows, full = refs[0].shape[2:]
    core, chip, _ = place_in(ops // 2, full // (ops // 2))
    here = sink_holder(ops, core, chip)
    fetches = Fetches(sems)
    for pair in range(quarter):
        firsts, (sink_own, source_own) = refs[4 * pair : 4 * pair + 2], refs[4 * pair + 2 : 4 * pair + 4]
        fetches.start(outs[pair], (here, sink_own), (None, source_own))
        fetch_sink(left, sink_slot(ops, chip, core, 2 * pair + 1) * rows, fetches, (None, firsts[0]))
        fetch_source(right, source_slot(ops, chip, core, 2 * pair) * rows, fetches, (None, firsts[1]))
    fetches.wait()


def lay_kernel(ops, *refs):
    half = ops // 2
    quarter = ops // 4
    blocks = refs[: 5 * quarter]
    left, right, *partials, sems = refs[5 * quarter + 2 :]
    rows, full = blocks[0].shape[2:]
    core, chip, jobs = place_in(half, full // half)
    here = sink_holder(ops, core, chip)
    side = chip // half
    fetches = Fetches(sems)
    for pair in range(quarter):
        own, own_across, passed = blocks[pair], blocks[quarter + pair], blocks[2 * quarter + pair]
        sink_first, source_first = blocks[3 * quarter + 2 * pair : 3 * quarter + 2 * pair + 2]
        fetch_sink(left, sink_slot(ops, chip, 1 - core, 2 * pair + 1) * rows, fetches, (None, sink_first))
        fetch_source(right, source_slot(ops, chip, 1 - core, 2 * pair) * rows, fetches, (None, source_first))
        place = sink_slot(ops, chip, side, 2 * pair) * rows
        fetch_sink(left, place, fetches, (here, own), (None, own_across))
        place = source_slot(ops, chip, 1 - side, 2 * pair + 1) * rows
        fetch_source(right, place, fetches, (here, own_across), (None, own))

        @pl.when(here)
        def _():
            mine = Fetches(sems, len(fetches.copies))
            fetch_source(right, source_slot(ops, chip, side, 2 * pair + 1) * rows, mine, (None, passed))
            mine.wait()

        @pl.when(jnp.logical_not(here))
        def _():
            mine = Fetches(sems, len(fetches.copies))
            fetch_sink(left, sink_slot(ops, chip, 1 - side, 2 * pair) * rows, mine, (None, passed))
            mine.wait()
    fetches.wait()
    for b in range(right.shape[0]):
        right[b, full:, :full] = -right[b, :full, full:]
    if partials:

        @pl.when(jnp.logical_not(here))
        def _():
            place = source_slot(ops, chip, side, 1) * rows
            for start in (place, full + place):
                right[:, aligned(start, rows, rows), :] = jnp.zeros((right.shape[0], rows, 2 * full), right.dtype)

        for index in range(partials[0].shape[0]):
            partials[0][index] = products_ahead(jobs[0], left, right, index)


def trace_kernel(ops, group, early, *refs):
    half = ops // 2
    quarter = ops // 4
    blocks = refs[:quarter]
    left, right, *partials, weights, columns, out = refs[quarter : quarter + 2 + early + 3]
    flip, product, flipped, sems = refs[-4:]
    rows, full = blocks[0].shape[2:]
    core, chip, jobs = place_in(half, full // half)
    here = sink_holder(ops, core, chip)
    side = chip // half

    @pl.when(here)
    def _():
        fetches = Fetches(sems)
        for pair in range(quarter):
            fetch_sink(left, sink_slot(ops, chip, 1 - side, 2 * pair) * rows, fetches, (None, blocks[pair]))
        fetches.wait()

    @pl.when(jnp.logical_not(here))
    def _():
        fetches = Fetches(sems)
        for pair in range(quarter):
            fetch_source(right, source_slot(ops, chip, side, 2 * pair + 1) * rows, fetches, (None, blocks[pair]))
        fetches.wait()
        for pair in range(quarter):
            place = source_slot(ops, chip, side, 2 * pair + 1) * rows
            for b in range(right.shape[0]):
                right[b, aligned(full + place, rows, rows), :full] = -right[b, aligned(place, rows, rows), full:]
        if partials:
            row_start, count, col_start, cols, _ = jobs[0]
            place = source_slot(ops, chip, side, 1) * rows
            lhs = [stacked(left, row_start, count, aligned(start, rows, LANES)) for start in (place, full + place)]
            lhs = jnp.concatenate(lhs, 1)
            for index in range(partials[0].shape[0]):
                at = aligned(index % 2 * full + col_start, cols, LANES)
                rhs = [right[index // 2, aligned(start, rows, rows), at] for start in (place, full + place)]
                more = jnp.dot(lhs, jnp.concatenate(rhs, 0), preferred_element_type=jnp.float32)
                partials[0][index] = partials[0][index] + more

    trace_rows(group, jobs, left, right, partials, flip, weights, columns, out, product, flipped)


def trace_rows(group, jobs, left, right, partials, flip, weights, columns, out, product, flipped):
    fields = left.shape[0]
    parts = 2 * fields * fields

    def put(into, lane, at, block):
        cols = block.shape[1]
        for g in range(block.shape[0] // group):
            into[at * group : (at + 1) * group, lane + g * cols : lane + (g + 1) * cols] = block[g * group : (g + 1) * group]

    lane = 0
    for number, job in enumerate(jobs):
        _, count, _, cols, weight = job
        for index in range(fields * 2):
            if number == 0 and partials:
                value = partials[0][index]
            else:
                value = products_ahead(job, left, right, index)
            value = value.astype(jnp.bfloat16)
            for a in range(fields):
                block = value[a * count : (a + 1) * count]
                place = a * fields * 2 + index
                put(product, lane, place, block)
                if not weight:
                    put(flipped, lane, place, block.T)
        if weight:
            value = (weight * products_behind(job, left, right, flip)).astype(jnp.bfloat16)
            for index in range(fields * 2):
                for a in range(fields):
                    block = value[index * count : (index + 1) * count, a * cols : (a + 1) * cols]
                    put(flipped, lane, a * fields * 2 + index, block)
        lane += count // group * cols
    total = lax.dot_general(
        product[...], flipped[...], (((1,), (1,)), ((), ())), preferred_element_type=jnp.float32
    )
    side = parts * group
    row = lax.broadcasted_iota(jnp.int32, (side, side), 0)
    lane = lax.broadcasted_iota(jnp.int32, (side, side), 1)
    total = jnp.where(lax.rem(row, group) == lax.rem(lane, group), total, 0.0)
    total = jnp.sum(total.reshape(parts, group, side), 1)
    source = lax.broadcasted_iota(jnp.int32, (side, LANES), 0)
    lane = lax.broadcasted_iota(jnp.int32, (side, LANES), 1)
    spread = (source // group == lax.rem(lane, parts)).astype(jnp.float32)
    total = jnp.dot(total, spread, precision=lax.Precision.HIGHEST, preferred_element_type=jnp.float32)
    row = lax.broadcasted_iota(jnp.int32, (parts, LANES), 0)
    lane = lax.broadcasted_iota(jnp.int32, (parts, LANES), 1)
    total = jnp.where(lane // parts == row, total, 0.0)
    total = jnp.dot(total, weights[...], precision=lax.Precision.HIGHEST, preferred_element_type=jnp.float32)
    total = jnp.sum(total, 0, keepdims=True) * columns[:1] + columns[1:]
    out[...] = jnp.broadcast_to(total[:, None, :], out.shape)


def chain_weights(chain_factors, chain_target, fields):
    pairs = fields * fields
    parts = 2 * pairs
    codes = (
        (chain_factors[:, 0] * fields + chain_factors[:, 1]) * pairs
        + chain_factors[:, 2] * fields
        + chain_factors[:, 3]
    )
    row = jnp.arange(LANES, dtype=jnp.int32)
    first, second = row // parts, row % parts
    used = row < parts * parts
    ahead = jnp.where(used, (first // 2) * pairs + second // 2, -1)
    behind = jnp.where(used, (second // 2) * pairs + first // 2, -1)
    column = jnp.arange(LANES, dtype=jnp.int32)
    on_row = (ahead[:, None] == codes[None, :]).astype(jnp.float32)
    on_row = 0.5 * (on_row + (behind[:, None] == codes[None, :]).astype(jnp.float32))
    on_column = (chain_target[:, None] == (column % NCORR)[None, :]).astype(jnp.float32)
    counts = jnp.dot(on_row, on_column, precision=lax.Precision.HIGHEST)
    mixed = (first % 2 != second % 2)[:, None]
    both_imag = (first % 2 + second % 2 == 2)[:, None]
    real_sign = jnp.where(mixed, 0.0, jnp.where(both_imag, -1.0, 1.0))
    imag_sign = jnp.where(mixed, 1.0, 0.0)
    sign = jnp.where((column < WIN * NCORR)[None, :], real_sign, imag_sign)
    return counts * sign


def source_times(times, ops):
    time, chip, source = (lax.broadcasted_iota(jnp.int32, (times, ops, times), axis) for axis in range(3))
    pair = (time // 2 + times // 2 - source_lag(ops, chip)) % (times // 2)
    return (source == pair * 2 + chip % 2).astype(jnp.float32)


def per_device(times, ops, sink_fields, source_fields, source_live, chain_factors, chain_target):
    fields, _, rows, full = sink_fields.shape[1:]
    half = ops // 2
    share = full // half
    parts = 2 * fields * fields
    group = 2 * LANES // parts
    chip = lax.axis_index("op")
    separation = jnp.where(chip // half == lax.rem(chip, 2), 2, 1)
    lane = jnp.arange(LANES, dtype=jnp.int32)
    used = 2 * WIN * NCORR
    wanted = (lane < used) & (lane // NCORR % WIN + 1 == separation)
    scale = jnp.where(wanted, 1.0 / math.sqrt(times), 0.0)
    flag = jnp.where(lane == used, source_live[0].astype(jnp.float32), 0.0)
    columns = jnp.stack([scale, flag]).astype(jnp.float32)
    weights = chain_weights(chain_factors, chain_target, fields)

    any_spec = pl.BlockSpec(memory_space=pl.ANY)
    vmem_spec = pl.BlockSpec(memory_space=pltpu.VMEM)
    jobs = jobs_of(half, share, 0)
    lanes = sum(count // group * cols for _, count, _, cols, _ in jobs)
    most = max(count for _, count, _, _, weight in jobs if weight)
    tables = weights, columns, source_times(times, ops)
    operands = [
        jax.ShapeDtypeStruct((fields, full, 2 * full), jnp.bfloat16),
        jax.ShapeDtypeStruct((fields, 2 * full, 2 * full), jnp.bfloat16),
    ]
    params = pltpu.CompilerParams(vmem_limit_bytes=24 * 1024 * 1024)
    block_shape = jax.ShapeDtypeStruct((fields, 2, rows, full), jnp.bfloat16)
    owns = []

    def lay(blocks):
        outs = pl.pallas_call(
            functools.partial(first_kernel, ops),
            out_shape=[block_shape] * (ops // 4) + operands,
            in_specs=[any_spec] * len(blocks),
            out_specs=[vmem_spec] * (ops // 4 + 2),
            scratch_shapes=[pltpu.SemaphoreType.DMA((11 * ops // 4,))],
            compiler_params=params,
            cost_estimate=pl.CostEstimate(flops=0, bytes_accessed=10 * ops * rows * full, transcendentals=0),
        )(*blocks)
        owns.extend(outs[:-2])
        return outs

    blocks, last, laid, (weights, columns, picks) = send_blocks(times, ops, sink_fields[0], source_fields[0], tables, lay)
    blocks = owns + blocks
    early = int(ops == 4 and rows % LANES == 0)
    if early:
        operands.append(jax.ShapeDtypeStruct((fields * 2, fields * share, share), jnp.float32))
    laid = pl.pallas_call(
        functools.partial(lay_kernel, ops),
        out_shape=[pltpu.VMEM(operand.shape, operand.dtype) for operand in operands],
        in_specs=[any_spec] * len(blocks) + [vmem_spec] * 2,
        out_specs=[vmem_spec] * len(operands),
        scratch_shapes=[pltpu.SemaphoreType.DMA((5 * ops,))],
        input_output_aliases={len(blocks): 0, len(blocks) + 1: 1},
        compiler_params=params,
        cost_estimate=pl.CostEstimate(flops=0, bytes_accessed=10 * ops * rows * full, transcendentals=0),
    )(*blocks, *laid)
    count = len(last)
    partial_sums, *_ = pl.pallas_call(
        functools.partial(trace_kernel, ops, group, early),
        out_shape=[jax.ShapeDtypeStruct((times * ops, 1, LANES), jnp.float32)] + operands,
        in_specs=[any_spec] * count + [vmem_spec] * (len(operands) + 2),
        out_specs=[vmem_spec] * (len(operands) + 1),
        scratch_shapes=[
            pltpu.VMEM((fields, 2, most, 2 * full), jnp.bfloat16),
            pltpu.VMEM((parts * group, lanes), jnp.bfloat16),
            pltpu.VMEM((parts * group, lanes), jnp.bfloat16),
            pltpu.SemaphoreType.DMA((3 * ops // 4,)),
        ],
        input_output_aliases={count + index: 1 + index for index in range(len(operands))},
        compiler_params=params,
        cost_estimate=pl.CostEstimate(
            flops=4 * 2 * fields * fields * share * full * full, bytes_accessed=10 * ops * rows * full, transcendentals=0
        ),
    )(*last, *laid, weights, columns)
    shares = lax.all_to_all(partial_sums, AXES, 0, 0, tiled=True).reshape(times, ops, LANES)
    live = shares[:, 0, used]
    weight = jnp.sum(picks * live, -1)
    totals = jnp.sum(shares * weight[:, :, None], (0, 1))[:used]
    return totals.reshape(2, WIN, NCORR).transpose(0, 2, 1)


def solution(mesh):
    in_specs = (P("tm", None, None, "op", None), P("tm", None, None, "op", None), P("tm"), P(), P())
    body = functools.partial(per_device, mesh.shape["tm"], mesh.shape["op"])
    return jax.shard_map(body, mesh=mesh, in_specs=in_specs, out_specs=P(), check_vma=False)
```

```python
import functools
import math

import jax
import jax.numpy as jnp
from jax import lax
from jax.experimental import pallas as pl
from jax.experimental.pallas import tpu as pltpu
from jax.sharding import PartitionSpec as P

WIN = 2
NCORR = 16
AXES = ("tm", "op")
LANES = 128


def routes(times, ops, place):
    pairs = []
    for pair in range(times // 2):
        for core in range(2):
            for op in range(ops):
                target = place(pair, core, op)
                if target is not None:
                    to_pair, to_core, to_op = target
                    to_time = (to_pair % (times // 2)) * 2 + to_core
                    pairs.append(((pair * 2 + core) * ops + op, to_time * ops + to_op))
    return pairs


def sink_slot(ops, chip, core, step):
    half = ops // 2
    return core * half + ((chip % half) ^ (chip // half) ^ core ^ step)


def sink_target(ops, core, op, step):
    half = ops // 2
    side = op // half
    return side, core * half + ((op % half) ^ side ^ core ^ step)


def source_slot(ops, chip, core, step):
    low = core ^ (chip // (ops // 2)) ^ (chip & 1) ^ 1
    return (((chip >> 1) ^ 1 ^ (chip & 1) ^ low ^ step) << 1) + low


def source_lag(ops, chip):
    return 1 - (1 - chip % 2) * (chip // (ops // 2))


def source_target(ops, core, op, step):
    target = (((op >> 1) ^ 1 ^ (op & 1) ^ core ^ step) << 1) | core
    return (op & 1) ^ core ^ 1 ^ (target // (ops // 2)), target


def sink_holder(ops, core, chip):
    return core == chip // (ops // 2)


def send_blocks(times, ops, sink, source, tables):
    def along(block, place):
        return lax.ppermute(block, AXES, routes(times, ops, place))

    def plain_sink(step, only):
        def place(pair, core, op):
            to_core, to_op = sink_target(ops, core, op, step)
            return None if only and not sink_holder(ops, to_core, to_op) else (pair, to_core, to_op)

        return place

    def plain_source(step, only):
        def place(pair, core, op):
            to_core, to_op = source_target(ops, core, op, step)
            to_pair = pair + source_lag(ops, to_op)
            return None if only and sink_holder(ops, to_core, to_op) else (to_pair, to_core, to_op)

        return place

    def pass_on(pair, core, op):
        if not sink_holder(ops, core, op):
            return pair, core, op ^ 1
        to_op = op ^ 2
        return pair - source_lag(ops, op) + source_lag(ops, to_op), to_op // (ops // 2), to_op

    def across(block):
        return along(block, lambda pair, core, op: (pair, 1 - core, op))

    holder = sink_holder(ops, lax.rem(lax.axis_index("tm"), 2), lax.axis_index("op"))
    blocks, last = [], []
    for pair in range(ops // 4):
        sink_first = along(sink, plain_sink(2 * pair + 1, False))
        source_first = along(source, plain_source(2 * pair, False))
        passed = along(jnp.where(holder, source_first, sink_first), pass_on)
        late_source, tables = lax.optimization_barrier((source, tables))
        source_own = along(late_source, plain_source(2 * pair + 1, True))
        sink_own = sink if pair == 0 else along(sink, plain_sink(2 * pair, True))
        own = jnp.where(holder, sink_own, source_own)
        three = [sink_first, source_first, own]
        blocks += three + [across(block) for block in three] + [passed]
        last.append(across(passed))
    return blocks, last, tables


class Fetches:
    def __init__(self, sems, used=0, begin=True):
        self.sems, self.used, self.begin, self.copies = sems, used, begin, []

    def start(self, dst, *choices):
        sem = self.sems.at[self.used + len(self.copies)]
        taken = None
        for index, (condition, src) in enumerate(choices):
            copy = pltpu.make_async_copy(src, dst, sem)
            if index == len(choices) - 1:
                condition = taken
            elif taken is not None:
                condition, taken = jnp.logical_and(taken, condition), jnp.logical_and(taken, jnp.logical_not(condition))
            else:
                taken = jnp.logical_not(condition)
            if not self.begin:
                continue
            if condition is None:
                copy.start()
            else:
                pl.when(condition)(copy.start)
        self.copies.append(copy)

    def wait(self):
        for copy in self.copies:
            copy.wait()


def aligned(start, size, unit):
    return pl.ds(pl.multiple_of(start, unit), size)


def fetch_source(right, place, fetches, *choices):
    rows, full = choices[0][1].shape[2:]
    inner = right.shape[1] // 2
    at, low = aligned(place, rows, rows), aligned(inner + place, rows, rows)
    for part, dst in ((0, right.at[:, at, :full]), (1, right.at[:, at, full:]), (0, right.at[:, low, full:])):
        fetches.start(dst, *[(condition, block.at[:, part]) for condition, block in choices])


def fetch_sink(left, place, fetches, *choices):
    rows, full = choices[0][1].shape[2:]
    for part in range(2):
        dst = left.at[:, aligned(place, rows, rows), pl.ds(part * full, full)]
        fetches.start(dst, *[(condition, block.at[:, part]) for condition, block in choices])


def jobs_of(half, share, member):
    jobs = [(member * share, share, member * share, share, 0)]
    for apart in range(1, half // 2 + 1):
        if 2 * apart < half:
            jobs.append((member * share, share, lax.rem(member + apart, half) * share, share, 2.0))
        elif share // 2 % LANES:
            jobs.append((member * share, share, lax.rem(member + apart, half) * share, share, 1.0))
        else:
            low = lax.rem(member, half // 2)
            start = low * share + member // (half // 2) * (share // 2)
            jobs.append((start, share // 2, (low + half // 2) * share, share, 2.0))
    return jobs


def stacked(left, start, count, lanes=slice(None)):
    rows = aligned(start, count, math.gcd(count, LANES))
    return jnp.concatenate([left[a, rows, lanes] for a in range(left.shape[0])], 0)


def products_ahead(job, left, right, index):
    row_start, count, col_start, cols, _ = job
    full = left.shape[1]
    rhs = right[index // 2, :, aligned(index % 2 * full + col_start, cols, LANES)]
    return jnp.dot(stacked(left, row_start, count), rhs, preferred_element_type=jnp.float32)


def products_behind(job, left, right, flip):
    row_start, count, col_start, cols, _ = job
    fields, full = left.shape[0], left.shape[1]
    unit = math.gcd(count, LANES)
    for b in range(fields):
        real_turned = right[b, :full, aligned(row_start, count, unit)].T
        imag_turned = right[b, :full, aligned(full + row_start, count, unit)].T
        flip[b, 0, :count, :full] = real_turned
        flip[b, 0, :count, full:] = -imag_turned
        flip[b, 1, :count, :full] = imag_turned
        flip[b, 1, :count, full:] = real_turned
    lhs = flip[:, :, :count, :].reshape(fields * 2 * count, 2 * full)
    rhs = stacked(left, col_start, cols)
    return lax.dot_general(lhs, rhs, (((1,), (1,)), ((), ())), preferred_element_type=jnp.float32)


def place_in(half, share):
    core = lax.rem(lax.axis_index("tm"), 2)
    chip = lax.axis_index("op")
    return core, chip, jobs_of(half, share, lax.rem(chip, half) // 2 * 2 + core)


def lay_kernel(ops, *refs):
    half = ops // 2
    many = 7 * (ops // 4)
    left, right, *partials, sems = refs[many:]
    rows, full = refs[0].shape[2:]
    core, chip, jobs = place_in(half, full // half)
    here = sink_holder(ops, core, chip)
    side = chip // half
    fetches = Fetches(sems)
    for pair in range(ops // 4):
        blocks = refs[7 * pair : 7 * pair + 7]
        for turn in range(2):
            at = core if turn == 0 else 1 - core
            sink_first, source_first, _ = blocks[3 * turn : 3 * turn + 3]
            fetch_sink(left, sink_slot(ops, chip, at, 2 * pair + 1) * rows, fetches, (None, sink_first))
            fetch_source(right, source_slot(ops, chip, at, 2 * pair) * rows, fetches, (None, source_first))
        own, own_across, passed = blocks[2], blocks[5], blocks[6]
        place = sink_slot(ops, chip, side, 2 * pair) * rows
        fetch_sink(left, place, fetches, (here, own), (None, own_across))
        place = source_slot(ops, chip, 1 - side, 2 * pair + 1) * rows
        fetch_source(right, place, fetches, (here, own_across), (None, own))


        @pl.when(here)
        def _():
            mine = Fetches(sems, len(fetches.copies))
            fetch_source(right, source_slot(ops, chip, side, 2 * pair + 1) * rows, mine, (None, passed))
            mine.wait()

        @pl.when(jnp.logical_not(here))
        def _():
            mine = Fetches(sems, len(fetches.copies))
            fetch_sink(left, sink_slot(ops, chip, 1 - side, 2 * pair) * rows, mine, (None, passed))
            mine.wait()
    fetches.wait()
    for b in range(right.shape[0]):
        right[b, full:, :full] = -right[b, :full, full:]
    if partials:

        @pl.when(jnp.logical_not(here))
        def _():
            place = source_slot(ops, chip, side, 1) * rows
            for start in (place, full + place):
                right[:, aligned(start, rows, rows), :] = jnp.zeros((right.shape[0], rows, 2 * full), right.dtype)

        for index in range(partials[0].shape[0]):
            partials[0][index] = products_ahead(jobs[0], left, right, index)


def trace_kernel(ops, group, early, *refs):
    half = ops // 2
    quarter = ops // 4
    blocks = refs[:quarter]
    left, right, *partials, weights, columns, out = refs[quarter : quarter + 2 + early + 3]
    flip, product, flipped, sems = refs[-4:]
    rows, full = blocks[0].shape[2:]
    core, chip, jobs = place_in(half, full // half)
    here = sink_holder(ops, core, chip)
    side = chip // half

    def fetch_late(begin):
        @pl.when(here)
        def _():
            fetches = Fetches(sems, begin=begin)
            for pair in range(quarter):
                fetch_sink(left, sink_slot(ops, chip, 1 - side, 2 * pair) * rows, fetches, (None, blocks[pair]))
            if not begin:
                fetches.wait()

        @pl.when(jnp.logical_not(here))
        def _():
            fetches = Fetches(sems, begin=begin)
            for pair in range(quarter):
                fetch_source(right, source_slot(ops, chip, side, 2 * pair + 1) * rows, fetches, (None, blocks[pair]))
            if not begin:
                fetches.wait()
                for pair in range(quarter):
                    place = source_slot(ops, chip, side, 2 * pair + 1) * rows
                    for b in range(right.shape[0]):
                        right[b, aligned(full + place, rows, rows), :full] = -right[b, aligned(place, rows, rows), full:]

    fetch_late(True)
    if partials:

        @pl.when(jnp.logical_not(here))
        def _():
            row_start, count, col_start, cols, _ = jobs[0]
            place = source_slot(ops, chip, side, 1) * rows
            lhs = [stacked(left, row_start, count, aligned(start, rows, LANES)) for start in (place, full + place)]
            lhs = jnp.concatenate(lhs, 1)
            at = aligned(col_start, cols, LANES)
            for b in range(blocks[0].shape[0]):
                real, imag = blocks[0][b, 0, :, at], blocks[0][b, 1, :, at]
                for part, rhs in enumerate(((real, -imag), (imag, real))):
                    more = jnp.dot(lhs, jnp.concatenate(rhs, 0), preferred_element_type=jnp.float32)
                    partials[0][2 * b + part] = partials[0][2 * b + part] + more

    ready = functools.partial(fetch_late, False)
    trace_rows(group, jobs, ready, left, right, partials, flip, weights, columns, out, product, flipped)


def trace_rows(group, jobs, ready, left, right, partials, flip, weights, columns, out, product, flipped):
    fields = left.shape[0]
    parts = 2 * fields * fields

    def put(into, lane, at, block):
        cols = block.shape[1]
        for g in range(block.shape[0] // group):
            into[at * group : (at + 1) * group, lane + g * cols : lane + (g + 1) * cols] = block[g * group : (g + 1) * group]

    lane = 0
    for number, job in enumerate(jobs):
        if number == len(partials):
            ready()
        _, count, _, cols, weight = job
        for index in range(fields * 2):
            if number == 0 and partials:
                value = partials[0][index]
            else:
                value = products_ahead(job, left, right, index)
            value = value.astype(jnp.bfloat16)
            for a in range(fields):
                block = value[a * count : (a + 1) * count]
                place = a * fields * 2 + index
                put(product, lane, place, block)
                if not weight:
                    put(flipped, lane, place, block.T)
        if weight:
            value = (weight * products_behind(job, left, right, flip)).astype(jnp.bfloat16)
            for index in range(fields * 2):
                for a in range(fields):
                    block = value[index * count : (index + 1) * count, a * cols : (a + 1) * cols]
                    put(flipped, lane, a * fields * 2 + index, block)
        lane += count // group * cols
    total = lax.dot_general(
        product[...], flipped[...], (((1,), (1,)), ((), ())), preferred_element_type=jnp.float32
    )
    side = parts * group
    row = lax.broadcasted_iota(jnp.int32, (side, side), 0)
    lane = lax.broadcasted_iota(jnp.int32, (side, side), 1)
    total = jnp.where(lax.rem(row, group) == lax.rem(lane, group), total, 0.0)
    total = jnp.sum(total.reshape(parts, group, side), 1)
    source = lax.broadcasted_iota(jnp.int32, (side, LANES), 0)
    lane = lax.broadcasted_iota(jnp.int32, (side, LANES), 1)
    spread = (source // group == lax.rem(lane, parts)).astype(jnp.float32)
    total = jnp.dot(total, spread, precision=lax.Precision.HIGHEST, preferred_element_type=jnp.float32)
    row = lax.broadcasted_iota(jnp.int32, (parts, LANES), 0)
    lane = lax.broadcasted_iota(jnp.int32, (parts, LANES), 1)
    total = jnp.where(lane // parts == row, total, 0.0)
    total = jnp.dot(total, weights[...], precision=lax.Precision.HIGHEST, preferred_element_type=jnp.float32)
    total = jnp.sum(total, 0, keepdims=True) * columns[:1] + columns[1:]
    out[...] = jnp.broadcast_to(total[:, None, :], out.shape)


def chain_weights(chain_factors, chain_target, fields):
    pairs = fields * fields
    parts = 2 * pairs
    codes = (
        (chain_factors[:, 0] * fields + chain_factors[:, 1]) * pairs
        + chain_factors[:, 2] * fields
        + chain_factors[:, 3]
    )
    row = jnp.arange(LANES, dtype=jnp.int32)
    first, second = row // parts, row % parts
    used = row < parts * parts
    ahead = jnp.where(used, (first // 2) * pairs + second // 2, -1)
    behind = jnp.where(used, (second // 2) * pairs + first // 2, -1)
    column = jnp.arange(LANES, dtype=jnp.int32)
    on_row = (ahead[:, None] == codes[None, :]).astype(jnp.float32)
    on_row = 0.5 * (on_row + (behind[:, None] == codes[None, :]).astype(jnp.float32))
    on_column = (chain_target[:, None] == (column % NCORR)[None, :]).astype(jnp.float32)
    counts = jnp.dot(on_row, on_column, precision=lax.Precision.HIGHEST)
    mixed = (first % 2 != second % 2)[:, None]
    both_imag = (first % 2 + second % 2 == 2)[:, None]
    real_sign = jnp.where(mixed, 0.0, jnp.where(both_imag, -1.0, 1.0))
    imag_sign = jnp.where(mixed, 1.0, 0.0)
    sign = jnp.where((column < WIN * NCORR)[None, :], real_sign, imag_sign)
    return counts * sign


def source_times(times, ops):
    time, chip, source = (lax.broadcasted_iota(jnp.int32, (times, ops, times), axis) for axis in range(3))
    pair = (time // 2 + times // 2 - source_lag(ops, chip)) % (times // 2)
    return (source == pair * 2 + chip % 2).astype(jnp.float32)


def per_device(times, ops, sink_fields, source_fields, source_live, chain_factors, chain_target):
    fields, _, rows, full = sink_fields.shape[1:]
    half = ops // 2
    share = full // half
    parts = 2 * fields * fields
    group = 2 * LANES // parts
    chip = lax.axis_index("op")
    separation = jnp.where(chip // half == lax.rem(chip, 2), 2, 1)
    lane = jnp.arange(LANES, dtype=jnp.int32)
    used = 2 * WIN * NCORR
    wanted = (lane < used) & (lane // NCORR % WIN + 1 == separation)
    scale = jnp.where(wanted, 1.0 / math.sqrt(times), 0.0)
    flag = jnp.where(lane == used, source_live[0].astype(jnp.float32), 0.0)
    columns = jnp.stack([scale, flag]).astype(jnp.float32)
    weights = chain_weights(chain_factors, chain_target, fields)

    any_spec = pl.BlockSpec(memory_space=pl.ANY)
    vmem_spec = pl.BlockSpec(memory_space=pltpu.VMEM)
    jobs = jobs_of(half, share, 0)
    lanes = sum(count // group * cols for _, count, _, cols, _ in jobs)
    most = max(count for _, count, _, _, weight in jobs if weight)
    tables = weights, columns, source_times(times, ops)
    blocks, last, (weights, columns, picks) = send_blocks(times, ops, sink_fields[0], source_fields[0], tables)
    operands = [
        jax.ShapeDtypeStruct((fields, full, 2 * full), jnp.bfloat16),
        jax.ShapeDtypeStruct((fields, 2 * full, 2 * full), jnp.bfloat16),
    ]
    early = int(ops == 4 and rows % LANES == 0)
    if early:
        operands.append(jax.ShapeDtypeStruct((fields * 2, fields * share, share), jnp.float32))
    params = pltpu.CompilerParams(vmem_limit_bytes=24 * 1024 * 1024)
    laid = pl.pallas_call(
        functools.partial(lay_kernel, ops),
        out_shape=operands,
        in_specs=[any_spec] * len(blocks),
        out_specs=[vmem_spec] * len(operands),
        scratch_shapes=[pltpu.SemaphoreType.DMA((5 * ops,))],
        compiler_params=params,
        cost_estimate=pl.CostEstimate(flops=0, bytes_accessed=10 * ops * rows * full, transcendentals=0),
    )(*blocks)
    count = len(last)
    partial_sums, *_ = pl.pallas_call(
        functools.partial(trace_kernel, ops, group, early),
        out_shape=[jax.ShapeDtypeStruct((times * ops, 1, LANES), jnp.float32)] + operands,
        in_specs=[vmem_spec if early else any_spec] * count + [vmem_spec] * (len(operands) + 2),
        out_specs=[vmem_spec] * (len(operands) + 1),
        scratch_shapes=[
            pltpu.VMEM((fields, 2, most, 2 * full), jnp.bfloat16),
            pltpu.VMEM((parts * group, lanes), jnp.bfloat16),
            pltpu.VMEM((parts * group, lanes), jnp.bfloat16),
            pltpu.SemaphoreType.DMA((3 * ops // 4,)),
        ],
        input_output_aliases={count + index: 1 + index for index in range(len(operands))},
        compiler_params=params,
        cost_estimate=pl.CostEstimate(
            flops=4 * 2 * fields * fields * share * full * full, bytes_accessed=10 * ops * rows * full, transcendentals=0
        ),
    )(*last, *laid, weights, columns)
    shares = lax.all_to_all(partial_sums, AXES, 0, 0, tiled=True).reshape(times, ops, LANES)
    live = shares[:, 0, used]
    weight = jnp.sum(picks * live, -1)
    totals = jnp.sum(shares * weight[:, :, None], (0, 1))[:used]
    return totals.reshape(2, WIN, NCORR).transpose(0, 2, 1)


def solution(mesh):
    in_specs = (P("tm", None, None, "op", None), P("tm", None, None, "op", None), P("tm"), P(), P())
    body = functools.partial(per_device, mesh.shape["tm"], mesh.shape["op"])
    return jax.shard_map(body, mesh=mesh, in_specs=in_specs, out_specs=P(), check_vma=False)
```

```python
import functools
import math

import jax
import jax.numpy as jnp
from jax import lax
from jax.experimental import pallas as pl
from jax.experimental.pallas import tpu as pltpu
from jax.sharding import PartitionSpec as P

WIN = 2
NCORR = 16
AXES = ("tm", "op")
LANES = 128


def routes(times, ops, place):
    pairs = []
    for pair in range(times // 2):
        for core in range(2):
            for op in range(ops):
                target = place(pair, core, op)
                if target is not None:
                    to_pair, to_core, to_op = target
                    to_time = (to_pair % (times // 2)) * 2 + to_core
                    pairs.append(((pair * 2 + core) * ops + op, to_time * ops + to_op))
    return pairs


def sink_slot(ops, chip, core, step):
    half = ops // 2
    return core * half + ((chip % half) ^ (chip // half) ^ core ^ step)


def sink_target(ops, core, op, step):
    half = ops // 2
    side = op // half
    return side, core * half + ((op % half) ^ side ^ core ^ step)


def source_slot(ops, chip, core, step):
    low = core ^ (chip // (ops // 2)) ^ (chip & 1) ^ 1
    return (((chip >> 1) ^ 1 ^ (chip & 1) ^ low ^ step) << 1) + low


def source_lag(ops, chip):
    return 1 - (1 - chip % 2) * (chip // (ops // 2))


def source_target(ops, core, op, step):
    target = (((op >> 1) ^ 1 ^ (op & 1) ^ core ^ step) << 1) | core
    return (op & 1) ^ core ^ 1 ^ (target // (ops // 2)), target


def sink_holder(ops, core, chip):
    return core == chip // (ops // 2)


def send_blocks(times, ops, sink, source, tables):
    def along(block, place):
        return lax.ppermute(block, AXES, routes(times, ops, place))

    def plain_sink(step, only):
        def place(pair, core, op):
            to_core, to_op = sink_target(ops, core, op, step)
            return None if only and not sink_holder(ops, to_core, to_op) else (pair, to_core, to_op)

        return place

    def plain_source(step, only):
        def place(pair, core, op):
            to_core, to_op = source_target(ops, core, op, step)
            to_pair = pair + source_lag(ops, to_op)
            return None if only and sink_holder(ops, to_core, to_op) else (to_pair, to_core, to_op)

        return place

    def pass_on(pair, core, op):
        if not sink_holder(ops, core, op):
            return pair, core, op ^ 1
        to_op = op ^ 2
        return pair - source_lag(ops, op) + source_lag(ops, to_op), to_op // (ops // 2), to_op

    def across(block):
        return along(block, lambda pair, core, op: (pair, 1 - core, op))

    holder = sink_holder(ops, lax.rem(lax.axis_index("tm"), 2), lax.axis_index("op"))
    blocks, last = [], []
    for pair in range(ops // 4):
        sink_first = along(sink, plain_sink(2 * pair + 1, False))
        source_first = along(source, plain_source(2 * pair, False))
        passed = along(jnp.where(holder, source_first, sink_first), pass_on)
        late_source, tables = lax.optimization_barrier((source, tables))
        source_own = along(late_source, plain_source(2 * pair + 1, True))
        sink_own = sink if pair == 0 else along(sink, plain_sink(2 * pair, True))
        own = jnp.where(holder, sink_own, source_own)
        three = [sink_first, source_first, own]
        blocks += three + [across(block) for block in three] + [passed]
        last.append(across(passed))
    return blocks, last, tables


class Fetches:
    def __init__(self, sems, used=0):
        self.sems, self.used, self.copies = sems, used, []

    def start(self, dst, *choices):
        sem = self.sems.at[self.used + len(self.copies)]
        taken = None
        for index, (condition, src) in enumerate(choices):
            copy = pltpu.make_async_copy(src, dst, sem)
            if index == len(choices) - 1:
                condition = taken
            elif taken is not None:
                condition, taken = jnp.logical_and(taken, condition), jnp.logical_and(taken, jnp.logical_not(condition))
            else:
                taken = jnp.logical_not(condition)
            if condition is None:
                copy.start()
            else:
                pl.when(condition)(copy.start)
        self.copies.append(copy)

    def wait(self):
        for copy in self.copies:
            copy.wait()


def aligned(start, size, unit):
    return pl.ds(pl.multiple_of(start, unit), size)


def fetch_source(right, place, fetches, *choices):
    rows, full = choices[0][1].shape[2:]
    inner = right.shape[1] // 2
    at, low = aligned(place, rows, rows), aligned(inner + place, rows, rows)
    for part, dst in ((0, right.at[:, at, :full]), (1, right.at[:, at, full:]), (0, right.at[:, low, full:])):
        fetches.start(dst, *[(condition, block.at[:, part]) for condition, block in choices])


def fetch_sink(left, place, fetches, *choices):
    rows, full = choices[0][1].shape[2:]
    for part in range(2):
        dst = left.at[:, aligned(place, rows, rows), pl.ds(part * full, full)]
        fetches.start(dst, *[(condition, block.at[:, part]) for condition, block in choices])


def jobs_of(half, share, member):
    jobs = [(member * share, share, member * share, share, 0)]
    for apart in range(1, half // 2 + 1):
        if 2 * apart < half:
            jobs.append((member * share, share, lax.rem(member + apart, half) * share, share, 2.0))
        elif share // 2 % LANES:
            jobs.append((member * share, share, lax.rem(member + apart, half) * share, share, 1.0))
        else:
            low = lax.rem(member, half // 2)
            start = low * share + member // (half // 2) * (share // 2)
            jobs.append((start, share // 2, (low + half // 2) * share, share, 2.0))
    return jobs


def stacked(left, start, count, lanes=slice(None)):
    rows = aligned(start, count, math.gcd(count, LANES))
    return jnp.concatenate([left[a, rows, lanes] for a in range(left.shape[0])], 0)


def products_ahead(job, left, right, index):
    row_start, count, col_start, cols, _ = job
    full = left.shape[1]
    rhs = right[index // 2, :, aligned(index % 2 * full + col_start, cols, LANES)]
    return jnp.dot(stacked(left, row_start, count), rhs, preferred_element_type=jnp.float32)


def products_behind(job, left, right, flip):
    row_start, count, col_start, cols, _ = job
    fields, full = left.shape[0], left.shape[1]
    unit = math.gcd(count, LANES)
    for b in range(fields):
        real_turned = right[b, :full, aligned(row_start, count, unit)].T
        imag_turned = right[b, :full, aligned(full + row_start, count, unit)].T
        flip[b, 0, :count, :full] = real_turned
        flip[b, 0, :count, full:] = -imag_turned
        flip[b, 1, :count, :full] = imag_turned
        flip[b, 1, :count, full:] = real_turned
    lhs = flip[:, :, :count, :].reshape(fields * 2 * count, 2 * full)
    rhs = stacked(left, col_start, cols)
    return lax.dot_general(lhs, rhs, (((1,), (1,)), ((), ())), preferred_element_type=jnp.float32)


def place_in(half, share):
    core = lax.rem(lax.axis_index("tm"), 2)
    chip = lax.axis_index("op")
    return core, chip, jobs_of(half, share, lax.rem(chip, half) // 2 * 2 + core)


def lay_kernel(ops, *refs):
    half = ops // 2
    many = 7 * (ops // 4)
    left, right, *partials, sems = refs[many:]
    rows, full = refs[0].shape[2:]
    core, chip, jobs = place_in(half, full // half)
    here = sink_holder(ops, core, chip)
    side = chip // half
    fetches = Fetches(sems)
    for pair in range(ops // 4):
        blocks = refs[7 * pair : 7 * pair + 7]
        for turn in range(2):
            at = core if turn == 0 else 1 - core
            sink_first, source_first, _ = blocks[3 * turn : 3 * turn + 3]
            fetch_sink(left, sink_slot(ops, chip, at, 2 * pair + 1) * rows, fetches, (None, sink_first))
            fetch_source(right, source_slot(ops, chip, at, 2 * pair) * rows, fetches, (None, source_first))
        own, own_across, passed = blocks[2], blocks[5], blocks[6]
        place = sink_slot(ops, chip, side, 2 * pair) * rows
        fetch_sink(left, place, fetches, (here, own), (None, own_across))
        place = source_slot(ops, chip, 1 - side, 2 * pair + 1) * rows
        fetch_source(right, place, fetches, (here, own_across), (None, own))


        @pl.when(here)
        def _():
            mine = Fetches(sems, len(fetches.copies))
            fetch_source(right, source_slot(ops, chip, side, 2 * pair + 1) * rows, mine, (None, passed))
            mine.wait()

        @pl.when(jnp.logical_not(here))
        def _():
            mine = Fetches(sems, len(fetches.copies))
            fetch_sink(left, sink_slot(ops, chip, 1 - side, 2 * pair) * rows, mine, (None, passed))
            mine.wait()
    fetches.wait()
    for b in range(right.shape[0]):
        right[b, full:, :full] = -right[b, :full, full:]
    if partials:

        @pl.when(jnp.logical_not(here))
        def _():
            place = source_slot(ops, chip, side, 1) * rows
            for start in (place, full + place):
                right[:, aligned(start, rows, rows), :] = jnp.zeros((right.shape[0], rows, 2 * full), right.dtype)

        for index in range(partials[0].shape[0]):
            partials[0][index] = products_ahead(jobs[0], left, right, index)


def trace_kernel(ops, group, early, *refs):
    half = ops // 2
    quarter = ops // 4
    blocks = refs[:quarter]
    left, right, *partials, weights, columns, out = refs[quarter : quarter + 2 + early + 3]
    flip, product, flipped, sems = refs[-4:]
    rows, full = blocks[0].shape[2:]
    core, chip, jobs = place_in(half, full // half)
    here = sink_holder(ops, core, chip)
    side = chip // half

    @pl.when(here)
    def _():
        fetches = Fetches(sems)
        for pair in range(quarter):
            fetch_sink(left, sink_slot(ops, chip, 1 - side, 2 * pair) * rows, fetches, (None, blocks[pair]))
        fetches.wait()

    @pl.when(jnp.logical_not(here))
    def _():
        fetches = Fetches(sems)
        for pair in range(quarter):
            fetch_source(right, source_slot(ops, chip, side, 2 * pair + 1) * rows, fetches, (None, blocks[pair]))
        if partials:
            row_start, count, col_start, cols, _ = jobs[0]
            place = source_slot(ops, chip, side, 1) * rows
            lhs = [stacked(left, row_start, count, aligned(start, rows, LANES)) for start in (place, full + place)]
            lhs = jnp.concatenate(lhs, 1)
            at = aligned(col_start, cols, LANES)
            for b in range(blocks[0].shape[0]):
                real, imag = blocks[0][b, 0, :, at], blocks[0][b, 1, :, at]
                for part, rhs in enumerate(((real, -imag), (imag, real))):
                    more = jnp.dot(lhs, jnp.concatenate(rhs, 0), preferred_element_type=jnp.float32)
                    partials[0][2 * b + part] = partials[0][2 * b + part] + more
        fetches.wait()
        for pair in range(quarter):
            place = source_slot(ops, chip, side, 2 * pair + 1) * rows
            for b in range(right.shape[0]):
                right[b, aligned(full + place, rows, rows), :full] = -right[b, aligned(place, rows, rows), full:]

    trace_rows(group, jobs, left, right, partials, flip, weights, columns, out, product, flipped)


def trace_rows(group, jobs, left, right, partials, flip, weights, columns, out, product, flipped):
    fields = left.shape[0]
    parts = 2 * fields * fields

    def put(into, lane, at, block):
        cols = block.shape[1]
        for g in range(block.shape[0] // group):
            into[at * group : (at + 1) * group, lane + g * cols : lane + (g + 1) * cols] = block[g * group : (g + 1) * group]

    lane = 0
    for number, job in enumerate(jobs):
        _, count, _, cols, weight = job
        for index in range(fields * 2):
            if number == 0 and partials:
                value = partials[0][index]
            else:
                value = products_ahead(job, left, right, index)
            value = value.astype(jnp.bfloat16)
            for a in range(fields):
                block = value[a * count : (a + 1) * count]
                place = a * fields * 2 + index
                put(product, lane, place, block)
                if not weight:
                    put(flipped, lane, place, block.T)
        if weight:
            value = (weight * products_behind(job, left, right, flip)).astype(jnp.bfloat16)
            for index in range(fields * 2):
                for a in range(fields):
                    block = value[index * count : (index + 1) * count, a * cols : (a + 1) * cols]
                    put(flipped, lane, a * fields * 2 + index, block)
        lane += count // group * cols
    total = lax.dot_general(
        product[...], flipped[...], (((1,), (1,)), ((), ())), preferred_element_type=jnp.float32
    )
    side = parts * group
    row = lax.broadcasted_iota(jnp.int32, (side, side), 0)
    lane = lax.broadcasted_iota(jnp.int32, (side, side), 1)
    total = jnp.where(lax.rem(row, group) == lax.rem(lane, group), total, 0.0)
    total = jnp.sum(total.reshape(parts, group, side), 1)
    source = lax.broadcasted_iota(jnp.int32, (side, LANES), 0)
    lane = lax.broadcasted_iota(jnp.int32, (side, LANES), 1)
    spread = (source // group == lax.rem(lane, parts)).astype(jnp.float32)
    total = jnp.dot(total, spread, precision=lax.Precision.HIGHEST, preferred_element_type=jnp.float32)
    row = lax.broadcasted_iota(jnp.int32, (parts, LANES), 0)
    lane = lax.broadcasted_iota(jnp.int32, (parts, LANES), 1)
    total = jnp.where(lane // parts == row, total, 0.0)
    total = jnp.dot(total, weights[...], precision=lax.Precision.HIGHEST, preferred_element_type=jnp.float32)
    total = jnp.sum(total, 0, keepdims=True) * columns[:1] + columns[1:]
    out[...] = jnp.broadcast_to(total[:, None, :], out.shape)


def chain_weights(chain_factors, chain_target, fields):
    pairs = fields * fields
    parts = 2 * pairs
    codes = (
        (chain_factors[:, 0] * fields + chain_factors[:, 1]) * pairs
        + chain_factors[:, 2] * fields
        + chain_factors[:, 3]
    )
    row = jnp.arange(LANES, dtype=jnp.int32)
    first, second = row // parts, row % parts
    used = row < parts * parts
    ahead = jnp.where(used, (first // 2) * pairs + second // 2, -1)
    behind = jnp.where(used, (second // 2) * pairs + first // 2, -1)
    column = jnp.arange(LANES, dtype=jnp.int32)
    on_row = (ahead[:, None] == codes[None, :]).astype(jnp.float32)
    on_row = 0.5 * (on_row + (behind[:, None] == codes[None, :]).astype(jnp.float32))
    on_column = (chain_target[:, None] == (column % NCORR)[None, :]).astype(jnp.float32)
    counts = jnp.dot(on_row, on_column, precision=lax.Precision.HIGHEST)
    mixed = (first % 2 != second % 2)[:, None]
    both_imag = (first % 2 + second % 2 == 2)[:, None]
    real_sign = jnp.where(mixed, 0.0, jnp.where(both_imag, -1.0, 1.0))
    imag_sign = jnp.where(mixed, 1.0, 0.0)
    sign = jnp.where((column < WIN * NCORR)[None, :], real_sign, imag_sign)
    return counts * sign


def source_times(times, ops):
    time, chip, source = (lax.broadcasted_iota(jnp.int32, (times, ops, times), axis) for axis in range(3))
    pair = (time // 2 + times // 2 - source_lag(ops, chip)) % (times // 2)
    return (source == pair * 2 + chip % 2).astype(jnp.float32)


def per_device(times, ops, sink_fields, source_fields, source_live, chain_factors, chain_target):
    fields, _, rows, full = sink_fields.shape[1:]
    half = ops // 2
    share = full // half
    parts = 2 * fields * fields
    group = 2 * LANES // parts
    chip = lax.axis_index("op")
    separation = jnp.where(chip // half == lax.rem(chip, 2), 2, 1)
    lane = jnp.arange(LANES, dtype=jnp.int32)
    used = 2 * WIN * NCORR
    wanted = (lane < used) & (lane // NCORR % WIN + 1 == separation)
    scale = jnp.where(wanted, 1.0 / math.sqrt(times), 0.0)
    flag = jnp.where(lane == used, source_live[0].astype(jnp.float32), 0.0)
    columns = jnp.stack([scale, flag]).astype(jnp.float32)
    weights = chain_weights(chain_factors, chain_target, fields)

    any_spec = pl.BlockSpec(memory_space=pl.ANY)
    vmem_spec = pl.BlockSpec(memory_space=pltpu.VMEM)
    jobs = jobs_of(half, share, 0)
    lanes = sum(count // group * cols for _, count, _, cols, _ in jobs)
    most = max(count for _, count, _, _, weight in jobs if weight)
    tables = weights, columns, source_times(times, ops)
    blocks, last, (weights, columns, picks) = send_blocks(times, ops, sink_fields[0], source_fields[0], tables)
    operands = [
        jax.ShapeDtypeStruct((fields, full, 2 * full), jnp.bfloat16),
        jax.ShapeDtypeStruct((fields, 2 * full, 2 * full), jnp.bfloat16),
    ]
    early = int(ops == 4 and rows % LANES == 0)
    if early:
        operands.append(jax.ShapeDtypeStruct((fields * 2, fields * share, share), jnp.float32))
    params = pltpu.CompilerParams(vmem_limit_bytes=24 * 1024 * 1024)
    laid = pl.pallas_call(
        functools.partial(lay_kernel, ops),
        out_shape=operands,
        in_specs=[any_spec] * len(blocks),
        out_specs=[vmem_spec] * len(operands),
        scratch_shapes=[pltpu.SemaphoreType.DMA((5 * ops,))],
        compiler_params=params,
        cost_estimate=pl.CostEstimate(flops=0, bytes_accessed=10 * ops * rows * full, transcendentals=0),
    )(*blocks)
    count = len(last)
    partial_sums, *_ = pl.pallas_call(
        functools.partial(trace_kernel, ops, group, early),
        out_shape=[jax.ShapeDtypeStruct((times * ops, 1, LANES), jnp.float32)] + operands,
        in_specs=[vmem_spec if early else any_spec] * count + [vmem_spec] * (len(operands) + 2),
        out_specs=[vmem_spec] * (len(operands) + 1),
        scratch_shapes=[
            pltpu.VMEM((fields, 2, most, 2 * full), jnp.bfloat16),
            pltpu.VMEM((parts * group, lanes), jnp.bfloat16),
            pltpu.VMEM((parts * group, lanes), jnp.bfloat16),
            pltpu.SemaphoreType.DMA((3 * ops // 4,)),
        ],
        input_output_aliases={count + index: 1 + index for index in range(len(operands))},
        compiler_params=params,
        cost_estimate=pl.CostEstimate(
            flops=4 * 2 * fields * fields * share * full * full, bytes_accessed=10 * ops * rows * full, transcendentals=0
        ),
    )(*last, *laid, weights, columns)
    shares = lax.all_to_all(partial_sums, AXES, 0, 0, tiled=True).reshape(times, ops, LANES)
    live = shares[:, 0, used]
    weight = jnp.sum(picks * live, -1)
    totals = jnp.sum(shares * weight[:, :, None], (0, 1))[:used]
    return totals.reshape(2, WIN, NCORR).transpose(0, 2, 1)


def solution(mesh):
    in_specs = (P("tm", None, None, "op", None), P("tm", None, None, "op", None), P("tm"), P(), P())
    body = functools.partial(per_device, mesh.shape["tm"], mesh.shape["op"])
    return jax.shard_map(body, mesh=mesh, in_specs=in_specs, out_specs=P(), check_vma=False)
```

```python
import functools
import math

import jax
import jax.numpy as jnp
from jax import lax
from jax.experimental import pallas as pl
from jax.experimental.pallas import tpu as pltpu
from jax.sharding import PartitionSpec as P

WIN = 2
NCORR = 16
AXES = ("tm", "op")
LANES = 128


def routes(times, ops, place):
    pairs = []
    for pair in range(times // 2):
        for core in range(2):
            for op in range(ops):
                target = place(pair, core, op)
                if target is not None:
                    to_pair, to_core, to_op = target
                    to_time = (to_pair % (times // 2)) * 2 + to_core
                    pairs.append(((pair * 2 + core) * ops + op, to_time * ops + to_op))
    return pairs


def sink_slot(ops, chip, core, step):
    half = ops // 2
    return core * half + ((chip % half) ^ (chip // half) ^ core ^ step)


def sink_target(ops, core, op, step):
    half = ops // 2
    side = op // half
    return side, core * half + ((op % half) ^ side ^ core ^ step)


def source_slot(ops, chip, core, step):
    low = core ^ (chip // (ops // 2)) ^ (chip & 1) ^ 1
    return (((chip >> 1) ^ 1 ^ (chip & 1) ^ low ^ step) << 1) + low


def source_lag(ops, chip):
    return 1 - (1 - chip % 2) * (chip // (ops // 2))


def source_target(ops, core, op, step):
    target = (((op >> 1) ^ 1 ^ (op & 1) ^ core ^ step) << 1) | core
    return (op & 1) ^ core ^ 1 ^ (target // (ops // 2)), target


def sink_holder(ops, core, chip):
    return core == chip // (ops // 2)


def send_blocks(times, ops, sink, source, tables):
    def along(block, place):
        return lax.ppermute(block, AXES, routes(times, ops, place))

    def plain_sink(step, only):
        def place(pair, core, op):
            to_core, to_op = sink_target(ops, core, op, step)
            return None if only and not sink_holder(ops, to_core, to_op) else (pair, to_core, to_op)

        return place

    def plain_source(step, only):
        def place(pair, core, op):
            to_core, to_op = source_target(ops, core, op, step)
            to_pair = pair + source_lag(ops, to_op)
            return None if only and sink_holder(ops, to_core, to_op) else (to_pair, to_core, to_op)

        return place

    def pass_on(pair, core, op):
        if not sink_holder(ops, core, op):
            return pair, core, op ^ 1
        to_op = op ^ 2
        return pair - source_lag(ops, op) + source_lag(ops, to_op), to_op // (ops // 2), to_op

    def across(block):
        return along(block, lambda pair, core, op: (pair, 1 - core, op))

    holder = sink_holder(ops, lax.rem(lax.axis_index("tm"), 2), lax.axis_index("op"))
    blocks, last = [], []
    for pair in range(ops // 4):
        sink_first = along(sink, plain_sink(2 * pair + 1, False))
        source_first = along(source, plain_source(2 * pair, False))
        passed = along(jnp.where(holder, source_first, sink_first), pass_on)
        late_source, tables = lax.optimization_barrier((source, tables))
        source_own = along(late_source, plain_source(2 * pair + 1, True))
        sink_own = sink if pair == 0 else along(sink, plain_sink(2 * pair, True))
        own = jnp.where(holder, sink_own, source_own)
        three = [sink_first, source_first, own]
        blocks += three + [across(block) for block in three] + [passed]
        last.append(across(passed))
    return blocks, last, tables


class Fetches:
    def __init__(self, sems, used=0):
        self.sems, self.used, self.copies = sems, used, []

    def start(self, dst, *choices):
        sem = self.sems.at[self.used + len(self.copies)]
        taken = None
        for index, (condition, src) in enumerate(choices):
            copy = pltpu.make_async_copy(src, dst, sem)
            if index == len(choices) - 1:
                condition = taken
            elif taken is not None:
                condition, taken = jnp.logical_and(taken, condition), jnp.logical_and(taken, jnp.logical_not(condition))
            else:
                taken = jnp.logical_not(condition)
            if condition is None:
                copy.start()
            else:
                pl.when(condition)(copy.start)
        self.copies.append(copy)

    def wait(self):
        for copy in self.copies:
            copy.wait()


def aligned(start, size, unit):
    return pl.ds(pl.multiple_of(start, unit), size)


def fetch_source(right, place, fetches, *choices):
    rows, full = choices[0][1].shape[2:]
    inner = right.shape[1] // 2
    at, low = aligned(place, rows, rows), aligned(inner + place, rows, rows)
    for part, dst in ((0, right.at[:, at, :full]), (1, right.at[:, at, full:]), (0, right.at[:, low, full:])):
        fetches.start(dst, *[(condition, block.at[:, part]) for condition, block in choices])


def fetch_sink(left, place, fetches, *choices):
    rows, full = choices[0][1].shape[2:]
    for part in range(2):
        dst = left.at[:, aligned(place, rows, rows), pl.ds(part * full, full)]
        fetches.start(dst, *[(condition, block.at[:, part]) for condition, block in choices])


def jobs_of(half, share, member):
    jobs = [(member * share, share, member * share, share, 0)]
    for apart in range(1, half // 2 + 1):
        if 2 * apart < half:
            jobs.append((member * share, share, lax.rem(member + apart, half) * share, share, 2.0))
        elif share // 2 % LANES:
            jobs.append((member * share, share, lax.rem(member + apart, half) * share, share, 1.0))
        else:
            low = lax.rem(member, half // 2)
            start = low * share + member // (half // 2) * (share // 2)
            jobs.append((start, share // 2, (low + half // 2) * share, share, 2.0))
    return jobs


def stacked(left, start, count, lanes=slice(None)):
    rows = aligned(start, count, math.gcd(count, LANES))
    return jnp.concatenate([left[a, rows, lanes] for a in range(left.shape[0])], 0)


def products_ahead(job, left, right, index):
    row_start, count, col_start, cols, _ = job
    full = left.shape[1]
    rhs = right[index // 2, :, aligned(index % 2 * full + col_start, cols, LANES)]
    return jnp.dot(stacked(left, row_start, count), rhs, preferred_element_type=jnp.float32)


def products_behind(job, left, right, flip):
    row_start, count, col_start, cols, _ = job
    fields, full = left.shape[0], left.shape[1]
    unit = math.gcd(count, LANES)
    for b in range(fields):
        real_turned = right[b, :full, aligned(row_start, count, unit)].T
        imag_turned = right[b, :full, aligned(full + row_start, count, unit)].T
        flip[b, 0, :count, :full] = real_turned
        flip[b, 0, :count, full:] = -imag_turned
        flip[b, 1, :count, :full] = imag_turned
        flip[b, 1, :count, full:] = real_turned
    lhs = flip[:, :, :count, :].reshape(fields * 2 * count, 2 * full)
    rhs = stacked(left, col_start, cols)
    return lax.dot_general(lhs, rhs, (((1,), (1,)), ((), ())), preferred_element_type=jnp.float32)


def place_in(half, share):
    core = lax.rem(lax.axis_index("tm"), 2)
    chip = lax.axis_index("op")
    return core, chip, jobs_of(half, share, lax.rem(chip, half) // 2 * 2 + core)


def lay_kernel(ops, *refs):
    half = ops // 2
    many = 7 * (ops // 4)
    left, right, *partials, sems = refs[many:]
    rows, full = refs[0].shape[2:]
    core, chip, jobs = place_in(half, full // half)
    here = sink_holder(ops, core, chip)
    side = chip // half
    fetches = Fetches(sems)
    for pair in range(ops // 4):
        blocks = refs[7 * pair : 7 * pair + 7]
        for turn in range(2):
            at = core if turn == 0 else 1 - core
            sink_first, source_first, _ = blocks[3 * turn : 3 * turn + 3]
            fetch_sink(left, sink_slot(ops, chip, at, 2 * pair + 1) * rows, fetches, (None, sink_first))
            fetch_source(right, source_slot(ops, chip, at, 2 * pair) * rows, fetches, (None, source_first))
        own, own_across, passed = blocks[2], blocks[5], blocks[6]
        place = sink_slot(ops, chip, side, 2 * pair) * rows
        fetch_sink(left, place, fetches, (here, own), (None, own_across))
        place = source_slot(ops, chip, 1 - side, 2 * pair + 1) * rows
        fetch_source(right, place, fetches, (here, own_across), (None, own))


        @pl.when(here)
        def _():
            mine = Fetches(sems, len(fetches.copies))
            fetch_source(right, source_slot(ops, chip, side, 2 * pair + 1) * rows, mine, (None, passed))
            mine.wait()

        @pl.when(jnp.logical_not(here))
        def _():
            mine = Fetches(sems, len(fetches.copies))
            fetch_sink(left, sink_slot(ops, chip, 1 - side, 2 * pair) * rows, mine, (None, passed))
            mine.wait()
    fetches.wait()
    for b in range(right.shape[0]):
        right[b, full:, :full] = -right[b, :full, full:]
    if partials:

        @pl.when(jnp.logical_not(here))
        def _():
            place = source_slot(ops, chip, side, 1) * rows
            for start in (place, full + place):
                right[:, aligned(start, rows, rows), :] = jnp.zeros((right.shape[0], rows, 2 * full), right.dtype)

        for index in range(partials[0].shape[0]):
            partials[0][index] = products_ahead(jobs[0], left, right, index)


def trace_kernel(ops, group, early, *refs):
    half = ops // 2
    quarter = ops // 4
    blocks = refs[:quarter]
    left, right, *partials, weights, columns, out = refs[quarter : quarter + 2 + early + 3]
    flip, product, flipped, sems = refs[-4:]
    rows, full = blocks[0].shape[2:]
    core, chip, jobs = place_in(half, full // half)
    here = sink_holder(ops, core, chip)
    side = chip // half

    @pl.when(here)
    def _():
        fetches = Fetches(sems)
        for pair in range(quarter):
            fetch_sink(left, sink_slot(ops, chip, 1 - side, 2 * pair) * rows, fetches, (None, blocks[pair]))
        fetches.wait()

    @pl.when(jnp.logical_not(here))
    def _():
        fetches = Fetches(sems)
        for pair in range(quarter):
            fetch_source(right, source_slot(ops, chip, side, 2 * pair + 1) * rows, fetches, (None, blocks[pair]))
        fetches.wait()
        for pair in range(quarter):
            place = source_slot(ops, chip, side, 2 * pair + 1) * rows
            for b in range(right.shape[0]):
                right[b, aligned(full + place, rows, rows), :full] = -right[b, aligned(place, rows, rows), full:]

    def rest(index):
        row_start, count, col_start, cols, _ = jobs[0]
        place = source_slot(ops, chip, side, 1) * rows
        lhs = [stacked(left, row_start, count, aligned(start, rows, LANES)) for start in (place, full + place)]
        at = aligned(col_start, cols, LANES)
        real, imag = [jnp.where(here, 0.0, blocks[0][index // 2, part, :, at]).astype(jnp.bfloat16) for part in range(2)]
        rhs = jnp.concatenate((imag, real) if index % 2 else (real, -imag), 0)
        return jnp.dot(jnp.concatenate(lhs, 1), rhs, preferred_element_type=jnp.float32)

    trace_rows(group, jobs, rest, left, right, partials, flip, weights, columns, out, product, flipped)


def trace_rows(group, jobs, rest, left, right, partials, flip, weights, columns, out, product, flipped):
    fields = left.shape[0]
    parts = 2 * fields * fields

    def put(into, lane, at, block):
        cols = block.shape[1]
        for g in range(block.shape[0] // group):
            into[at * group : (at + 1) * group, lane + g * cols : lane + (g + 1) * cols] = block[g * group : (g + 1) * group]

    lane = 0
    for number, job in enumerate(jobs):
        _, count, _, cols, weight = job
        for index in range(fields * 2):
            if number == 0 and partials:
                value = partials[0][index] + rest(index)
            else:
                value = products_ahead(job, left, right, index)
            value = value.astype(jnp.bfloat16)
            for a in range(fields):
                block = value[a * count : (a + 1) * count]
                place = a * fields * 2 + index
                put(product, lane, place, block)
                if not weight:
                    put(flipped, lane, place, block.T)
        if weight:
            value = (weight * products_behind(job, left, right, flip)).astype(jnp.bfloat16)
            for index in range(fields * 2):
                for a in range(fields):
                    block = value[index * count : (index + 1) * count, a * cols : (a + 1) * cols]
                    put(flipped, lane, a * fields * 2 + index, block)
        lane += count // group * cols
    total = lax.dot_general(
        product[...], flipped[...], (((1,), (1,)), ((), ())), preferred_element_type=jnp.float32
    )
    side = parts * group
    row = lax.broadcasted_iota(jnp.int32, (side, side), 0)
    lane = lax.broadcasted_iota(jnp.int32, (side, side), 1)
    total = jnp.where(lax.rem(row, group) == lax.rem(lane, group), total, 0.0)
    total = jnp.sum(total.reshape(parts, group, side), 1)
    source = lax.broadcasted_iota(jnp.int32, (side, LANES), 0)
    lane = lax.broadcasted_iota(jnp.int32, (side, LANES), 1)
    spread = (source // group == lax.rem(lane, parts)).astype(jnp.float32)
    total = jnp.dot(total, spread, precision=lax.Precision.HIGHEST, preferred_element_type=jnp.float32)
    row = lax.broadcasted_iota(jnp.int32, (parts, LANES), 0)
    lane = lax.broadcasted_iota(jnp.int32, (parts, LANES), 1)
    total = jnp.where(lane // parts == row, total, 0.0)
    total = jnp.dot(total, weights[...], precision=lax.Precision.HIGHEST, preferred_element_type=jnp.float32)
    total = jnp.sum(total, 0, keepdims=True) * columns[:1] + columns[1:]
    out[...] = jnp.broadcast_to(total[:, None, :], out.shape)


def chain_weights(chain_factors, chain_target, fields):
    pairs = fields * fields
    parts = 2 * pairs
    codes = (
        (chain_factors[:, 0] * fields + chain_factors[:, 1]) * pairs
        + chain_factors[:, 2] * fields
        + chain_factors[:, 3]
    )
    row = jnp.arange(LANES, dtype=jnp.int32)
    first, second = row // parts, row % parts
    used = row < parts * parts
    ahead = jnp.where(used, (first // 2) * pairs + second // 2, -1)
    behind = jnp.where(used, (second // 2) * pairs + first // 2, -1)
    column = jnp.arange(LANES, dtype=jnp.int32)
    on_row = (ahead[:, None] == codes[None, :]).astype(jnp.float32)
    on_row = 0.5 * (on_row + (behind[:, None] == codes[None, :]).astype(jnp.float32))
    on_column = (chain_target[:, None] == (column % NCORR)[None, :]).astype(jnp.float32)
    counts = jnp.dot(on_row, on_column, precision=lax.Precision.HIGHEST)
    mixed = (first % 2 != second % 2)[:, None]
    both_imag = (first % 2 + second % 2 == 2)[:, None]
    real_sign = jnp.where(mixed, 0.0, jnp.where(both_imag, -1.0, 1.0))
    imag_sign = jnp.where(mixed, 1.0, 0.0)
    sign = jnp.where((column < WIN * NCORR)[None, :], real_sign, imag_sign)
    return counts * sign


def source_times(times, ops):
    time, chip, source = (lax.broadcasted_iota(jnp.int32, (times, ops, times), axis) for axis in range(3))
    pair = (time // 2 + times // 2 - source_lag(ops, chip)) % (times // 2)
    return (source == pair * 2 + chip % 2).astype(jnp.float32)


def per_device(times, ops, sink_fields, source_fields, source_live, chain_factors, chain_target):
    fields, _, rows, full = sink_fields.shape[1:]
    half = ops // 2
    share = full // half
    parts = 2 * fields * fields
    group = 2 * LANES // parts
    chip = lax.axis_index("op")
    separation = jnp.where(chip // half == lax.rem(chip, 2), 2, 1)
    lane = jnp.arange(LANES, dtype=jnp.int32)
    used = 2 * WIN * NCORR
    wanted = (lane < used) & (lane // NCORR % WIN + 1 == separation)
    scale = jnp.where(wanted, 1.0 / math.sqrt(times), 0.0)
    flag = jnp.where(lane == used, source_live[0].astype(jnp.float32), 0.0)
    columns = jnp.stack([scale, flag]).astype(jnp.float32)
    weights = chain_weights(chain_factors, chain_target, fields)

    any_spec = pl.BlockSpec(memory_space=pl.ANY)
    vmem_spec = pl.BlockSpec(memory_space=pltpu.VMEM)
    jobs = jobs_of(half, share, 0)
    lanes = sum(count // group * cols for _, count, _, cols, _ in jobs)
    most = max(count for _, count, _, _, weight in jobs if weight)
    tables = weights, columns, source_times(times, ops)
    blocks, last, (weights, columns, picks) = send_blocks(times, ops, sink_fields[0], source_fields[0], tables)
    operands = [
        jax.ShapeDtypeStruct((fields, full, 2 * full), jnp.bfloat16),
        jax.ShapeDtypeStruct((fields, 2 * full, 2 * full), jnp.bfloat16),
    ]
    early = int(ops == 4 and rows % LANES == 0)
    if early:
        operands.append(jax.ShapeDtypeStruct((fields * 2, fields * share, share), jnp.float32))
    params = pltpu.CompilerParams(vmem_limit_bytes=24 * 1024 * 1024)
    laid = pl.pallas_call(
        functools.partial(lay_kernel, ops),
        out_shape=operands,
        in_specs=[any_spec] * len(blocks),
        out_specs=[vmem_spec] * len(operands),
        scratch_shapes=[pltpu.SemaphoreType.DMA((5 * ops,))],
        compiler_params=params,
        cost_estimate=pl.CostEstimate(flops=0, bytes_accessed=10 * ops * rows * full, transcendentals=0),
    )(*blocks)
    count = len(last)
    partial_sums, *_ = pl.pallas_call(
        functools.partial(trace_kernel, ops, group, early),
        out_shape=[jax.ShapeDtypeStruct((times * ops, 1, LANES), jnp.float32)] + operands,
        in_specs=[vmem_spec if early else any_spec] * count + [vmem_spec] * (len(operands) + 2),
        out_specs=[vmem_spec] * (len(operands) + 1),
        scratch_shapes=[
            pltpu.VMEM((fields, 2, most, 2 * full), jnp.bfloat16),
            pltpu.VMEM((parts * group, lanes), jnp.bfloat16),
            pltpu.VMEM((parts * group, lanes), jnp.bfloat16),
            pltpu.SemaphoreType.DMA((3 * ops // 4,)),
        ],
        input_output_aliases={count + index: 1 + index for index in range(len(operands))},
        compiler_params=params,
        cost_estimate=pl.CostEstimate(
            flops=4 * 2 * fields * fields * share * full * full, bytes_accessed=10 * ops * rows * full, transcendentals=0
        ),
    )(*last, *laid, weights, columns)
    shares = lax.all_to_all(partial_sums, AXES, 0, 0, tiled=True).reshape(times, ops, LANES)
    live = shares[:, 0, used]
    weight = jnp.sum(picks * live, -1)
    totals = jnp.sum(shares * weight[:, :, None], (0, 1))[:used]
    return totals.reshape(2, WIN, NCORR).transpose(0, 2, 1)


def solution(mesh):
    in_specs = (P("tm", None, None, "op", None), P("tm", None, None, "op", None), P("tm"), P(), P())
    body = functools.partial(per_device, mesh.shape["tm"], mesh.shape["op"])
    return jax.shard_map(body, mesh=mesh, in_specs=in_specs, out_specs=P(), check_vma=False)
```

```python
import functools
import math

import jax
import jax.numpy as jnp
from jax import lax
from jax.experimental import pallas as pl
from jax.experimental.pallas import tpu as pltpu
from jax.sharding import PartitionSpec as P

WIN = 2
NCORR = 16
AXES = ("tm", "op")
LANES = 128


def routes(times, ops, place):
    pairs = []
    for pair in range(times // 2):
        for core in range(2):
            for op in range(ops):
                target = place(pair, core, op)
                if target is not None:
                    to_pair, to_core, to_op = target
                    to_time = (to_pair % (times // 2)) * 2 + to_core
                    pairs.append(((pair * 2 + core) * ops + op, to_time * ops + to_op))
    return pairs


def sink_slot(ops, chip, core, step):
    half = ops // 2
    return core * half + ((chip % half) ^ (chip // half) ^ core ^ step)


def sink_target(ops, core, op, step):
    half = ops // 2
    side = op // half
    return side, core * half + ((op % half) ^ side ^ core ^ step)


def source_slot(ops, chip, core, step):
    low = core ^ (chip // (ops // 2)) ^ (chip & 1) ^ 1
    return (((chip >> 1) ^ 1 ^ (chip & 1) ^ low ^ step) << 1) + low


def source_lag(ops, chip):
    return 1 - (1 - chip % 2) * (chip // (ops // 2))


def source_target(ops, core, op, step):
    target = (((op >> 1) ^ 1 ^ (op & 1) ^ core ^ step) << 1) | core
    return (op & 1) ^ core ^ 1 ^ (target // (ops // 2)), target


def sink_holder(ops, core, chip):
    return core == chip // (ops // 2)


def send_blocks(times, ops, sink, source, tables):
    def along(block, place):
        return lax.ppermute(block, AXES, routes(times, ops, place))

    def plain_sink(step, only):
        def place(pair, core, op):
            to_core, to_op = sink_target(ops, core, op, step)
            return None if only and not sink_holder(ops, to_core, to_op) else (pair, to_core, to_op)

        return place

    def plain_source(step, only):
        def place(pair, core, op):
            to_core, to_op = source_target(ops, core, op, step)
            to_pair = pair + source_lag(ops, to_op)
            return None if only and sink_holder(ops, to_core, to_op) else (to_pair, to_core, to_op)

        return place

    def pass_on(pair, core, op):
        if not sink_holder(ops, core, op):
            return pair, core, op ^ 1
        to_op = op ^ 2
        return pair - source_lag(ops, op) + source_lag(ops, to_op), to_op // (ops // 2), to_op

    def across(block):
        return along(block, lambda pair, core, op: (pair, 1 - core, op))

    holder = sink_holder(ops, lax.rem(lax.axis_index("tm"), 2), lax.axis_index("op"))
    blocks, last = [], []
    for pair in range(ops // 4):
        sink_first = along(sink, plain_sink(2 * pair + 1, False))
        source_first = along(source, plain_source(2 * pair, False))
        passed = along(jnp.where(holder, source_first, sink_first), pass_on)
        late_source, tables = lax.optimization_barrier((source, tables))
        source_own = along(late_source, plain_source(2 * pair + 1, True))
        sink_own = sink if pair == 0 else along(sink, plain_sink(2 * pair, True))
        own = jnp.where(holder, sink_own, source_own)
        three = [sink_first, source_first, own]
        blocks += three + [across(block) for block in three] + [passed]
        last.append(across(passed))
    return blocks, last, tables


class Fetches:
    def __init__(self, sems, used=0):
        self.sems, self.used, self.copies = sems, used, []

    def start(self, dst, *choices):
        sem = self.sems.at[self.used + len(self.copies)]
        taken = None
        for index, (condition, src) in enumerate(choices):
            copy = pltpu.make_async_copy(src, dst, sem)
            if index == len(choices) - 1:
                condition = taken
            elif taken is not None:
                condition, taken = jnp.logical_and(taken, condition), jnp.logical_and(taken, jnp.logical_not(condition))
            else:
                taken = jnp.logical_not(condition)
            if condition is None:
                copy.start()
            else:
                pl.when(condition)(copy.start)
        self.copies.append(copy)

    def wait(self):
        for copy in self.copies:
            copy.wait()


def aligned(start, size, unit):
    return pl.ds(pl.multiple_of(start, unit), size)


def fetch_source(right, place, fetches, *choices):
    rows, full = choices[0][1].shape[2:]
    inner = right.shape[1] // 2
    at, low = aligned(place, rows, rows), aligned(inner + place, rows, rows)
    for part, dst in ((0, right.at[:, at, :full]), (1, right.at[:, at, full:]), (0, right.at[:, low, full:])):
        fetches.start(dst, *[(condition, block.at[:, part]) for condition, block in choices])


def fetch_sink(left, place, fetches, *choices):
    rows, full = choices[0][1].shape[2:]
    for part in range(2):
        dst = left.at[:, aligned(place, rows, rows), pl.ds(part * full, full)]
        fetches.start(dst, *[(condition, block.at[:, part]) for condition, block in choices])


def jobs_of(half, share, member):
    jobs = [(member * share, share, member * share, share, 0)]
    for apart in range(1, half // 2 + 1):
        if 2 * apart < half:
            jobs.append((member * share, share, lax.rem(member + apart, half) * share, share, 2.0))
        elif share // 2 % LANES:
            jobs.append((member * share, share, lax.rem(member + apart, half) * share, share, 1.0))
        else:
            low = lax.rem(member, half // 2)
            start = low * share + member // (half // 2) * (share // 2)
            jobs.append((start, share // 2, (low + half // 2) * share, share, 2.0))
    return jobs


def stacked(left, start, count, lanes=slice(None)):
    rows = aligned(start, count, math.gcd(count, LANES))
    return jnp.concatenate([left[a, rows, lanes] for a in range(left.shape[0])], 0)


def products_ahead(job, left, right, index):
    row_start, count, col_start, cols, _ = job
    full = left.shape[1]
    rhs = right[index // 2, :, aligned(index % 2 * full + col_start, cols, LANES)]
    return jnp.dot(stacked(left, row_start, count), rhs, preferred_element_type=jnp.float32)


def products_behind(job, left, right, flip):
    row_start, count, col_start, cols, _ = job
    fields, full = left.shape[0], left.shape[1]
    unit = math.gcd(count, LANES)
    for b in range(fields):
        real_turned = right[b, :full, aligned(row_start, count, unit)].T
        imag_turned = right[b, :full, aligned(full + row_start, count, unit)].T
        flip[b, 0, :count, :full] = real_turned
        flip[b, 0, :count, full:] = -imag_turned
        flip[b, 1, :count, :full] = imag_turned
        flip[b, 1, :count, full:] = real_turned
    lhs = flip[:, :, :count, :].reshape(fields * 2 * count, 2 * full)
    rhs = stacked(left, col_start, cols)
    return lax.dot_general(lhs, rhs, (((1,), (1,)), ((), ())), preferred_element_type=jnp.float32)


def place_in(half, share):
    core = lax.rem(lax.axis_index("tm"), 2)
    chip = lax.axis_index("op")
    return core, chip, jobs_of(half, share, lax.rem(chip, half) // 2 * 2 + core)


def lay_kernel(ops, *refs):
    half = ops // 2
    many = 7 * (ops // 4)
    left, right, *partials, sems = refs[many:]
    rows, full = refs[0].shape[2:]
    core, chip, jobs = place_in(half, full // half)
    here = sink_holder(ops, core, chip)
    side = chip // half
    fetches = Fetches(sems)
    for pair in range(ops // 4):
        blocks = refs[7 * pair : 7 * pair + 7]
        for turn in range(2):
            at = core if turn == 0 else 1 - core
            sink_first, source_first, _ = blocks[3 * turn : 3 * turn + 3]
            fetch_sink(left, sink_slot(ops, chip, at, 2 * pair + 1) * rows, fetches, (None, sink_first))
            fetch_source(right, source_slot(ops, chip, at, 2 * pair) * rows, fetches, (None, source_first))
        own, own_across, passed = blocks[2], blocks[5], blocks[6]
        place = sink_slot(ops, chip, side, 2 * pair) * rows
        fetch_sink(left, place, fetches, (here, own), (None, own_across))
        place = source_slot(ops, chip, 1 - side, 2 * pair + 1) * rows
        fetch_source(right, place, fetches, (here, own_across), (None, own))


        @pl.when(here)
        def _():
            mine = Fetches(sems, len(fetches.copies))
            fetch_source(right, source_slot(ops, chip, side, 2 * pair + 1) * rows, mine, (None, passed))
            mine.wait()

        @pl.when(jnp.logical_not(here))
        def _():
            mine = Fetches(sems, len(fetches.copies))
            fetch_sink(left, sink_slot(ops, chip, 1 - side, 2 * pair) * rows, mine, (None, passed))
            mine.wait()
    fetches.wait()
    for b in range(right.shape[0]):
        right[b, full:, :full] = -right[b, :full, full:]
    if partials:

        @pl.when(jnp.logical_not(here))
        def _():
            place = source_slot(ops, chip, side, 1) * rows
            for start in (place, full + place):
                right[:, aligned(start, rows, rows), :] = jnp.zeros((right.shape[0], rows, 2 * full), right.dtype)

        for index in range(partials[0].shape[0]):
            partials[0][index] = products_ahead(jobs[0], left, right, index)


def trace_kernel(ops, group, early, *refs):
    half = ops // 2
    quarter = ops // 4
    blocks = refs[:quarter]
    left, right, *partials, weights, columns, out = refs[quarter : quarter + 2 + early + 3]
    flip, product, flipped, sems = refs[-4:]
    rows, full = blocks[0].shape[2:]
    core, chip, jobs = place_in(half, full // half)
    here = sink_holder(ops, core, chip)
    side = chip // half

    @pl.when(here)
    def _():
        fetches = Fetches(sems)
        for pair in range(quarter):
            fetch_sink(left, sink_slot(ops, chip, 1 - side, 2 * pair) * rows, fetches, (None, blocks[pair]))
        fetches.wait()

    @pl.when(jnp.logical_not(here))
    def _():
        fetches = Fetches(sems)
        for pair in range(quarter):
            fetch_source(right, source_slot(ops, chip, side, 2 * pair + 1) * rows, fetches, (None, blocks[pair]))
        fetches.wait()
        for pair in range(quarter):
            place = source_slot(ops, chip, side, 2 * pair + 1) * rows
            for b in range(right.shape[0]):
                right[b, aligned(full + place, rows, rows), :full] = -right[b, aligned(place, rows, rows), full:]

    def rest(index):
        row_start, count, col_start, cols, _ = jobs[0]
        place = source_slot(ops, chip, side, 1) * rows
        lhs = [stacked(left, row_start, count, aligned(start, rows, LANES)) for start in (place, full + place)]
        at = aligned(col_start, cols, LANES)
        real, imag = [jnp.where(here, 0.0, blocks[0][index // 2, part, :, at]).astype(jnp.bfloat16) for part in range(2)]
        rhs = jnp.concatenate((imag, real) if index % 2 else (real, -imag), 0)
        return jnp.dot(jnp.concatenate(lhs, 1), rhs, preferred_element_type=jnp.float32)

    trace_rows(group, jobs, rest, left, right, partials, flip, weights, columns, out, product, flipped)


def trace_rows(group, jobs, rest, left, right, partials, flip, weights, columns, out, product, flipped):
    fields = left.shape[0]
    parts = 2 * fields * fields

    def put(into, lane, at, block):
        cols = block.shape[1]
        for g in range(block.shape[0] // group):
            into[at * group : (at + 1) * group, lane + g * cols : lane + (g + 1) * cols] = block[g * group : (g + 1) * group]

    lane = 0
    for number, job in enumerate(jobs):
        _, count, _, cols, weight = job
        for index in range(fields * 2):
            if number == 0 and partials:
                value = partials[0][index] + rest(index)
            else:
                value = products_ahead(job, left, right, index)
            value = value.astype(jnp.bfloat16)
            for a in range(fields):
                block = value[a * count : (a + 1) * count]
                place = a * fields * 2 + index
                put(product, lane, place, block)
                if not weight:
                    put(flipped, lane, place, block.T)
        if weight:
            value = (weight * products_behind(job, left, right, flip)).astype(jnp.bfloat16)
            for index in range(fields * 2):
                for a in range(fields):
                    block = value[index * count : (index + 1) * count, a * cols : (a + 1) * cols]
                    put(flipped, lane, a * fields * 2 + index, block)
        lane += count // group * cols
    total = lax.dot_general(
        product[...], flipped[...], (((1,), (1,)), ((), ())), preferred_element_type=jnp.float32
    )
    side = parts * group
    row = lax.broadcasted_iota(jnp.int32, (side, side), 0)
    lane = lax.broadcasted_iota(jnp.int32, (side, side), 1)
    total = jnp.where(lax.rem(row, group) == lax.rem(lane, group), total, 0.0)
    total = jnp.sum(total.reshape(parts, group, side), 1)
    source = lax.broadcasted_iota(jnp.int32, (side, LANES), 0)
    lane = lax.broadcasted_iota(jnp.int32, (side, LANES), 1)
    spread = (source // group == lax.rem(lane, parts)).astype(jnp.float32)
    total = jnp.dot(total, spread, precision=lax.Precision.HIGHEST, preferred_element_type=jnp.float32)
    row = lax.broadcasted_iota(jnp.int32, (parts, LANES), 0)
    lane = lax.broadcasted_iota(jnp.int32, (parts, LANES), 1)
    total = jnp.where(lane // parts == row, total, 0.0)
    total = jnp.dot(total, weights[...], precision=lax.Precision.HIGHEST, preferred_element_type=jnp.float32)
    total = jnp.sum(total, 0, keepdims=True) * columns[:1] + columns[1:]
    out[...] = jnp.broadcast_to(total[:, None, :], out.shape)


def chain_weights(chain_factors, chain_target, fields):
    pairs = fields * fields
    parts = 2 * pairs
    codes = (
        (chain_factors[:, 0] * fields + chain_factors[:, 1]) * pairs
        + chain_factors[:, 2] * fields
        + chain_factors[:, 3]
    )
    row = jnp.arange(LANES, dtype=jnp.int32)
    first, second = row // parts, row % parts
    used = row < parts * parts
    ahead = jnp.where(used, (first // 2) * pairs + second // 2, -1)
    behind = jnp.where(used, (second // 2) * pairs + first // 2, -1)
    column = jnp.arange(LANES, dtype=jnp.int32)
    on_row = (ahead[:, None] == codes[None, :]).astype(jnp.float32)
    on_row = 0.5 * (on_row + (behind[:, None] == codes[None, :]).astype(jnp.float32))
    on_column = (chain_target[:, None] == (column % NCORR)[None, :]).astype(jnp.float32)
    counts = jnp.dot(on_row, on_column)
    mixed = (first % 2 != second % 2)[:, None]
    both_imag = (first % 2 + second % 2 == 2)[:, None]
    real_sign = jnp.where(mixed, 0.0, jnp.where(both_imag, -1.0, 1.0))
    imag_sign = jnp.where(mixed, 1.0, 0.0)
    sign = jnp.where((column < WIN * NCORR)[None, :], real_sign, imag_sign)
    return counts * sign


def source_times(times, ops):
    time, chip, source = (lax.broadcasted_iota(jnp.int32, (times, ops, times), axis) for axis in range(3))
    pair = (time // 2 + times // 2 - source_lag(ops, chip)) % (times // 2)
    return (source == pair * 2 + chip % 2).astype(jnp.float32)


def per_device(times, ops, sink_fields, source_fields, source_live, chain_factors, chain_target):
    fields, _, rows, full = sink_fields.shape[1:]
    half = ops // 2
    share = full // half
    parts = 2 * fields * fields
    group = 2 * LANES // parts
    chip = lax.axis_index("op")
    separation = jnp.where(chip // half == lax.rem(chip, 2), 2, 1)
    lane = jnp.arange(LANES, dtype=jnp.int32)
    used = 2 * WIN * NCORR
    wanted = (lane < used) & (lane // NCORR % WIN + 1 == separation)
    scale = jnp.where(wanted, 1.0 / math.sqrt(times), 0.0)
    flag = jnp.where(lane == used, source_live[0].astype(jnp.float32), 0.0)
    columns = jnp.stack([scale, flag]).astype(jnp.float32)
    weights = chain_weights(chain_factors, chain_target, fields)

    any_spec = pl.BlockSpec(memory_space=pl.ANY)
    vmem_spec = pl.BlockSpec(memory_space=pltpu.VMEM)
    jobs = jobs_of(half, share, 0)
    lanes = sum(count // group * cols for _, count, _, cols, _ in jobs)
    most = max(count for _, count, _, _, weight in jobs if weight)
    tables = weights, columns, source_times(times, ops)
    blocks, last, (weights, columns, picks) = send_blocks(times, ops, sink_fields[0], source_fields[0], tables)
    operands = [
        jax.ShapeDtypeStruct((fields, full, 2 * full), jnp.bfloat16),
        jax.ShapeDtypeStruct((fields, 2 * full, 2 * full), jnp.bfloat16),
    ]
    early = int(ops == 4 and rows % LANES == 0)
    if early:
        operands.append(jax.ShapeDtypeStruct((fields * 2, fields * share, share), jnp.float32))
    params = pltpu.CompilerParams(vmem_limit_bytes=24 * 1024 * 1024)
    laid = pl.pallas_call(
        functools.partial(lay_kernel, ops),
        out_shape=operands,
        in_specs=[any_spec] * len(blocks),
        out_specs=[vmem_spec] * len(operands),
        scratch_shapes=[pltpu.SemaphoreType.DMA((5 * ops,))],
        compiler_params=params,
        cost_estimate=pl.CostEstimate(flops=0, bytes_accessed=10 * ops * rows * full, transcendentals=0),
    )(*blocks)
    count = len(last)
    partial_sums, *_ = pl.pallas_call(
        functools.partial(trace_kernel, ops, group, early),
        out_shape=[jax.ShapeDtypeStruct((times * ops, 1, LANES), jnp.float32)] + operands,
        in_specs=[vmem_spec if early else any_spec] * count + [vmem_spec] * (len(operands) + 2),
        out_specs=[vmem_spec] * (len(operands) + 1),
        scratch_shapes=[
            pltpu.VMEM((fields, 2, most, 2 * full), jnp.bfloat16),
            pltpu.VMEM((parts * group, lanes), jnp.bfloat16),
            pltpu.VMEM((parts * group, lanes), jnp.bfloat16),
            pltpu.SemaphoreType.DMA((3 * ops // 4,)),
        ],
        input_output_aliases={count + index: 1 + index for index in range(len(operands))},
        compiler_params=params,
        cost_estimate=pl.CostEstimate(
            flops=4 * 2 * fields * fields * share * full * full, bytes_accessed=10 * ops * rows * full, transcendentals=0
        ),
    )(*last, *laid, weights, columns)
    shares = lax.all_to_all(partial_sums, AXES, 0, 0, tiled=True).reshape(times, ops, LANES)
    live = shares[:, 0, used]
    weight = jnp.sum(picks * live, -1)
    totals = jnp.sum(shares * weight[:, :, None], (0, 1))[:used]
    return totals.reshape(2, WIN, NCORR).transpose(0, 2, 1)


def solution(mesh):
    in_specs = (P("tm", None, None, "op", None), P("tm", None, None, "op", None), P("tm"), P(), P())
    body = functools.partial(per_device, mesh.shape["tm"], mesh.shape["op"])
    return jax.shard_map(body, mesh=mesh, in_specs=in_specs, out_specs=P(), check_vma=False)
```
